32 devices in a mesh: dp: 16 (over z, y, x), tensor: 2 (over core).
Axes of the slice: x: 2, y: 2, z: 4, core: 2. Of those that a mesh axis runs over, the one named last changes fastest.
Arguments:
- tokens: bfloat16 [16, 384, 768], P('dp'), may hold values from -6 to 6
- segments: int32 [16, 384], P('dp'), may hold values from 0 to 7, never falling along the last dimension, each value on 1 to 96 neighbouring positions
- cotangent: bfloat16 [16, 384, 768], P('dp'), may hold values from -6 to 6
- norm_gains: float32 [2, 2, 768], P(None, None, 'dp'), may hold values from 0.5 to 1.5
- shifts: float32 [2, 4, 768], P(None, None, 'dp'), may hold values from -2 to 2
- qkv_weight: float32 [2, 3, 768, 768], P(None, None, 'dp', 'tensor'), may hold values from -0.21875 to 0.21875
- qkv_bias: float32 [2, 3, 768], P(None, None, ('tensor', 'dp')), may hold values from -2 to 2
- out_weight: float32 [2, 768, 768], P(None, 'tensor', 'dp'), may hold values from -0.75 to 0.75
- up_weight: float32 [2, 768, 3072], P(None, 'dp', 'tensor'), may hold values from -0.21875 to 0.21875
- up_bias: float32 [2, 3072], P(None, ('tensor', 'dp')), may hold values from -2 to 2
- down_weight: float32 [2, 3072, 768], P(None, 'tensor', 'dp'), may hold values from -0.15625 to 0.15625
Outputs:
- result: bfloat16 [16, 384, 768], P('dp')
- input_grad: float32 [16, 384, 768], P('dp')
- grad_norm_gains: float32 [2, 2, 768], P(None, None, 'dp')
- grad_shifts: float32 [2, 4, 768], P(None, None, 'dp')
- grad_qkv_weight: float32 [2, 3, 768, 768], P(None, None, 'dp', 'tensor')
- grad_qkv_bias: float32 [2, 3, 768], P(None, None, ('tensor', 'dp'))
- grad_out_weight: float32 [2, 768, 768], P(None, 'tensor', 'dp')
- grad_up_weight: float32 [2, 768, 3072], P(None, 'dp', 'tensor')
- grad_up_bias: float32 [2, 3072], P(None, ('tensor', 'dp'))
- grad_down_weight: float32 [2, 3072, 768], P(None, 'tensor', 'dp')
The draws below stay inside these ranges and needn't reach their ends.
Inputs may be any that keep to these rules, and one draw needn't show every extreme that they name: `segments`: in each row the cell numbers never fall; a cell holds 1 to 96 tokens and some cell of every row exactly that many.
All inputs are finite; a program needn't handle non-finite values.
Results may differ from the reference program's by a relative error of at most 0.02.
Values may be sent and summed in bfloat16 or wider, within the bound.
No kernel may reach another device: no remote copies, remote signals or barrier semaphores. Data moves between devices by JAX's collectives and lax.ppermute only.
A program may use at most 192 MiB of HBM per device.

```python
import math
import jax
import jax.numpy as jnp
import numpy as np
from jax import lax

D = 768
HEADS = 12
HD = 64
FF = 3072
SEQ = 384
LAYERS = 2
ROWS = 16
N_TENSOR = 2


def raised(values, own_key, source, target, blocks, factor):
    owner, partner = [(jnp.arange(values.shape[dim]) // (values.shape[dim] // blocks)).reshape([-1 if axis == dim else 1 for axis in range(values.ndim)]) for dim in (source, target)]
    chosen = jax.random.permutation(own_key, blocks)[partner]
    strong = (owner == chosen) | (owner == (partner + blocks // 2) % blocks)
    return jnp.where(strong, factor * values, values)


def levels(key, dims, split, least, largest):
    level = 1.0
    for dim, blocks in split:
        steps = jax.random.uniform(jax.random.fold_in(jax.random.fold_in(key, 6), dim), (blocks,), jnp.float32, least / len(split), largest / len(split))
        level = level * jnp.repeat(jnp.exp(steps), dims[dim] // blocks).reshape((-1,) + (1,) * (len(dims) - 1 - dim))
    return level


def split_up(amount, total, most, skew):
    portions = [(1 << 20) // math.isqrt(rank ** skew) + 1 for rank in range(2, amount + 1)]
    rest, counts = total - most - (amount - 1), [1] * (amount - 1)
    while rest > 0:
        movable = [i for i in range(amount - 1) if counts[i] < most]
        mass, budget = sum([portions[i] for i in movable]), rest
        for i in movable:
            extra = min(most - counts[i], max(1, budget * portions[i] // mass), rest)
            counts[i] = counts[i] + extra
            rest = rest - extra
    return np.array([most] + counts)


def ragged(stream_key, amount, total, bound, skew):
    if amount == 2:
        one = jax.random.randint(stream_key, (), max(1, total - bound), min(bound, total - 1) + 1)
        return jnp.stack([one, total - one])
    sizes = jnp.asarray(split_up(amount, total, bound, skew), jnp.int32)
    couples = (amount - 1) // 2
    donor, receiver = sizes[1:1 + 2 * couples:2], sizes[2:2 + 2 * couples:2]
    room = jnp.minimum(donor - 1, bound - receiver)
    shifted = jax.random.randint(jax.random.fold_in(stream_key, 1), (couples,), 0, 1 << 20) % (room + 1)
    sizes = sizes.at[1:1 + 2 * couples:2].set(donor - shifted).at[2:2 + 2 * couples:2].set(receiver + shifted)
    return sizes[jax.random.permutation(jax.random.fold_in(stream_key, 2), amount)]


def noise(rng, extent, deviation, limit, shards=(), held_as=jnp.bfloat16):
    factor_of = levels(rng, extent, shards, -0.22, 0.18) if shards else 1.0
    values = jax.random.normal(rng, extent, jnp.float32) * deviation * factor_of
    return jnp.minimum(jnp.maximum(values, -limit), limit).astype(held_as)


def noise_with(own_key, dims, scale, most, shards, heavy, kind=jnp.bfloat16):
    drawn = scale * jax.random.normal(own_key, dims, jnp.float32)
    if shards:
        drawn = drawn * levels(own_key, dims, shards, -0.22, 0.18)
    return jnp.clip(raised(drawn, jax.random.fold_in(own_key, 3), *heavy), -most, most).astype(kind)


def setup_inputs(seed: int = 0) -> dict:
    arg_keys = jax.random.split(jax.random.key(seed), 12)
    return {
        "tokens": noise(arg_keys[0], (ROWS, SEQ, D), 1.0, 6.0, ((0, 16),)),
        "segments": jax.vmap(lambda own: jnp.searchsorted(jnp.cumsum(ragged(own, 8, SEQ, SEQ // 4, 2)), jnp.arange(SEQ), side="right"))(jax.random.split(arg_keys[1], ROWS)).reshape((ROWS, SEQ)).astype(jnp.int32),
        "cotangent": noise_with(arg_keys[2], (ROWS, SEQ, D), 1.0, 6.0, ((0, 16),), (0, 2, 16, 2.0)),
        "norm_gains": jnp.clip(1.0 + 0.1 * jax.random.normal(arg_keys[3], (LAYERS, 2, D), jnp.float32), 0.5, 1.5),
        "shifts": noise(arg_keys[4], (LAYERS, 4, D), 0.3, 2.0, ((2, 16),), jnp.float32),
        "qkv_weight": noise(arg_keys[5], (LAYERS, 3, D, D), D ** -0.5, 0.21875, ((2, 16), (3, 2)), jnp.float32),
        "qkv_bias": noise(arg_keys[6], (LAYERS, 3, D), 0.3, 2.0, ((2, 32),), jnp.float32),
        "out_weight": noise(arg_keys[7], (LAYERS, D, D), (D // 12) ** -0.5, 0.75, ((1, 2), (2, 16)), jnp.float32),
        "up_weight": noise(arg_keys[8], (LAYERS, D, FF), D ** -0.5, 0.21875, ((1, 16), (2, 2)), jnp.float32),
        "up_bias": noise(arg_keys[9], (LAYERS, FF), 0.3, 2.0, ((1, 32),), jnp.float32),
        "down_weight": noise(arg_keys[10], (LAYERS, FF, D), (FF // 2) ** -0.5, 0.15625, ((1, 2), (2, 16)), jnp.float32),
    }


HIGH = lax.Precision.HIGHEST
EPSILON = 1e-05
MASKED = -1e+30

@jax.custom_vjp
def low(v):
    return lax.optimization_barrier(v.astype(jnp.bfloat16)).astype(jnp.float32)

@jax.custom_vjp
def low_back(v):
    return v

def low_keep(v):
    return (low(v), None)

def low_pass(kept, grad):
    return (grad,)

def back_keep(v):
    return (v, None)

def back_low(kept, grad):
    return (low(grad),)
low.defvjp(low_keep, low_pass)
low_back.defvjp(back_keep, back_low)

def layer_norm(state, gain, shift):
    mean = lax.optimization_barrier(jnp.mean(state, axis=-1, keepdims=True))
    centred = state - mean
    variance = lax.optimization_barrier(jnp.mean(centred * centred, axis=-1, keepdims=True))
    return centred * lax.rsqrt(variance + EPSILON) * gain + shift

def attend_row(pair):
    proj, seg_row = pair
    query = proj[:, 0].reshape(SEQ, HEADS, HD)
    keys = proj[:, 1].reshape(SEQ, HEADS, HD)
    values = proj[:, 2].reshape(SEQ, HEADS, HD)
    raw = jnp.einsum('qhe,khe->hqk', query, keys, precision=HIGH) * HD ** (-0.5)
    same = seg_row[:, None] == seg_row[None, :]
    scores = low_back(jnp.where(same[None, :, :], raw, MASKED))
    probs = low(jax.nn.softmax(scores, axis=-1))
    mixed = jnp.einsum('hqk,khe->qhe', probs, values, precision=HIGH)
    return mixed.reshape(SEQ, HEADS * HD)

def encoder_layer(state, seg, weights):
    gains, shifts, w_qkv, b_qkv, w_out, w_up, b_up, w_down = [low(w) for w in weights]
    group = state.shape[0]
    first = low(layer_norm(state, gains[0], shifts[0]))
    proj = jnp.einsum('rsd,cde->rsce', first, w_qkv, precision=HIGH) + b_qkv[None, None]
    proj = low(low_back(proj))
    attn = low(low_back(lax.map(jax.checkpoint(attend_row), (proj, seg))))
    split_attn = attn.reshape(group, SEQ, N_TENSOR, D // N_TENSOR)
    parts = low(jnp.einsum('rstk,tkd->rstd', split_attn, w_out.reshape(N_TENSOR, D // N_TENSOR, D), precision=HIGH))
    middle = state + low_back(lax.optimization_barrier(jnp.sum(parts, axis=2))) + shifts[2]
    second = low(layer_norm(middle, gains[1], shifts[1]))
    hidden_in = low_back(jnp.einsum('rsd,df->rsf', second, w_up, precision=HIGH) + b_up)
    hidden = low(jax.nn.gelu(hidden_in, approximate=False))
    split_hidden = hidden.reshape(group, SEQ, N_TENSOR, FF // N_TENSOR)
    parts_two = low(jnp.einsum('rstk,tkd->rstd', split_hidden, w_down.reshape(N_TENSOR, FF // N_TENSOR, D), precision=HIGH))
    return middle + low_back(lax.optimization_barrier(jnp.sum(parts_two, axis=2))) + shifts[3]

def whole_model(state, seg, params):
    for depth in range(LAYERS):
        state = encoder_layer(state, seg, tuple((w[depth] for w in params)))
    return state

def reference(tokens, segments, cotangent, norm_gains, shifts, qkv_weight, qkv_bias, out_weight, up_weight, up_bias, down_weight):
    params = (norm_gains, shifts, qkv_weight, qkv_bias, out_weight, up_weight, up_bias, down_weight)
    group = math.gcd(ROWS, max(1, 4096 // SEQ))
    steps_count = ROWS // group
    states = tokens.astype(jnp.float32).reshape(steps_count, group, SEQ, D)
    seg_all = segments.reshape(steps_count, group, SEQ)
    cot_all = cotangent.astype(jnp.float32).reshape(steps_count, group, SEQ, D)

    def step(totals, item):
        state, seg, cot = item
        output, pull = jax.vjp(lambda inputs, weights: whole_model(inputs, seg, weights), state, params)
        grad_state, grad_params = pull(cot)
        totals = jax.tree.map(jnp.add, totals, grad_params)
        return (totals, (output, grad_state))
    zeros = jax.tree.map(jnp.zeros_like, params)
    grads, (outputs, grad_states) = lax.scan(step, zeros, (states, seg_all, cot_all))
    result = outputs.reshape(ROWS, SEQ, D).astype(jnp.bfloat16)
    input_grad = grad_states.reshape(ROWS, SEQ, D)
    return (result, input_grad, grads[0], grads[1], grads[2], grads[3], grads[4], grads[5], grads[6], grads[7])
```

```python
import functools
import math

import jax
import jax.numpy as jnp
from jax import lax
from jax.experimental import pallas as pl
from jax.experimental.pallas import tpu as pltpu
from jax.sharding import PartitionSpec as P

HD = 64
EPSILON = 1e-05
MASKED = -1e30
BF = jnp.bfloat16
F32 = jnp.float32
SEGMENT_MAX = 96
QUERY_BLOCK = 128
HIDDEN_BLOCK = 256
LANES = 128

SZ, SY, SX = 4, 2, 2
PARTS = SZ * SY * SX


def contract(left, right, left_dim, right_dim):
    dims = (((left_dim,), (right_dim,)), ((), ()))
    return lax.dot_general(left, right, dims, preferred_element_type=F32)


def dot_nn(left, right):
    return contract(left, right, 1, 0)


def dot_nt(left, right):
    return contract(left, right, 1, 1)


def dot_tn(left, right):
    return contract(left, right, 0, 0)


def normed(state):
    mean = jnp.mean(state, axis=-1, keepdims=True)
    centred = state - mean
    inverse = lax.rsqrt(jnp.mean(centred * centred, axis=-1, keepdims=True) + EPSILON)
    return centred * inverse, inverse


def norm_back(grad, norm, inverse, gain):
    grad_gain = jnp.sum(grad * norm, axis=0, keepdims=True)
    grad_shift = jnp.sum(grad, axis=0, keepdims=True)
    scaled = grad * gain
    back = inverse * (
        scaled
        - jnp.mean(scaled, axis=-1, keepdims=True)
        - norm * jnp.mean(scaled * norm, axis=-1, keepdims=True)
    )
    return back, grad_gain, grad_shift


def query_blocks(length):
    blocks = []
    for start in range(0, length, QUERY_BLOCK):
        low = max(0, start - SEGMENT_MAX + 1) // QUERY_BLOCK * QUERY_BLOCK
        high = min(length, -(-(start + QUERY_BLOCK + SEGMENT_MAX - 1) // QUERY_BLOCK) * QUERY_BLOCK)
        blocks.append((start, low, high))
    return blocks


def call(kernel, outs, args, scratch=(), flops=0, limit=40):
    shapes = [jax.ShapeDtypeStruct(shape, kind) for shape, kind in outs]
    moved = sum(math.prod(a.shape) * a.dtype.itemsize for a in list(args) + shapes)
    vmem = pl.BlockSpec(memory_space=pltpu.VMEM)
    return pl.pallas_call(
        kernel,
        out_shape=shapes,
        in_specs=[vmem] * len(args),
        out_specs=[vmem] * len(outs),
        scratch_shapes=list(scratch),
        cost_estimate=pl.CostEstimate(flops=flops, bytes_accessed=moved, transcendentals=0),
        compiler_params=pltpu.CompilerParams(vmem_limit_bytes=limit << 20),
    )(*args)


def flip(value, mask):
    count = lax.axis_size("dp")
    return lax.ppermute(value, "dp", [(i, i ^ mask) for i in range(count)])


def swap(part):
    count = lax.axis_size("tensor")
    return lax.ppermute(part, "tensor", [(i, (i + 1) % count) for i in range(count)])


def place():
    me = lax.axis_index("dp")
    return me // (SY * SX), (me // SX) % SY, me % SX


def relative(order, z, y, x):
    blocks = []
    for number in range(PARTS):
        first, second, kz = number // 8, number // 4 % 2, number % 4
        ky, kx = (second, first) if order == "x" else (first, second)
        blocks.append(((z ^ kz) * SY + (y ^ ky)) * SX + (x ^ kx))
    return blocks


def join_kernel(split, *refs):
    blocks, front, back = refs[:-2], refs[-2], refs[-1]
    rows = blocks[0].shape[0]
    for number, ref in enumerate(blocks):
        front[number * rows : (number + 1) * rows, :] = ref[:, :split]
        back[number * rows : (number + 1) * rows, :] = ref[:, split:]


def place_kernel(split, *refs):
    out = refs[-1]
    z, y, x = place()
    rows = out.shape[0] // PARTS
    for part, order in enumerate("yx"):
        start = part * split
        for number, block in enumerate(relative(order, z, y, x)):
            ref, line = refs[part * 4 + number // 4], number % 4
            out[pl.ds(pl.multiple_of(block * rows, 16), rows), start : start + ref.shape[1]] = ref[
                line * rows : (line + 1) * rows, :
            ]


def gather(piece, planned):
    rows, columns = piece.shape
    if not planned:
        return lax.all_gather(piece, "dp", axis=0, tiled=True)
    arrived = [piece] + [flip(piece, kz * SY * SX) for kz in range(1, SZ)]
    split = columns // 256 * 128
    front, back = call(
        functools.partial(join_kernel, split),
        [((SZ * rows, split), BF), ((SZ * rows, columns - split), BF)],
        arrived,
        limit=16,
    )
    front_y, back_x = flip(front, SX), flip(back, 1)
    front_x, back_y = flip(front, 1), flip(back, SX)
    front_xy, back_xy = flip(front_y, 1), flip(back_x, SX)
    parts = [front, front_x, front_y, front_xy, back, back_y, back_x, back_xy]
    return call(
        functools.partial(place_kernel, split),
        [((PARTS * rows, columns), BF)],
        parts,
        limit=16,
    )[0]


def product_kernel(order, shares, *refs):
    count = 1 if order is None else 2
    scratch = refs[-1]
    outs = refs[-1 - count : -1]
    width = scratch.shape[0]
    blocks = None if order is None else relative(order, *place())
    rows = width // PARTS

    def put(start, size):
        if order is None:
            outs[0][:, start : start + size] = scratch[:, :size]
            return
        for number, block in enumerate(blocks):
            out, line = outs[number // 8 == 0], number % 8
            out[line * rows : (line + 1) * rows, start : start + size] = scratch[
                pl.ds(pl.multiple_of(block * rows, 16), rows), :size
            ]

    start, place_in = 0, 0
    for kind in shares:
        if kind == "ready":
            ready = refs[place_in]
            place_in += 1
            size = ready.shape[1]
            scratch[:, :size] = ready[...]
            put(start, size)
            start += size
            continue
        left, right = refs[place_in], refs[place_in + 1]
        place_in += 2
        turned = left[...].T
        for first in range(0, right.shape[1], 384):
            size = min(384, right.shape[1] - first)
            scratch[:, :size] = dot_nn(turned, right[:, first : first + size]).astype(BF)
            put(start, size)
            start += size


def products(order, *shares):
    args, kinds, columns, flops = [], [], 0, 0
    for share in shares:
        if isinstance(share, tuple):
            kinds.append("product")
            args += share
            columns += share[1].shape[1]
            width = share[0].shape[1]
            flops += 2 * math.prod(share[0].shape) * share[1].shape[1]
        else:
            kinds.append("ready")
            args.append(share)
            columns += share.shape[1]
            width = share.shape[0]
    outs = [((width, columns), BF)] if order is None else [((width // 2, columns), BF)] * 2
    return call(
        functools.partial(product_kernel, order, tuple(kinds)),
        outs,
        args,
        scratch=[pltpu.VMEM((width, 384), BF)],
        flops=flops,
        limit=24,
    )


def fold_kernel(keep, moved, away, stay):
    half = keep.shape[0] // 2
    total = keep[...].astype(F32) + moved[...].astype(F32)
    stay[...] = total[:half].astype(BF)
    away[...] = total[half:].astype(BF)


def line_kernel(keep_a, moved_a, keep_b, moved_b, *outs):
    rows = keep_a.shape[0] // SZ
    split = keep_a.shape[1]
    for number, out in enumerate(outs):
        line = slice(number * rows, (number + 1) * rows)
        total_a = keep_a[line, :].astype(F32) + moved_a[line, :].astype(F32)
        total_b = keep_b[line, :].astype(F32) + moved_b[line, :].astype(F32)
        out[:, :split] = total_a.astype(out.dtype)
        out[:, split:] = total_b.astype(out.dtype)


def scatter(half_a, half_b):
    ends = []
    for (away, stay), first, second in ((half_a, 1, SX), (half_b, SX, 1)):
        moved = flip(away, first)
        shape = (stay.shape[0] // 2, stay.shape[1])
        away, stay = call(fold_kernel, [(shape, BF)] * 2, [stay, moved], limit=16)
        ends += [stay, flip(away, second)]
    rows = ends[0].shape[0] // SZ
    shape = (rows, ends[0].shape[1] + ends[2].shape[1])
    own, *line = call(line_kernel, [(shape, F32)] + [(shape, BF)] * (SZ - 1), ends, limit=16)
    return [own] + [flip(block, kz * SY * SX) for kz, block in zip(range(1, SZ), line)]


def lanes_of(layers):
    up = 6 * layers
    return up, up + 2 * layers


def pack_kernel(gains, shifts, b_up, b_qkv, qkv, out, up, down, *refs):
    scratch, outs = refs[-1], refs[:-1]
    layers, _, rows, width = qkv.shape
    lane_up, lane_qkv = lanes_of(layers)
    scratch[...] = jnp.zeros(scratch.shape, F32)
    for layer in range(layers):
        base = 6 * layer
        scratch[base : base + 2, :rows] = gains[layer]
        scratch[base + 2 : base + 6, :rows] = shifts[layer]
        line = lane_up + 2 * layer
        scratch[line : line + 2, :rows] = b_up[2 * layer : 2 * layer + 2, :]
        line = lane_qkv + 3 * layer
        scratch[line : line + 3, : b_qkv.shape[2]] = b_qkv[layer]
    for layer in range(layers):
        first, second = outs[2 * layer], outs[2 * layer + 1]
        for c in range(3):
            first[:, c * width : (c + 1) * width] = qkv[layer, c].astype(BF)
        first[:, 3 * width : 4 * width] = out[layer].astype(BF)
        if layer == 0:
            first[:, 4 * width :] = scratch[...].T[:rows].astype(BF)
        hidden = up.shape[2]
        second[:, :hidden] = up[layer].astype(BF)
        second[:, hidden:] = down[layer].astype(BF)


def unpack_kernel(layers, size, columns, rows_out, up_out, qkv_out, up_scratch, qkv_scratch):
    lane_up, lane_qkv = lanes_of(layers)
    wide = columns[...].astype(F32)
    rows_out[...] = wide.T[: rows_out.shape[0]]
    rows = columns.shape[0] // PARTS
    lane = lax.broadcasted_iota(jnp.int32, (rows, LANES), 1)

    def merged(block, lanes):
        total = jnp.zeros((block.shape[0], LANES), F32)
        for layer, at in enumerate(lanes):
            total = jnp.where(lane[: block.shape[0]] == layer, block[:, at : at + 1], total)
        return total

    width = qkv_out.shape[1] // 3
    for part in range(PARTS):
        block = wide[part * rows : (part + 1) * rows]
        for c in range(2):
            start = (part * 2 + c) * rows
            up_scratch[start : start + rows, :] = merged(
                block, [lane_up + 2 * layer + c for layer in range(layers)]
            )
        for c in range(3):
            start = c * width + part * size
            qkv_scratch[start : start + size, :] = merged(
                block[:size], [lane_qkv + 3 * layer + c for layer in range(layers)]
            )
    up_out[...] = up_scratch[...].T[: up_out.shape[0]]
    qkv_out[...] = qkv_scratch[...].T[: qkv_out.shape[0]]


def pack_grads_kernel(layers, size, *refs):
    out, rows_scratch, up_scratch, qkv_scratch = refs[-4:]
    lane_up, lane_qkv = lanes_of(layers)
    rows_scratch[...] = jnp.zeros(rows_scratch.shape, F32)
    up_scratch[...] = jnp.zeros(up_scratch.shape, F32)
    qkv_scratch[...] = jnp.zeros(qkv_scratch.shape, F32)
    for layer in range(layers):
        given = refs[8 * layer : 8 * layer + 8]
        for number in range(6):
            line = 6 * layer + number
            rows_scratch[line : line + 1, :] = given[number][...]
        up_scratch[layer : layer + 1, :] = given[6][...]
        qkv_scratch[layer : layer + 1, :] = given[7][...]
    columns = rows_scratch[...].T
    up, qkv = up_scratch[...].T, qkv_scratch[...].T
    rows = out.shape[0] // PARTS
    width = qkv.shape[0] // 3
    lane = lax.broadcasted_iota(jnp.int32, (rows, LANES), 1)
    for part in range(PARTS):
        total = columns[part * rows : (part + 1) * rows]
        for layer in range(layers):
            for c in range(2):
                start = (part * 2 + c) * rows
                value = up[start : start + rows, layer : layer + 1]
                total = jnp.where(lane == lane_up + 2 * layer + c, value, total)
            for c in range(3):
                start = c * width + part * size
                value = jnp.concatenate(
                    [
                        qkv[start : start + size, layer : layer + 1],
                        jnp.zeros((rows - size, 1), F32),
                    ],
                    axis=0,
                )
                total = jnp.where(lane == lane_qkv + 3 * layer + c, value, total)
        out[part * rows : (part + 1) * rows, :] = total.astype(BF)


def finish_kernel(layers, *refs):
    terms, outs = refs[: 8 * layers], refs[8 * layers :]
    gains, shifts, qkv, b_qkv, out, up, b_up, down = outs
    rows, width = qkv.shape[2:]
    hidden = up.shape[2]
    lane_up, lane_qkv = lanes_of(layers)
    for layer in range(layers):
        first = terms[8 * layer : 8 * layer + 4]
        second = terms[8 * layer + 4 : 8 * layer + 8]

        def total(group, start, size):
            value = group[0][:, start : start + size]
            for term in group[1:]:
                value = value + term[:, start : start + size].astype(F32)
            return value

        for c in range(3):
            qkv[layer, c] = total(first, c * width, width)
        out[layer] = total(first, 3 * width, width)
        down[layer] = total(second, 0, hidden)
        up[layer] = total(second, hidden, hidden)
        if layer == 0:
            small = total(first, 4 * width, LANES)
            small = jnp.concatenate([small, jnp.zeros((LANES - rows, LANES), F32)], axis=0).T
            for k in range(layers):
                gains[k] = small[6 * k : 6 * k + 2, :rows]
                shifts[k] = small[6 * k + 2 : 6 * k + 6, :rows]
                line = lane_up + 2 * k
                b_up[2 * k : 2 * k + 2, :] = small[line : line + 2, :rows]
                line = lane_qkv + 3 * k
                b_qkv[k] = small[line : line + 3, : b_qkv.shape[2]]


def attention_forward_kernel(layer, *refs):
    if layer == 0:
        tokens, *refs = refs
        state = tokens[...].astype(F32)
    else:
        middle, own, moved, *refs = refs
    rows, b_qkv, weight, seg_row, seg_column, x_ref, first_ref, proj_ref, attn_ref, lse_ref, part_ref, turned = refs
    base = 6 * layer
    if layer > 0:
        state = middle[...] + (own[...].astype(F32) + moved[...].astype(F32))
        state = state + rows[base - 1 : base, :]
    x_ref[...] = state
    norm, _ = normed(state)
    first = (norm * rows[base : base + 1, :] + rows[base + 2 : base + 3, :]).astype(BF)
    first_ref[...] = first
    width = weight.shape[1] // 512 * 128
    proj = dot_nn(first, weight[:, : 3 * width]) + b_qkv[layer : layer + 1, :]
    proj_ref[...] = proj.astype(BF).T
    length = state.shape[0]
    lse_ref[...] = jnp.zeros(lse_ref.shape, F32)
    for head in range(width // HD):
        own_rows = slice(head * HD, (head + 1) * HD)
        query = proj_ref[own_rows, :] * BF(HD**-0.5)
        keys = proj_ref[width + head * HD : width + (head + 1) * HD, :]
        values = proj_ref[2 * width + head * HD : 2 * width + (head + 1) * HD, :]
        for start, low, high in query_blocks(length):
            block = slice(start, start + QUERY_BLOCK)
            scores = dot_tn(keys[:, low:high], query[:, block])
            same = seg_column[low:high, :] == seg_row[:, block]
            scores = jnp.where(same, scores, MASKED)
            highest = jnp.max(scores, axis=0, keepdims=True)
            unnormed = jnp.exp(scores - highest)
            summed = jnp.sum(unnormed, axis=0, keepdims=True)
            lse_ref[head : head + 1, block] = highest + jnp.log(summed)
            probs = (unnormed * (1.0 / summed)).astype(BF)
            turned[own_rows, block] = dot_nn(values[:, low:high], probs).astype(BF)
    attn = turned[...].T
    attn_ref[...] = attn
    part_ref[...] = dot_nt(attn, weight[:, 3 * width : 4 * width]).astype(BF)


def up_kernel(layer, state, own, moved, rows, b_up, weight, middle_ref, second_ref, hidden_ref, slope_ref):
    base = 6 * layer
    middle = state[...] + (own[...].astype(F32) + moved[...].astype(F32))
    middle = middle + rows[base + 4 : base + 5, :]
    middle_ref[...] = middle
    norm, _ = normed(middle)
    second = (norm * rows[base + 1 : base + 2, :] + rows[base + 3 : base + 4, :]).astype(BF)
    second_ref[...] = second
    for start in range(0, hidden_ref.shape[1], HIDDEN_BLOCK):
        block = slice(start, start + HIDDEN_BLOCK)
        pre = dot_nn(second, weight[:, block]) + b_up[layer : layer + 1, block]
        below = 0.5 * (1.0 + lax.erf(pre * 0.7071067811865476))
        hidden_ref[:, block] = (pre * below).astype(BF)
        density = jnp.exp(-0.5 * pre * pre) * 0.3989422804014327
        slope_ref[:, block] = below + pre * density


def down_kernel(hidden, weight, part_ref):
    half = weight.shape[1] // 2
    part_ref[...] = dot_nt(hidden[...], weight[:, half:]).astype(BF)


def hidden_back_kernel(layer, last, *refs):
    if last:
        cotangent, *refs = refs
        grad = cotangent[...].astype(F32)
    else:
        above, own, moved, state, *refs = refs
    rows, weight, slope, grad_ref, low_ref, pre_ref, part_ref, shift_ref, bias_ref, *more = refs
    if not last:
        gain_ref, norm_shift_ref = more
        arrived = own[...].astype(F32) + moved[...].astype(F32)
        norm, inverse = normed(state[...])
        upper = 6 * (layer + 1)
        back, gain_ref[...], norm_shift_ref[...] = norm_back(
            arrived, norm, inverse, rows[upper : upper + 1, :]
        )
        grad = above[...] + back
    grad_ref[...] = grad
    low = grad.astype(BF)
    low_ref[...] = low
    shift_ref[...] = jnp.sum(grad, axis=0, keepdims=True)
    hidden = weight.shape[1] // 2
    for start in range(0, hidden, HIDDEN_BLOCK):
        block = slice(start, start + HIDDEN_BLOCK)
        back = dot_nn(low, weight[:, hidden + start : hidden + start + HIDDEN_BLOCK])
        pre = (back * slope[:, block]).astype(BF)
        pre_ref[:, block] = pre
        bias_ref[:, block] = jnp.sum(pre.astype(F32), axis=0, keepdims=True)
    part_ref[...] = dot_nt(pre_ref[...], weight[:, :hidden]).astype(BF)


def attention_back_kernel(layer, *refs):
    (grad, own, moved, middle, rows, weight, proj, lse, seg_row, seg_column) = refs[:10]
    (below_ref, low_ref, grad_proj_ref, part_ref, gain_ref, norm_shift_ref, shift_ref, bias_ref) = refs[10:18]
    turned, turned_proj, probs_ref, scores_ref = refs[18:]
    base = 6 * layer
    arrived = own[...].astype(F32) + moved[...].astype(F32)
    norm, inverse = normed(middle[...])
    back, gain_ref[...], norm_shift_ref[...] = norm_back(
        arrived, norm, inverse, rows[base + 1 : base + 2, :]
    )
    below = grad[...] + back
    below_ref[...] = below
    shift_ref[...] = jnp.sum(below, axis=0, keepdims=True)
    low = below.astype(BF)
    low_ref[...] = low
    width = weight.shape[1] // 512 * 128
    turned[...] = dot_nn(low, weight[:, 3 * width : 4 * width]).astype(BF).T
    length = below.shape[0]
    probs_ref[...] = jnp.zeros(probs_ref.shape, BF)
    scores_ref[...] = jnp.zeros(scores_ref.shape, BF)
    for head in range(width // HD):
        slot = head % 2
        own_rows = slice(head * HD, (head + 1) * HD)
        key_rows = slice(width + head * HD, width + (head + 1) * HD)
        value_rows = slice(2 * width + head * HD, 2 * width + (head + 1) * HD)
        query = proj[own_rows, :] * BF(HD**-0.5)
        keys, values, mixed = proj[key_rows, :], proj[value_rows, :], turned[own_rows, :]
        for start, low_key, high in query_blocks(length):
            block = slice(start, start + QUERY_BLOCK)
            scores = dot_tn(keys[:, low_key:high], query[:, block])
            same = seg_column[low_key:high, :] == seg_row[:, block]
            scores = jnp.where(same, scores, MASKED)
            probs = jnp.exp(scores - lse[head : head + 1, block])
            probs_ref[slot, low_key:high, block] = probs.astype(BF)
            grad_probs = dot_tn(values[:, low_key:high], mixed[:, block])
            centre = jnp.sum(probs * grad_probs, axis=0, keepdims=True)
            scores_ref[slot, low_key:high, block] = (probs * (grad_probs - centre)).astype(BF)
        grad_scores = scores_ref[slot]
        scaled_keys = keys * BF(HD**-0.5)
        turned_proj[own_rows, :] = dot_nn(scaled_keys, grad_scores).astype(BF)
        turned_proj[key_rows, :] = dot_nt(query, grad_scores).astype(BF)
        turned_proj[value_rows, :] = dot_nt(mixed, probs_ref[slot]).astype(BF)
    grad_proj = turned_proj[...].T
    grad_proj_ref[...] = grad_proj
    bias_ref[...] = jnp.sum(grad_proj.astype(F32), axis=0, keepdims=True)
    part_ref[...] = dot_nt(grad_proj, weight[:, : 3 * width]).astype(BF)


def input_back_kernel(above, own, moved, tokens, rows, out_ref, gain_ref, norm_shift_ref):
    arrived = own[...].astype(F32) + moved[...].astype(F32)
    norm, inverse = normed(tokens[...].astype(F32))
    back, gain_ref[...], norm_shift_ref[...] = norm_back(arrived, norm, inverse, rows[:1, :])
    out_ref[...] = above[...] + back


def packed_plainly(norm_gains, shifts, qkv_weight, qkv_bias, out_turned, up_weight, up_bias, down_turned):
    layers = norm_gains.shape[0]
    pieces = []
    for layer in range(layers):
        first = [qkv_weight[layer, c] for c in range(3)] + [out_turned[layer]]
        pieces.append(jnp.concatenate(first, axis=1).astype(BF))
        pieces.append(jnp.concatenate([up_weight[layer], down_turned[layer]], axis=1).astype(BF))

    def whole(vector, axis):
        return lax.all_gather(vector.astype(BF), "dp", axis=axis, tiled=True).astype(F32)

    both = jnp.concatenate([norm_gains, shifts], axis=1)
    rows = whole(both, 2).reshape(6 * layers, -1)
    rows = jnp.pad(rows, ((0, -rows.shape[0] % 16), (0, 0)))
    up = jnp.pad(whole(up_bias, 1), ((0, 8 - layers), (0, 0)))
    qkv = jnp.pad(whole(qkv_bias, 2).reshape(layers, -1), ((0, 8 - layers), (0, 0)))
    return pieces, (rows, up, qkv)


def on_device(
    tokens,
    segments,
    cotangent,
    norm_gains,
    shifts,
    qkv_weight,
    qkv_bias,
    out_weight,
    up_weight,
    up_bias,
    down_weight,
):
    count, length, width = tokens.shape
    layers, _, rows, head_width = qkv_weight.shape
    hidden = up_weight.shape[2]
    planned = lax.axis_size("dp") == PARTS and rows % 48 == 0
    tokens = tokens.reshape(length, width)
    cotangent = cotangent.reshape(length, width)
    seg_row, seg_column = segments.reshape(1, length), segments.reshape(length, 1)
    out_turned, down_turned = jnp.swapaxes(out_weight, 1, 2), jnp.swapaxes(down_weight, 1, 2)

    if planned:
        size = qkv_bias.shape[2]
        outs = []
        for layer in range(layers):
            outs.append(((rows, 4 * head_width + (LANES if layer == 0 else 0)), BF))
            outs.append(((rows, 2 * hidden), BF))
        up_lines = up_bias.reshape(2 * layers, rows)
        args = [norm_gains, shifts, up_lines, qkv_bias, qkv_weight, out_turned, up_weight, down_turned]
        pieces = call(pack_kernel, outs, args, scratch=[pltpu.VMEM((LANES, LANES), F32)], limit=24)
    else:
        pieces, vectors = packed_plainly(
            norm_gains, shifts, qkv_weight, qkv_bias, out_turned, up_weight, up_bias, down_turned
        )
    weights = [gather(piece, planned) for piece in pieces]
    if planned:
        vectors = call(
            functools.partial(unpack_kernel, layers, size),
            [((16, width), F32), ((8, hidden), F32), ((8, 3 * head_width), F32)],
            [weights[0][:, 4 * head_width :]],
            scratch=[pltpu.VMEM((hidden, LANES), F32), pltpu.VMEM((3 * head_width, LANES), F32)],
            limit=16,
        )
    rows_all, b_up, b_qkv = vectors

    token_f32, token_bf = ((length, width), F32), ((length, width), BF)
    proj_flops = 2 * length * width * 3 * head_width
    out_flops = 2 * length * width * head_width
    hidden_flops = 2 * length * width * hidden
    head_flops = 2 * length * length * head_width

    records, before = [], [tokens]
    for layer in range(layers):
        w_qkvo, w_ffn = weights[2 * layer], weights[2 * layer + 1]
        state, first, proj, attn, lse, part = call(
            functools.partial(attention_forward_kernel, layer),
            [
                token_f32,
                token_bf,
                ((3 * head_width, length), BF),
                ((length, head_width), BF),
                ((8, length), F32),
                token_bf,
            ],
            before + [rows_all, b_qkv, w_qkvo, seg_row, seg_column],
            scratch=[pltpu.VMEM((head_width, length), BF)],
            flops=proj_flops + out_flops + 2 * head_flops,
        )
        middle, second, active, slope = call(
            functools.partial(up_kernel, layer),
            [token_f32, token_bf, ((length, hidden), BF), ((length, hidden), F32)],
            [state, part, swap(part), rows_all, b_up, w_ffn[:, :hidden]],
            flops=2 * hidden_flops,
        )
        (part,) = call(down_kernel, [token_bf], [active, w_ffn], flops=hidden_flops)
        before = [middle, part, swap(part)]
        records.append((state, first, proj, attn, lse, middle, second, active, slope))
    middle, part, moved = before
    result = middle + (part.astype(F32) + moved.astype(F32)) + rows_all[6 * layers - 1]
    result = result.astype(BF).reshape(count, length, width)

    vector_grads = [[None] * 8 for _ in range(layers)]
    orders = ("x", "y") if planned else (None, None)
    line = ((1, width), F32)
    above, terms, products_of = [cotangent], [None] * (2 * layers), [None] * (2 * layers)
    for layer in reversed(range(layers)):
        w_qkvo, w_ffn = weights[2 * layer], weights[2 * layer + 1]
        state, first, proj, attn, lse, middle, second, active, slope = records[layer]
        last = layer == layers - 1
        outs = [token_f32, token_bf, ((length, hidden), BF), token_bf, line, ((1, hidden), F32)]
        grad, low, pre, part, grad_shift, grad_up, *more = call(
            functools.partial(hidden_back_kernel, layer, last),
            outs + ([] if last else [line] * 2),
            above + [rows_all, w_ffn, slope],
            flops=2 * hidden_flops,
        )
        mine = vector_grads[layer]
        mine[5], mine[6] = grad_shift, grad_up
        if not last:
            vector_grads[layer + 1][0], vector_grads[layer + 1][2] = more
        products_of[2 * layer + 1] = [(low, active)], [(second, pre)]
        below, low, grad_proj, part, *more = call(
            functools.partial(attention_back_kernel, layer),
            [
                token_f32,
                token_bf,
                ((length, 3 * head_width), BF),
                token_bf,
                line,
                line,
                line,
                ((1, 3 * head_width), F32),
            ],
            [grad, part, swap(part), middle, rows_all, w_qkvo, proj, lse, seg_row, seg_column],
            scratch=[
                pltpu.VMEM((head_width, length), BF),
                pltpu.VMEM((3 * head_width, length), BF),
                pltpu.VMEM((2, length, length), BF),
                pltpu.VMEM((2, length, length), BF),
            ],
            flops=proj_flops + out_flops + 5 * head_flops,
        )
        mine[1], mine[3], mine[4], mine[7] = more
        products_of[2 * layer] = (
            [(first, grad_proj[:, : 2 * head_width])],
            [(first, grad_proj[:, 2 * head_width :]), (low, attn)],
        )
        above = [below, part, swap(part), state]
        for number in (2 * layer + 1, 2 * layer) if layer > 0 else (1,):
            halves = [products(o, *p) for o, p in zip(orders, products_of[number])]
            terms[number] = scatter(*halves) if planned else halves
    below, part, moved, _ = above
    input_grad, grad_gain, grad_shift = call(
        input_back_kernel, [token_f32, line, line], [below, part, moved, tokens, rows_all]
    )
    vector_grads[0][0], vector_grads[0][2] = grad_gain, grad_shift
    input_grad = input_grad.reshape(count, length, width)

    if planned:
        (columns,) = call(
            functools.partial(pack_grads_kernel, layers, size),
            [((width, LANES), BF)],
            [vector for mine in vector_grads for vector in mine],
            scratch=[
                pltpu.VMEM((LANES, width), F32),
                pltpu.VMEM((LANES, hidden), F32),
                pltpu.VMEM((LANES, 3 * head_width), F32),
            ],
            limit=16,
        )
        front, back = products_of[0]
        terms[0] = scatter(products("x", *front), products("y", *back, columns))
        outs = [
            (norm_gains.shape, F32),
            (shifts.shape, F32),
            (qkv_weight.shape, F32),
            (qkv_bias.shape, F32),
            (out_turned.shape, F32),
            (up_weight.shape, F32),
            (up_lines.shape, F32),
            (down_turned.shape, F32),
        ]
        given = [term for number in range(2 * layers) for term in terms[number]]
        done = call(functools.partial(finish_kernel, layers), outs, given, limit=24)
        gains, shift, qkv, b_qkv_grad, out, up, b_up_grad, down = done
        b_up_grad = b_up_grad.reshape(up_bias.shape)
    else:
        halves = [products(o, *p) for o, p in zip(orders, products_of[0])]
        terms[0] = halves

        def shared(value, axis):
            return lax.psum_scatter(value, "dp", scatter_dimension=axis, tiled=True)

        summed = [[shared(half[0].astype(F32), 0) for half in pair] for pair in terms]
        cut = [jnp.concatenate(summed[2 * layer], axis=1) for layer in range(layers)]
        qkv = jnp.stack(
            [
                jnp.stack([piece[:, c * head_width : (c + 1) * head_width] for c in range(3)])
                for piece in cut
            ]
        )
        out = jnp.stack([piece[:, 3 * head_width :] for piece in cut])
        down = jnp.stack([summed[2 * layer + 1][0] for layer in range(layers)])
        up = jnp.stack([summed[2 * layer + 1][1] for layer in range(layers)])
        both = jnp.stack([jnp.concatenate(mine[:6], axis=0) for mine in vector_grads])
        both = shared(both, 2)
        gains, shift = both[:, :2], both[:, 2:]
        b_up_grad = shared(jnp.concatenate([mine[6] for mine in vector_grads], axis=0), 1)
        b_qkv_grad = jnp.stack([mine[7].reshape(3, head_width) for mine in vector_grads])
        b_qkv_grad = shared(b_qkv_grad, 2)
    out, down = jnp.swapaxes(out, 1, 2), jnp.swapaxes(down, 1, 2)
    return (result, input_grad, gains, shift, qkv, b_qkv_grad, out, up, b_up_grad, down)


def solution(mesh):
    weights = (
        P(None, None, "dp"),
        P(None, None, "dp"),
        P(None, None, "dp", "tensor"),
        P(None, None, ("tensor", "dp")),
        P(None, "tensor", "dp"),
        P(None, "dp", "tensor"),
        P(None, ("tensor", "dp")),
        P(None, "tensor", "dp"),
    )
    rows = P("dp", None, None)
    return jax.shard_map(
        on_device,
        mesh=mesh,
        in_specs=(rows, P("dp", None), rows) + weights,
        out_specs=(rows, rows) + weights,
        check_vma=False,
    )
```

```python
import functools
import math

import jax
import jax.numpy as jnp
from jax import lax
from jax.experimental import pallas as pl
from jax.experimental.pallas import tpu as pltpu
from jax.sharding import PartitionSpec as P

HD = 64
EPSILON = 1e-05
MASKED = -1e30
BF = jnp.bfloat16
F32 = jnp.float32
SEGMENT_MAX = 96
QUERY_BLOCK = 128
HIDDEN_BLOCK = 256
LANES = 128
WINDOWS = 2, 2, 3

SZ, SY, SX = 4, 2, 2
PARTS = SZ * SY * SX


def contract(left, right, left_dim, right_dim):
    dims = (((left_dim,), (right_dim,)), ((), ()))
    return lax.dot_general(left, right, dims, preferred_element_type=F32)


def dot_nn(left, right):
    return contract(left, right, 1, 0)


def dot_nt(left, right):
    return contract(left, right, 1, 1)


def dot_tn(left, right):
    return contract(left, right, 0, 0)


def normed(state):
    mean = jnp.mean(state, axis=-1, keepdims=True)
    centred = state - mean
    inverse = lax.rsqrt(jnp.mean(centred * centred, axis=-1, keepdims=True) + EPSILON)
    return centred * inverse, inverse


def norm_back(grad, norm, inverse, gain):
    grad_gain = jnp.sum(grad * norm, axis=0, keepdims=True)
    grad_shift = jnp.sum(grad, axis=0, keepdims=True)
    scaled = grad * gain
    back = inverse * (
        scaled
        - jnp.mean(scaled, axis=-1, keepdims=True)
        - norm * jnp.mean(scaled * norm, axis=-1, keepdims=True)
    )
    return back, grad_gain, grad_shift


def query_blocks(length):
    blocks = []
    for start in range(0, length, QUERY_BLOCK):
        low = max(0, start - SEGMENT_MAX + 1) // QUERY_BLOCK * QUERY_BLOCK
        high = min(length, -(-(start + QUERY_BLOCK + SEGMENT_MAX - 1) // QUERY_BLOCK) * QUERY_BLOCK)
        blocks.append((start, low, high))
    return blocks


def call(kernel, outs, args, scratch=(), flops=0, limit=20, space=pltpu.VMEM):
    shapes = [jax.ShapeDtypeStruct(shape, kind) for shape, kind in outs]
    moved = sum(math.prod(a.shape) * a.dtype.itemsize for a in list(args) + shapes)
    vmem = pl.BlockSpec(memory_space=pltpu.VMEM)
    return pl.pallas_call(
        kernel,
        out_shape=shapes,
        in_specs=[pl.BlockSpec(memory_space=space)] * len(args),
        out_specs=[vmem] * len(outs),
        scratch_shapes=list(scratch),
        cost_estimate=pl.CostEstimate(flops=flops, bytes_accessed=moved, transcendentals=0),
        compiler_params=pltpu.CompilerParams(vmem_limit_bytes=limit << 20),
    )(*args)


def flip(value, mask):
    count = lax.axis_size("dp")
    return lax.ppermute(value, "dp", [(i, i ^ mask) for i in range(count)])


class Link:
    def __init__(self, window):
        self.window, self.sent = window, []

    def send(self, value, mask):
        if len(self.sent) >= self.window:
            value, _ = lax.optimization_barrier((value, self.sent[-self.window]))
        self.sent.append(flip(value, mask))
        return self.sent[-1]


def swap(part):
    count = lax.axis_size("tensor")
    return lax.ppermute(part, "tensor", [(i, (i + 1) % count) for i in range(count)])


def place():
    me = lax.axis_index("dp")
    return me // (SY * SX), (me // SX) % SY, me % SX


def relative(order, y, x):
    blocks = []
    for number in range(PARTS):
        first, second, line = number // 8, number // 4 % 2, number % 4
        ky, kx = (second, first) if order == "x" else (first, second)
        blocks.append((line * SY + (y ^ ky)) * SX + (x ^ kx))
    return blocks


def join_kernel(split, *refs):
    blocks, front, back = refs[:-2], refs[-2], refs[-1]
    rows = front.shape[0] // SZ
    z = place()[0]
    for distance, ref in enumerate(blocks):
        line = pl.ds(pl.multiple_of((z ^ distance) * rows, 16), rows)
        front[line, :] = ref[:, :split]
        back[line, :] = ref[:, split:]


def cut_kernel(line, *outs):
    start = 0
    for out in outs:
        out[...] = line[:, start : start + out.shape[1]]
        start += out.shape[1]


def place_kernel(*refs):
    parts, outs = refs[:8], refs[8:]
    _, y, x = place()
    rows = outs[0].shape[0] // PARTS
    reach = 0
    for half, order in enumerate("yx"):
        begin, reach = reach, reach + parts[4 * half].shape[1]
        start = 0
        for out in outs:
            end = start + out.shape[1]
            low, high = max(start, begin), min(end, reach)
            if low < high:
                for number, block in enumerate(relative(order, y, x)):
                    ref, line = parts[half * 4 + number // 4], number % 4
                    out[pl.ds(pl.multiple_of(block * rows, 16), rows), low - start : high - start] = ref[
                        line * rows : (line + 1) * rows, low - begin : high - begin
                    ]
            start = end


def lines():
    across = SY * SX
    return [[z * across + column for z in range(SZ)] for column in range(across)]


def gather(groups):
    along_x, along_y, along_z = (Link(window) for window in WINDOWS)
    whole = []
    for number, (piece, chunks) in enumerate(groups):
        rows = piece.shape[0]
        halves = []
        for widths in chunks:
            split = sum(widths) // 256 * 128
            halves += [split, sum(widths) - split]
        shapes = [((SZ * rows, size), BF) for size in halves]
        if number == 0:
            arrived = [piece] + [along_z.send(piece, kz * SY * SX) for kz in range(1, SZ)]
            cut = call(functools.partial(join_kernel, halves[0]), shapes, arrived, limit=8)
        else:
            line = lax.all_gather(piece, "dp", axis=0, tiled=True, axis_index_groups=lines())
            cut = call(cut_kernel, shapes, [line], limit=16)
        for at, widths in enumerate(chunks):
            front, back = cut[2 * at], cut[2 * at + 1]
            front_y, back_x = along_y.send(front, SX), along_x.send(back, 1)
            front_x, back_y = along_x.send(front, 1), along_y.send(back, SX)
            front_xy, back_xy = along_x.send(front_y, 1), along_y.send(back_x, SX)
            parts = [front, front_x, front_y, front_xy, back, back_y, back_x, back_xy]
            outs = [((PARTS * rows, width), BF) for width in widths]
            whole.append(call(place_kernel, outs, parts, limit=16))
    return whole


def product_kernel(order, shares, *refs):
    count = 1 if order is None else 2
    scratch = refs[-1]
    outs = refs[-1 - count : -1]
    width = scratch.shape[0]
    blocks = None if order is None else relative(order, *place()[1:])
    rows = width // PARTS

    def put(start, size):
        if order is None:
            outs[0][:, start : start + size] = scratch[:, :size]
            return
        for number, block in enumerate(blocks):
            out, line = outs[number // 8 == 0], number % 8
            out[line * rows : (line + 1) * rows, start : start + size] = scratch[
                pl.ds(pl.multiple_of(block * rows, 16), rows), :size
            ]

    start, place_in = 0, 0
    for kind in shares:
        if kind == "ready":
            ready = refs[place_in]
            place_in += 1
            size = ready.shape[1]
            scratch[:, :size] = ready[...]
            put(start, size)
            start += size
            continue
        left, right = refs[place_in], refs[place_in + 1]
        place_in += 2
        turned = left[...].T
        for first in range(0, right.shape[1], 384):
            size = min(384, right.shape[1] - first)
            scratch[:, :size] = dot_nn(turned, right[:, first : first + size]).astype(BF)
            put(start, size)
            start += size


def products(order, *shares):
    args, kinds, columns, flops = [], [], 0, 0
    for share in shares:
        if isinstance(share, tuple):
            kinds.append("product")
            args += share
            columns += share[1].shape[1]
            width = share[0].shape[1]
            flops += 2 * math.prod(share[0].shape) * share[1].shape[1]
        else:
            kinds.append("ready")
            args.append(share)
            columns += share.shape[1]
            width = share.shape[0]
    outs = [((width, columns), BF)] if order is None else [((width // 2, columns), BF)] * 2
    return call(
        functools.partial(product_kernel, order, tuple(kinds)),
        outs,
        args,
        scratch=[pltpu.VMEM((width, 384), BF)],
        flops=flops,
        limit=24,
    )


def fold_kernel(keep, moved, away, stay):
    half = keep.shape[0] // 2
    total = keep[...].astype(F32) + moved[...].astype(F32)
    stay[...] = total[:half].astype(BF)
    away[...] = total[half:].astype(BF)


def line_kernel(keep_a, moved_a, keep_b, moved_b, *outs):
    rows = keep_a.shape[0] // SZ
    split = keep_a.shape[1]
    z = place()[0]
    for distance, out in enumerate(outs):
        line = slice(None)
        if len(outs) > 1:
            line = pl.ds(pl.multiple_of((z ^ distance) * rows, 16), rows)
        total_a = keep_a[line, :].astype(F32) + moved_a[line, :].astype(F32)
        total_b = keep_b[line, :].astype(F32) + moved_b[line, :].astype(F32)
        out[:, :split] = total_a.astype(out.dtype)
        out[:, split:] = total_b.astype(out.dtype)


def after(value, token):
    return lax.optimization_barrier((value, token))[0]


def scatter_begin(links, half_a, half_b):
    along_x, along_y, _ = links
    moved_a, moved_b = along_x.send(half_a[0], 1), along_y.send(half_b[0], SX)
    return (half_a[1], moved_a), (half_b[1], moved_b)


def scatter_fold(links, *halves):
    along_x, along_y, _ = links
    folded = []
    for stay, moved in halves:
        shape = (stay.shape[0] // 2, stay.shape[1])
        folded.append(call(fold_kernel, [(shape, BF)] * 2, [stay, moved], limit=16))
    (away_a, stay_a), (away_b, stay_b) = folded
    moved_a, moved_b = along_y.send(away_a, SX), along_x.send(away_b, 1)
    return [stay_a, moved_a, stay_b, moved_b], [away_a, away_b]


def scatter_end(links, kind, ends):
    along_z = links[2]
    height, columns = ends[0].shape[0], ends[0].shape[1] + ends[2].shape[1]
    if kind == "line":
        (line,) = call(line_kernel, [((height, columns), BF)], ends, limit=16)
        return [
            lax.psum_scatter(
                line, "dp", scatter_dimension=0, tiled=True, axis_index_groups=lines()
            )
        ]
    shape = (height // SZ, columns)
    own, *line = call(line_kernel, [(shape, F32)] + [(shape, BF)] * (SZ - 1), ends, limit=16)
    return [own] + [along_z.send(block, kz * SY * SX) for kz, block in zip(range(1, SZ), line)]


def lanes_of(layers):
    up = 6 * layers
    return up, up + 2 * layers


def pack_first_kernel(*refs):
    given, piece, held, scratch, sems = refs[:6], refs[6], refs[7:13], refs[13], refs[14]
    sources = list(given[:4]) + [given[4].at[0], given[5].at[0]]
    copies = [
        pltpu.make_async_copy(source, target, sems.at[number])
        for number, (source, target) in enumerate(zip(sources, held))
    ]
    for copy in copies:
        copy.start()
    scratch[...] = jnp.zeros(scratch.shape, F32)
    for copy in copies:
        copy.wait()
    gains, shifts, b_up, b_qkv, qkv, out = held
    _, rows, width = qkv.shape
    layers = gains.shape[0]
    lane_up, lane_qkv = lanes_of(layers)
    for layer in range(layers):
        base = 6 * layer
        scratch[base : base + 2, :rows] = gains[layer]
        scratch[base + 2 : base + 6, :rows] = shifts[layer]
        for c in range(2):
            line = lane_up + 2 * layer + c
            scratch[line : line + 1, :rows] = b_up[layer : layer + 1, c * rows : (c + 1) * rows]
        for c in range(3):
            line = lane_qkv + 3 * layer + c
            scratch[line : line + 1, : b_qkv.shape[2]] = b_qkv[c, layer : layer + 1]
    for c in range(3):
        piece[:, c * width : (c + 1) * width] = qkv[c].astype(BF)
    piece[:, 3 * width : 4 * width] = out[...].astype(BF)
    piece[:, 4 * width :] = scratch[...].T[:rows].astype(BF)


def pack_kernel(qkv, out, up, down, *pieces):
    width, hidden = qkv.shape[3], up.shape[2]
    for layer, piece in enumerate(pieces):
        start = 0
        if layer > 0:
            for c in range(3):
                piece[:, c * width : (c + 1) * width] = qkv[layer, c].astype(BF)
            piece[:, 3 * width : 4 * width] = out[layer].astype(BF)
            start = 4 * width
        piece[:, start : start + hidden] = up[layer].astype(BF)
        piece[:, start + hidden :] = down[layer].astype(BF)


def unpack_kernel(layers, size, columns, rows_out, up_out, qkv_out, up_scratch, qkv_scratch):
    lane_up, lane_qkv = lanes_of(layers)
    wide = columns[...].astype(F32)
    rows_out[...] = wide.T[: rows_out.shape[0]]
    rows = columns.shape[0] // PARTS
    lane = lax.broadcasted_iota(jnp.int32, (rows, LANES), 1)

    def merged(block, lanes):
        total = jnp.zeros((block.shape[0], LANES), F32)
        for layer, at in enumerate(lanes):
            total = jnp.where(lane[: block.shape[0]] == layer, block[:, at : at + 1], total)
        return total

    width = qkv_out.shape[1] // 3
    for part in range(PARTS):
        block = wide[part * rows : (part + 1) * rows]
        for c in range(2):
            start = (part * 2 + c) * rows
            up_scratch[start : start + rows, :] = merged(
                block, [lane_up + 2 * layer + c for layer in range(layers)]
            )
        for c in range(3):
            start = c * width + part * size
            qkv_scratch[start : start + size, :] = merged(
                block[:size], [lane_qkv + 3 * layer + c for layer in range(layers)]
            )
    up_out[...] = up_scratch[...].T[: up_out.shape[0]]
    qkv_out[...] = qkv_scratch[...].T[: qkv_out.shape[0]]


def pack_grads_kernel(layers, size, *refs):
    out, rows_scratch, up_scratch, qkv_scratch = refs[-4:]
    lane_up, lane_qkv = lanes_of(layers)
    rows_scratch[...] = jnp.zeros(rows_scratch.shape, F32)
    up_scratch[...] = jnp.zeros(up_scratch.shape, F32)
    qkv_scratch[...] = jnp.zeros(qkv_scratch.shape, F32)
    for layer in range(layers):
        given = refs[8 * layer : 8 * layer + 8]
        for number in range(6):
            line = 6 * layer + number
            rows_scratch[line : line + 1, :] = given[number][...]
        up_scratch[layer : layer + 1, :] = given[6][...]
        qkv_scratch[layer : layer + 1, :] = given[7][...]
    columns = rows_scratch[...].T
    up, qkv = up_scratch[...].T, qkv_scratch[...].T
    rows = out.shape[0] // PARTS
    width = qkv.shape[0] // 3
    lane = lax.broadcasted_iota(jnp.int32, (rows, LANES), 1)
    for part in range(PARTS):
        total = columns[part * rows : (part + 1) * rows]
        for layer in range(layers):
            for c in range(2):
                start = (part * 2 + c) * rows
                value = up[start : start + rows, layer : layer + 1]
                total = jnp.where(lane == lane_up + 2 * layer + c, value, total)
            for c in range(3):
                start = c * width + part * size
                value = jnp.concatenate(
                    [
                        qkv[start : start + size, layer : layer + 1],
                        jnp.zeros((rows - size, 1), F32),
                    ],
                    axis=0,
                )
                total = jnp.where(lane == lane_qkv + 3 * layer + c, value, total)
        out[part * rows : (part + 1) * rows, :] = total.astype(BF)


def finish_kernel(layers, counts, *refs):
    outs, groups, start = refs[sum(counts) :], [], 0
    for count in counts:
        groups.append(refs[start : start + count])
        start += count
    gains, shifts, qkv, b_qkv, out, up, b_up, down = outs
    rows, width = qkv.shape[2:]
    hidden = up.shape[2]
    lane_up, lane_qkv = lanes_of(layers)
    for layer in range(layers):
        first, second = groups[2 * layer], groups[2 * layer + 1]

        def total(group, start, size):
            value = group[0][:, start : start + size].astype(F32)
            for term in group[1:]:
                value = value + term[:, start : start + size].astype(F32)
            return value

        for c in range(3):
            qkv[layer, c] = total(first, c * width, width)
        out[layer] = total(first, 3 * width, width)
        down[layer] = total(second, 0, hidden)
        up[layer] = total(second, hidden, hidden)
        if layer == 0:
            small = total(first, 4 * width, LANES)
            small = jnp.concatenate([small, jnp.zeros((LANES - rows, LANES), F32)], axis=0).T
            for k in range(layers):
                gains[k] = small[6 * k : 6 * k + 2, :rows]
                shifts[k] = small[6 * k + 2 : 6 * k + 6, :rows]
                for c in range(2):
                    line = lane_up + 2 * k + c
                    b_up[k : k + 1, c * rows : (c + 1) * rows] = small[line : line + 1, :rows]
                for c in range(3):
                    line = lane_qkv + 3 * k + c
                    b_qkv[c, k : k + 1] = small[line : line + 1, : b_qkv.shape[2]]


def attention_forward_kernel(layer, *refs):
    if layer == 0:
        tokens, *refs = refs
        state = tokens[...].astype(F32)
    else:
        middle, own, moved, *refs = refs
    rows, b_qkv, weight, seg_row, seg_column, x_ref, first_ref, proj_ref, attn_ref, lse_ref, part_ref, turned = refs
    base = 6 * layer
    if layer > 0:
        state = middle[...] + (own[...].astype(F32) + moved[...].astype(F32))
        state = state + rows[base - 1 : base, :]
    x_ref[...] = state
    norm, _ = normed(state)
    first = (norm * rows[base : base + 1, :] + rows[base + 2 : base + 3, :]).astype(BF)
    first_ref[...] = first
    width = weight.shape[1] // 512 * 128
    proj = dot_nn(first, weight[:, : 3 * width]) + b_qkv[layer : layer + 1, :]
    proj_ref[...] = proj.astype(BF).T
    length = state.shape[0]
    lse_ref[...] = jnp.zeros(lse_ref.shape, F32)
    for head in range(width // HD):
        own_rows = slice(head * HD, (head + 1) * HD)
        query = proj_ref[own_rows, :] * BF(HD**-0.5)
        keys = proj_ref[width + head * HD : width + (head + 1) * HD, :]
        values = proj_ref[2 * width + head * HD : 2 * width + (head + 1) * HD, :]
        for start, low, high in query_blocks(length):
            block = slice(start, start + QUERY_BLOCK)
            scores = dot_tn(keys[:, low:high], query[:, block])
            same = seg_column[low:high, :] == seg_row[:, block]
            scores = jnp.where(same, scores, MASKED)
            highest = jnp.max(scores, axis=0, keepdims=True)
            unnormed = jnp.exp(scores - highest)
            summed = jnp.sum(unnormed, axis=0, keepdims=True)
            lse_ref[head : head + 1, block] = highest + jnp.log(summed)
            probs = (unnormed * (1.0 / summed)).astype(BF)
            turned[own_rows, block] = dot_nn(values[:, low:high], probs).astype(BF)
    attn = turned[...].T
    attn_ref[...] = attn
    part_ref[...] = dot_nt(attn, weight[:, 3 * width : 4 * width]).astype(BF)


def up_kernel(layer, state, own, moved, rows, b_up, weight, middle_ref, second_ref, hidden_ref, slope_ref):
    base = 6 * layer
    middle = state[...] + (own[...].astype(F32) + moved[...].astype(F32))
    middle = middle + rows[base + 4 : base + 5, :]
    middle_ref[...] = middle
    norm, _ = normed(middle)
    second = (norm * rows[base + 1 : base + 2, :] + rows[base + 3 : base + 4, :]).astype(BF)
    second_ref[...] = second
    for start in range(0, hidden_ref.shape[1], HIDDEN_BLOCK):
        block = slice(start, start + HIDDEN_BLOCK)
        pre = dot_nn(second, weight[:, block]) + b_up[layer : layer + 1, block]
        below = 0.5 * (1.0 + lax.erf(pre * 0.7071067811865476))
        hidden_ref[:, block] = (pre * below).astype(BF)
        density = jnp.exp(-0.5 * pre * pre) * 0.3989422804014327
        slope_ref[:, block] = below + pre * density


def down_kernel(hidden, weight, part_ref):
    part_ref[...] = dot_nt(hidden[...], weight[...]).astype(BF)


def hidden_back_kernel(layer, last, *refs):
    if last:
        cotangent, *refs = refs
        grad = cotangent[...].astype(F32)
    else:
        above, own, moved, state, *refs = refs
    rows, w_up, w_down, slope, grad_ref, low_ref, pre_ref, part_ref, shift_ref, bias_ref, *more = refs
    if not last:
        gain_ref, norm_shift_ref = more
        arrived = own[...].astype(F32) + moved[...].astype(F32)
        norm, inverse = normed(state[...])
        upper = 6 * (layer + 1)
        back, gain_ref[...], norm_shift_ref[...] = norm_back(
            arrived, norm, inverse, rows[upper : upper + 1, :]
        )
        grad = above[...] + back
    grad_ref[...] = grad
    low = grad.astype(BF)
    low_ref[...] = low
    shift_ref[...] = jnp.sum(grad, axis=0, keepdims=True)
    for start in range(0, w_up.shape[1], HIDDEN_BLOCK):
        block = slice(start, start + HIDDEN_BLOCK)
        back = dot_nn(low, w_down[:, block])
        pre = (back * slope[:, block]).astype(BF)
        pre_ref[:, block] = pre
        bias_ref[:, block] = jnp.sum(pre.astype(F32), axis=0, keepdims=True)
    part_ref[...] = dot_nt(pre_ref[...], w_up[...]).astype(BF)


def attention_back_kernel(layer, *refs):
    (grad, own, moved, middle, rows, weight, proj, lse, seg_row, seg_column) = refs[:10]
    (below_ref, low_ref, grad_qk_ref, grad_v_ref, part_ref, gain_ref, norm_shift_ref, shift_ref, bias_ref) = refs[10:19]
    turned, turned_proj, probs_ref, scores_ref = refs[19:]
    base = 6 * layer
    arrived = own[...].astype(F32) + moved[...].astype(F32)
    norm, inverse = normed(middle[...])
    back, gain_ref[...], norm_shift_ref[...] = norm_back(
        arrived, norm, inverse, rows[base + 1 : base + 2, :]
    )
    below = grad[...] + back
    below_ref[...] = below
    shift_ref[...] = jnp.sum(below, axis=0, keepdims=True)
    low = below.astype(BF)
    low_ref[...] = low
    width = weight.shape[1] // 512 * 128
    turned[...] = dot_nn(low, weight[:, 3 * width : 4 * width]).astype(BF).T
    length = below.shape[0]
    probs_ref[...] = jnp.zeros(probs_ref.shape, BF)
    scores_ref[...] = jnp.zeros(scores_ref.shape, BF)
    for head in range(width // HD):
        slot = head % 2
        own_rows = slice(head * HD, (head + 1) * HD)
        key_rows = slice(width + head * HD, width + (head + 1) * HD)
        value_rows = slice(2 * width + head * HD, 2 * width + (head + 1) * HD)
        query = proj[own_rows, :] * BF(HD**-0.5)
        keys, values, mixed = proj[key_rows, :], proj[value_rows, :], turned[own_rows, :]
        for start, low_key, high in query_blocks(length):
            block = slice(start, start + QUERY_BLOCK)
            scores = dot_tn(keys[:, low_key:high], query[:, block])
            same = seg_column[low_key:high, :] == seg_row[:, block]
            scores = jnp.where(same, scores, MASKED)
            probs = jnp.exp(scores - lse[head : head + 1, block])
            probs_ref[slot, low_key:high, block] = probs.astype(BF)
            grad_probs = dot_tn(values[:, low_key:high], mixed[:, block])
            centre = jnp.sum(probs * grad_probs, axis=0, keepdims=True)
            scores_ref[slot, low_key:high, block] = (probs * (grad_probs - centre)).astype(BF)
        grad_scores = scores_ref[slot]
        scaled_keys = keys * BF(HD**-0.5)
        turned_proj[own_rows, :] = dot_nn(scaled_keys, grad_scores).astype(BF)
        turned_proj[key_rows, :] = dot_nt(query, grad_scores).astype(BF)
        turned_proj[value_rows, :] = dot_nt(mixed, probs_ref[slot]).astype(BF)
    grad_proj = turned_proj[...].T
    grad_qk_ref[...] = grad_proj[:, : 2 * width]
    grad_v_ref[...] = grad_proj[:, 2 * width :]
    bias_ref[...] = jnp.sum(grad_proj.astype(F32), axis=0, keepdims=True)
    part_ref[...] = dot_nt(grad_proj, weight[:, : 3 * width]).astype(BF)


def input_back_kernel(above, own, moved, tokens, rows, out_ref, gain_ref, norm_shift_ref):
    arrived = own[...].astype(F32) + moved[...].astype(F32)
    norm, inverse = normed(tokens[...].astype(F32))
    back, gain_ref[...], norm_shift_ref[...] = norm_back(arrived, norm, inverse, rows[:1, :])
    out_ref[...] = above[...] + back


def packed_plainly(norm_gains, shifts, qkv_weight, qkv_bias, out_turned, up_weight, up_bias, down_turned):
    layers = norm_gains.shape[0]
    pieces = []
    for layer in range(layers):
        first = [qkv_weight[layer, c] for c in range(3)] + [out_turned[layer]]
        given = [jnp.concatenate(first, axis=1), up_weight[layer], down_turned[layer]]
        pieces.append([lax.all_gather(w.astype(BF), "dp", axis=0, tiled=True) for w in given])

    def whole(vector, axis):
        return lax.all_gather(vector.astype(BF), "dp", axis=axis, tiled=True).astype(F32)

    both = jnp.concatenate([norm_gains, shifts], axis=1)
    rows = whole(both, 2).reshape(6 * layers, -1)
    rows = jnp.pad(rows, ((0, -rows.shape[0] % 16), (0, 0)))
    up = jnp.pad(whole(up_bias, 1), ((0, 8 - layers), (0, 0)))
    qkv = jnp.pad(whole(qkv_bias, 2).reshape(layers, -1), ((0, 8 - layers), (0, 0)))
    return pieces, (rows, up, qkv)


def on_device(
    tokens,
    segments,
    cotangent,
    norm_gains,
    shifts,
    qkv_weight,
    qkv_bias,
    out_weight,
    up_weight,
    up_bias,
    down_weight,
):
    count, length, width = tokens.shape
    layers, _, rows, head_width = qkv_weight.shape
    hidden = up_weight.shape[2]
    planned = lax.axis_size("dp") == PARTS and rows % 48 == 0
    tokens = tokens.reshape(length, width)
    cotangent = cotangent.reshape(length, width)
    seg_row, seg_column = segments.reshape(1, length), segments.reshape(length, 1)
    out_turned, down_turned = jnp.swapaxes(out_weight, 1, 2), jnp.swapaxes(down_weight, 1, 2)

    if planned:
        size = qkv_bias.shape[2]
        bias_turned = jnp.swapaxes(qkv_bias, 0, 1)
        wide = 4 * head_width
        given = [norm_gains, shifts, up_bias, bias_turned, qkv_weight, out_turned]
        held = [a.shape for a in given[:4]] + [a.shape[1:] for a in given[4:]]
        (first_piece,) = call(
            pack_first_kernel,
            [((rows, wide + LANES), BF)],
            given,
            scratch=[pltpu.VMEM(shape, F32) for shape in held]
            + [pltpu.VMEM((LANES, LANES), F32), pltpu.SemaphoreType.DMA((len(held),))],
            limit=8,
            space=pl.ANY,
        )
        shapes = [((rows, 2 * hidden + (wide if layer > 0 else 0)), BF) for layer in range(layers)]
        pieces = call(pack_kernel, shapes, [qkv_weight, out_turned, up_weight, down_turned])
        groups = [(first_piece, [[wide, LANES]]), (pieces[0], [[hidden, hidden]])]
        groups += [(piece, [[wide, hidden], [hidden]]) for piece in pieces[1:]]
        arrays = [array for chunk in gather(groups) for array in chunk]
        columns = arrays.pop(1)
        weights = [arrays[3 * layer : 3 * layer + 3] for layer in range(layers)]
        vectors = call(
            functools.partial(unpack_kernel, layers, size),
            [((16, width), F32), ((8, hidden), F32), ((8, 3 * head_width), F32)],
            [columns],
            scratch=[pltpu.VMEM((hidden, LANES), F32), pltpu.VMEM((3 * head_width, LANES), F32)],
            limit=8,
        )
        links = [Link(window) for window in WINDOWS]
    else:
        weights, vectors = packed_plainly(
            norm_gains, shifts, qkv_weight, qkv_bias, out_turned, up_weight, up_bias, down_turned
        )
    rows_all, b_up, b_qkv = vectors

    token_f32, token_bf = ((length, width), F32), ((length, width), BF)
    proj_flops = 2 * length * width * 3 * head_width
    out_flops = 2 * length * width * head_width
    hidden_flops = 2 * length * width * hidden
    head_flops = 2 * length * length * head_width

    records, before = [], [tokens]
    for layer in range(layers):
        w_qkvo, w_up, w_down = weights[layer]
        state, first, proj, attn, lse, part = call(
            functools.partial(attention_forward_kernel, layer),
            [
                token_f32,
                token_bf,
                ((3 * head_width, length), BF),
                ((length, head_width), BF),
                ((8, length), F32),
                token_bf,
            ],
            before + [rows_all, b_qkv, w_qkvo, seg_row, seg_column],
            scratch=[pltpu.VMEM((head_width, length), BF)],
            flops=proj_flops + out_flops + 2 * head_flops,
        )
        middle, second, active, slope = call(
            functools.partial(up_kernel, layer),
            [token_f32, token_bf, ((length, hidden), BF), ((length, hidden), F32)],
            [state, part, swap(part), rows_all, b_up, w_up],
            flops=2 * hidden_flops,
        )
        (part,) = call(down_kernel, [token_bf], [active, w_down], flops=hidden_flops)
        before = [middle, part, swap(part)]
        records.append((state, first, proj, attn, lse, middle, second, active, slope))
    middle, part, moved = before
    result = middle + (part.astype(F32) + moved.astype(F32)) + rows_all[6 * layers - 1]
    result = result.astype(BF).reshape(count, length, width)

    vector_grads = [[None] * 8 for _ in range(layers)]
    orders = ("x", "y") if planned else (None, None)
    line = ((1, width), F32)
    above, terms = [cotangent], [None] * (2 * layers)
    halves_of, begun, folded = [None] * (2 * layers), [None] * (2 * layers), [None] * (2 * layers)

    def begin(number, front, back):
        halves_of[number] = [products(orders[0], *front), products(orders[1], *back)]
        if planned:
            begun[number] = scatter_begin(links, *halves_of[number])
        return [half[0] for half in halves_of[number]]

    def fold(number, token):
        if not planned:
            return []
        halves = [(after(stay, token), moved) for stay, moved in begun[number]]
        folded[number], sent = scatter_fold(links, *halves)
        return sent

    def end(number, token):
        kind, (stay, *others) = "line" if number else "steps", folded[number]
        terms[number] = scatter_end(links, kind, [after(stay, token)] + others)

    def arrived(number):
        return [moved for _, moved in begun[number]] if planned else []

    for layer in reversed(range(layers)):
        w_qkvo, w_up, w_down = weights[layer]
        state, first, proj, attn, lse, middle, second, active, slope = records[layer]
        last = layer == layers - 1
        if not last:
            above[0] = after(above[0], fold(2 * layer + 3, ready))
        outs = [token_f32, token_bf, ((length, hidden), BF), token_bf, line, ((1, hidden), F32)]
        grad, low, pre, part, grad_shift, grad_up, *more = call(
            functools.partial(hidden_back_kernel, layer, last),
            outs + ([] if last else [line] * 2),
            above + [rows_all, w_up, w_down, slope],
            flops=2 * hidden_flops,
        )
        mine = vector_grads[layer]
        mine[5], mine[6] = grad_shift, grad_up
        if not last:
            vector_grads[layer + 1][0], vector_grads[layer + 1][2] = more
        moved = swap(part)
        ready = begin(2 * layer + 1, [(low, active)], [(second, pre)])
        if not last:
            ready += arrived(2 * layer + 2)
        below, low, grad_qk, grad_v, part, *more = call(
            functools.partial(attention_back_kernel, layer),
            [
                token_f32,
                token_bf,
                ((length, 2 * head_width), BF),
                ((length, head_width), BF),
                token_bf,
                line,
                line,
                line,
                ((1, 3 * head_width), F32),
            ],
            [after(grad, ready), part, moved, middle, rows_all, w_qkvo, proj, lse]
            + [seg_row, seg_column],
            scratch=[
                pltpu.VMEM((head_width, length), BF),
                pltpu.VMEM((3 * head_width, length), BF),
                pltpu.VMEM((2, length, length), BF),
                pltpu.VMEM((2, length, length), BF),
            ],
            flops=proj_flops + out_flops + 5 * head_flops,
        )
        mine[1], mine[3], mine[4], mine[7] = more
        moved = swap(part)
        front, back = [(first, grad_qk)], [(first, grad_v), (low, attn)]
        if not last:
            fold(2 * layer + 2, part)
        if layer > 0:
            ready = begin(2 * layer, front, back)
            below = after(below, ready)
        above = [below, part, moved, state]
    below, part, moved, _ = above
    input_grad, grad_gain, grad_shift = call(
        input_back_kernel, [token_f32, line, line], [below, part, moved, tokens, rows_all]
    )
    vector_grads[0][0], vector_grads[0][2] = grad_gain, grad_shift
    input_grad = input_grad.reshape(count, length, width)

    if planned:
        (columns,) = call(
            functools.partial(pack_grads_kernel, layers, size),
            [((width, LANES), BF)],
            [vector for mine in vector_grads for vector in mine],
            scratch=[
                pltpu.VMEM((LANES, width), F32),
                pltpu.VMEM((LANES, hidden), F32),
                pltpu.VMEM((LANES, 3 * head_width), F32),
            ],
            limit=16,
        )
        halves_of[0] = products("x", *front), products("y", *back, columns)
        ready = [half[0] for half in halves_of[0]]
        begun[0] = scatter_begin(links, *halves_of[0])
        end(3, ready)
        fold(1, ready)
        end(2, ready)
        fold(0, ready)
        end(1, ready)
        end(0, ready)
        outs = [
            (norm_gains.shape, F32),
            (shifts.shape, F32),
            (qkv_weight.shape, F32),
            (bias_turned.shape, F32),
            (out_turned.shape, F32),
            (up_weight.shape, F32),
            (up_bias.shape, F32),
            (down_turned.shape, F32),
        ]
        given = [term for number in range(2 * layers) for term in terms[number]]
        counts = [len(group) for group in terms]
        done = call(functools.partial(finish_kernel, layers, counts), outs, given, limit=24)
        gains, shift, qkv, b_qkv_grad, out, up, b_up_grad, down = done
        b_qkv_grad = jnp.swapaxes(b_qkv_grad, 0, 1)
    else:
        terms = halves_of
        terms[0] = [products(orders[0], *front), products(orders[1], *back)]

        def shared(value, axis):
            return lax.psum_scatter(value, "dp", scatter_dimension=axis, tiled=True)

        summed = [[shared(half[0].astype(F32), 0) for half in pair] for pair in terms]
        cut = [jnp.concatenate(summed[2 * layer], axis=1) for layer in range(layers)]
        qkv = jnp.stack(
            [
                jnp.stack([piece[:, c * head_width : (c + 1) * head_width] for c in range(3)])
                for piece in cut
            ]
        )
        out = jnp.stack([piece[:, 3 * head_width :] for piece in cut])
        down = jnp.stack([summed[2 * layer + 1][0] for layer in range(layers)])
        up = jnp.stack([summed[2 * layer + 1][1] for layer in range(layers)])
        both = jnp.stack([jnp.concatenate(mine[:6], axis=0) for mine in vector_grads])
        both = shared(both, 2)
        gains, shift = both[:, :2], both[:, 2:]
        b_up_grad = shared(jnp.concatenate([mine[6] for mine in vector_grads], axis=0), 1)
        b_qkv_grad = jnp.stack([mine[7].reshape(3, head_width) for mine in vector_grads])
        b_qkv_grad = shared(b_qkv_grad, 2)
    out, down = jnp.swapaxes(out, 1, 2), jnp.swapaxes(down, 1, 2)
    return (result, input_grad, gains, shift, qkv, b_qkv_grad, out, up, b_up_grad, down)


def solution(mesh):
    weights = (
        P(None, None, "dp"),
        P(None, None, "dp"),
        P(None, None, "dp", "tensor"),
        P(None, None, ("tensor", "dp")),
        P(None, "tensor", "dp"),
        P(None, "dp", "tensor"),
        P(None, ("tensor", "dp")),
        P(None, "tensor", "dp"),
    )
    rows = P("dp", None, None)
    return jax.shard_map(
        on_device,
        mesh=mesh,
        in_specs=(rows, P("dp", None), rows) + weights,
        out_specs=(rows, rows) + weights,
        check_vma=False,
    )
```

```python
import functools
import math

import jax
import jax.numpy as jnp
from jax import lax
from jax.experimental import pallas as pl
from jax.experimental.pallas import tpu as pltpu
from jax.sharding import PartitionSpec as P

HD = 64
EPSILON = 1e-05
MASKED = -1e30
BF = jnp.bfloat16
F32 = jnp.float32
SEGMENT_MAX = 96
QUERY_BLOCK = 128
HIDDEN_BLOCK = 256
LANES = 128
WINDOWS = 2, 2, 3

SZ, SY, SX = 4, 2, 2
PARTS = SZ * SY * SX


def contract(left, right, left_dim, right_dim):
    dims = (((left_dim,), (right_dim,)), ((), ()))
    return lax.dot_general(left, right, dims, preferred_element_type=F32)


def dot_nn(left, right):
    return contract(left, right, 1, 0)


def dot_nt(left, right):
    return contract(left, right, 1, 1)


def dot_tn(left, right):
    return contract(left, right, 0, 0)


def normed(state):
    mean = jnp.mean(state, axis=-1, keepdims=True)
    centred = state - mean
    inverse = lax.rsqrt(jnp.mean(centred * centred, axis=-1, keepdims=True) + EPSILON)
    return centred * inverse, inverse


def norm_back(grad, norm, inverse, gain):
    grad_gain = jnp.sum(grad * norm, axis=0, keepdims=True)
    grad_shift = jnp.sum(grad, axis=0, keepdims=True)
    scaled = grad * gain
    back = inverse * (
        scaled
        - jnp.mean(scaled, axis=-1, keepdims=True)
        - norm * jnp.mean(scaled * norm, axis=-1, keepdims=True)
    )
    return back, grad_gain, grad_shift


def query_blocks(length):
    blocks = []
    for start in range(0, length, QUERY_BLOCK):
        low = max(0, start - SEGMENT_MAX + 1) // QUERY_BLOCK * QUERY_BLOCK
        high = min(length, -(-(start + QUERY_BLOCK + SEGMENT_MAX - 1) // QUERY_BLOCK) * QUERY_BLOCK)
        blocks.append((start, low, high))
    return blocks


def call(kernel, outs, args, scratch=(), flops=0, limit=20, space=pltpu.VMEM):
    shapes = [jax.ShapeDtypeStruct(shape, kind) for shape, kind in outs]
    moved = sum(math.prod(a.shape) * a.dtype.itemsize for a in list(args) + shapes)
    vmem = pl.BlockSpec(memory_space=pltpu.VMEM)
    return pl.pallas_call(
        kernel,
        out_shape=shapes,
        in_specs=[pl.BlockSpec(memory_space=space)] * len(args),
        out_specs=[vmem] * len(outs),
        scratch_shapes=list(scratch),
        cost_estimate=pl.CostEstimate(flops=flops, bytes_accessed=moved, transcendentals=0),
        compiler_params=pltpu.CompilerParams(vmem_limit_bytes=limit << 20),
    )(*args)


def flip(value, mask):
    count = lax.axis_size("dp")
    return lax.ppermute(value, "dp", [(i, i ^ mask) for i in range(count)])


class Link:
    def __init__(self, window):
        self.window, self.sent = window, []

    def send(self, value, mask):
        if len(self.sent) >= self.window:
            value, _ = lax.optimization_barrier((value, self.sent[-self.window]))
        self.sent.append(flip(value, mask))
        return self.sent[-1]


def after(value, token):
    return lax.optimization_barrier((value, token))[0]


def swap(part):
    count = lax.axis_size("tensor")
    return lax.ppermute(part, "tensor", [(i, (i + 1) % count) for i in range(count)])


def place():
    me = lax.axis_index("dp")
    return me // (SY * SX), (me // SX) % SY, me % SX


def relative(order, y, x):
    blocks = []
    for number in range(PARTS):
        first, second, line = number // 8, number // 4 % 2, number % 4
        ky, kx = (second, first) if order == "x" else (first, second)
        blocks.append((line * SY + (y ^ ky)) * SX + (x ^ kx))
    return blocks


def join_kernel(split, *refs):
    blocks, front, back = refs[:-2], refs[-2], refs[-1]
    rows = front.shape[0] // SZ
    z = place()[0]
    for distance, ref in enumerate(blocks):
        line = pl.ds(pl.multiple_of((z ^ distance) * rows, 16), rows)
        front[line, :] = ref[:, :split]
        back[line, :] = ref[:, split:]


def cut_kernel(line, *outs):
    start = 0
    for out in outs:
        out[...] = line[:, start : start + out.shape[1]]
        start += out.shape[1]


def place_kernel(*refs):
    parts, outs = refs[:8], refs[8:]
    _, y, x = place()
    rows = outs[0].shape[0] // PARTS
    reach = 0
    for half, order in enumerate("yx"):
        begin, reach = reach, reach + parts[4 * half].shape[1]
        start = 0
        for out in outs:
            end = start + out.shape[1]
            low, high = max(start, begin), min(end, reach)
            if low < high:
                for number, block in enumerate(relative(order, y, x)):
                    ref, line = parts[half * 4 + number // 4], number % 4
                    out[pl.ds(pl.multiple_of(block * rows, 16), rows), low - start : high - start] = ref[
                        line * rows : (line + 1) * rows, low - begin : high - begin
                    ]
            start = end


def lines():
    across = SY * SX
    return [[z * across + column for z in range(SZ)] for column in range(across)]


def pair_kernel(front, front_y, back, back_x, out):
    rows, split = front.shape
    for number, (left, right) in enumerate(((front, back), (front_y, back_x))):
        line = slice(number * rows, (number + 1) * rows)
        out[line, :split] = left[...]
        out[line, split:] = right[...]


def place_pairs_kernel(front, front_x, back, back_y, *outs):
    _, y, x = place()
    rows = outs[0].shape[0] // PARTS
    reach = 0
    for half, refs in enumerate(((front, front_x), (back, back_y))):
        begin, reach = reach, reach + refs[0].shape[1]
        start = 0
        for out in outs:
            end = start + out.shape[1]
            low, high = max(start, begin), min(end, reach)
            if low < high:
                for number in range(PARTS):
                    last, line, first = number // 8, number // 2 % 4, number % 2
                    ky, kx = (first, last) if half == 0 else (last, first)
                    block = (line * SY + (y ^ ky)) * SX + (x ^ kx)
                    at = (line * 2 + first) * rows
                    out[pl.ds(pl.multiple_of(block * rows, 16), rows), low - start : high - start] = refs[last][
                        at : at + rows, low - begin : high - begin
                    ]
            start = end


def over_z(piece):
    return lax.all_gather(piece, "dp", axis=0, tiled=True, axis_index_groups=lines())


def gather(pieces, widths):
    along_x, along_y, along_z = (Link(window) for window in WINDOWS)
    whole, line = [], None
    early = [(front, flip(front, SX), back, flip(back, 1)) for front, back in pieces[2:]]
    for number, piece in enumerate(pieces[:2]):
        rows, columns = piece.shape
        split = columns // 256 * 128
        shapes = [((SZ * rows, split), BF), ((SZ * rows, columns - split), BF)]
        if number == 0:
            arrived = [piece] + [along_z.send(piece, kz * SY * SX) for kz in range(1, SZ)]
            arrived[0] = after(piece, early)
            front, back = call(functools.partial(join_kernel, split), shapes, arrived, limit=8)
            tokens = [front]
        else:
            line = after(over_z(piece), tokens)
            tokens.append(line)
            front, back = call(cut_kernel, shapes, [line], limit=8)
        front_y, back_x = along_y.send(front, SX), along_x.send(back, 1)
        front_x, back_y = along_x.send(front, 1), along_y.send(back, SX)
        front_xy, back_xy = along_x.send(front_y, 1), along_y.send(back_x, SX)
        parts = [front, front_x, front_y, front_xy, back, back_y, back_x, back_xy]
        outs = [((PARTS * rows, width), BF) for width in widths[number]]
        whole.append(call(place_kernel, outs, parts, limit=12))
    for number, given in enumerate(early):
        rows, columns = given[0].shape[0], given[0].shape[1] + given[2].shape[1]
        (pair,) = call(pair_kernel, [((2 * rows, columns), BF)], given, limit=8)
        line = over_z(after(pair, tokens[number]))
        shapes = [((2 * SZ * rows, half.shape[1]), BF) for half in given[::2]]
        front, back = call(cut_kernel, shapes, [line], limit=8)
        front_x, back_y = along_x.send(front, 1), along_y.send(back, SX)
        outs = [((PARTS * rows, width), BF) for width in widths[2 + number]]
        whole.append(call(place_pairs_kernel, outs, [front, front_x, back, back_y], limit=12))
    return whole


def product_kernel(order, shares, *refs):
    count = 1 if order is None else 2
    scratch = refs[-1]
    outs = refs[-1 - count : -1]
    width = scratch.shape[0]
    blocks = None if order is None else relative(order, *place()[1:])
    rows = width // PARTS

    def put(start, size):
        if order is None:
            outs[0][:, start : start + size] = scratch[:, :size]
            return
        for number, block in enumerate(blocks):
            out, line = outs[number // 8 == 0], number % 8
            out[line * rows : (line + 1) * rows, start : start + size] = scratch[
                pl.ds(pl.multiple_of(block * rows, 16), rows), :size
            ]

    start, place_in = 0, 0
    for kind in shares:
        if kind == "ready":
            ready = refs[place_in]
            place_in += 1
            size = ready.shape[1]
            scratch[:, :size] = ready[...]
            put(start, size)
            start += size
            continue
        left, right = refs[place_in], refs[place_in + 1]
        place_in += 2
        turned = left[...].T
        for first in range(0, right.shape[1], 384):
            size = min(384, right.shape[1] - first)
            scratch[:, :size] = dot_nn(turned, right[:, first : first + size]).astype(BF)
            put(start, size)
            start += size


def products(order, *shares):
    args, kinds, columns, flops = [], [], 0, 0
    for share in shares:
        if isinstance(share, tuple):
            kinds.append("product")
            args += share
            columns += share[1].shape[1]
            width = share[0].shape[1]
            flops += 2 * math.prod(share[0].shape) * share[1].shape[1]
        else:
            kinds.append("ready")
            args.append(share)
            columns += share.shape[1]
            width = share.shape[0]
    outs = [((width, columns), BF)] if order is None else [((width // 2, columns), BF)] * 2
    return call(
        functools.partial(product_kernel, order, tuple(kinds)),
        outs,
        args,
        scratch=[pltpu.VMEM((width, 384), BF)],
        flops=flops,
        limit=24,
    )


def fold_kernel(keep, moved, away, stay):
    half = keep.shape[0] // 2
    total = keep[...].astype(F32) + moved[...].astype(F32)
    stay[...] = total[:half].astype(BF)
    away[...] = total[half:].astype(BF)


def line_kernel(keep_a, moved_a, keep_b, moved_b, *outs):
    rows = keep_a.shape[0] // SZ
    split = keep_a.shape[1]
    z = place()[0]
    for distance, out in enumerate(outs):
        line = slice(None)
        if len(outs) > 1:
            line = pl.ds(pl.multiple_of((z ^ distance) * rows, 16), rows)
        total_a = keep_a[line, :].astype(F32) + moved_a[line, :].astype(F32)
        total_b = keep_b[line, :].astype(F32) + moved_b[line, :].astype(F32)
        out[:, :split] = total_a.astype(out.dtype)
        out[:, split:] = total_b.astype(out.dtype)


def scatter_begin(links, half_a, half_b):
    along_x, along_y, _ = links
    moved_a, moved_b = along_x.send(half_a[0], 1), along_y.send(half_b[0], SX)
    return (half_a[1], moved_a), (half_b[1], moved_b)


def scatter_fold(links, *halves):
    along_x, along_y, _ = links
    folded = []
    for stay, moved in halves:
        shape = (stay.shape[0] // 2, stay.shape[1])
        folded.append(call(fold_kernel, [(shape, BF)] * 2, [stay, moved], limit=8))
    (away_a, stay_a), (away_b, stay_b) = folded
    moved_a, moved_b = along_y.send(away_a, SX), along_x.send(away_b, 1)
    return [stay_a, moved_a, stay_b, moved_b], [away_a, away_b]


def scatter_end(links, kind, ends):
    along_z = links[2]
    height, columns = ends[0].shape[0], ends[0].shape[1] + ends[2].shape[1]
    if kind == "line":
        (line,) = call(line_kernel, [((height, columns), BF)], ends, limit=8)
        return [
            lax.psum_scatter(
                line, "dp", scatter_dimension=0, tiled=True, axis_index_groups=lines()
            )
        ]
    shape = (height // SZ, columns)
    own, *line = call(line_kernel, [(shape, F32)] + [(shape, BF)] * (SZ - 1), ends, limit=16)
    return [own] + [along_z.send(block, kz * SY * SX) for kz, block in zip(range(1, SZ), line)]


def lanes_of(layers):
    up = 6 * layers
    return up, up + 2 * layers


def pack_first_kernel(*refs):
    given, piece, held, scratch, sems = refs[:6], refs[6], refs[7:13], refs[13], refs[14]
    sources = list(given[:4]) + [given[4].at[0], given[5].at[0]]
    copies = [
        pltpu.make_async_copy(source, target, sems.at[number])
        for number, (source, target) in enumerate(zip(sources, held))
    ]
    for copy in copies:
        copy.start()
    scratch[...] = jnp.zeros(scratch.shape, F32)
    for copy in copies:
        copy.wait()
    gains, shifts, b_up, b_qkv, qkv, out = held
    _, rows, width = qkv.shape
    layers = gains.shape[0]
    lane_up, lane_qkv = lanes_of(layers)
    for layer in range(layers):
        base = 6 * layer
        scratch[base : base + 2, :rows] = gains[layer]
        scratch[base + 2 : base + 6, :rows] = shifts[layer]
        for c in range(2):
            line = lane_up + 2 * layer + c
            scratch[line : line + 1, :rows] = b_up[layer : layer + 1, c * rows : (c + 1) * rows]
        for c in range(3):
            line = lane_qkv + 3 * layer + c
            scratch[line : line + 1, : b_qkv.shape[2]] = b_qkv[c, layer : layer + 1]
    for c in range(3):
        piece[:, c * width : (c + 1) * width] = qkv[c].astype(BF)
    piece[:, 3 * width : 4 * width] = out[...].astype(BF)
    piece[:, 4 * width :] = scratch[...].T[:rows].astype(BF)


def pack_kernel(qkv, out, up, down, ffn, second, up_half, down_front, down_back):
    width, hidden = qkv.shape[3], up.shape[2]
    ffn[:, :hidden] = up[0].astype(BF)
    ffn[:, hidden:] = down[0].astype(BF)
    for c in range(3):
        second[:, c * width : (c + 1) * width] = qkv[1, c].astype(BF)
    second[:, 3 * width :] = out[1].astype(BF)
    up_half[...] = up[1].astype(BF)
    split = down_front.shape[1]
    down_front[...] = down[1, :, :split].astype(BF)
    down_back[...] = down[1, :, split:].astype(BF)


def unpack_kernel(layers, size, columns, rows_out, up_out, qkv_out, up_scratch, qkv_scratch):
    lane_up, lane_qkv = lanes_of(layers)
    wide = columns[...].astype(F32)
    rows_out[...] = wide.T[: rows_out.shape[0]]
    rows = columns.shape[0] // PARTS
    lane = lax.broadcasted_iota(jnp.int32, (rows, LANES), 1)

    def merged(block, lanes):
        total = jnp.zeros((block.shape[0], LANES), F32)
        for layer, at in enumerate(lanes):
            total = jnp.where(lane[: block.shape[0]] == layer, block[:, at : at + 1], total)
        return total

    width = qkv_out.shape[1] // 3
    for part in range(PARTS):
        block = wide[part * rows : (part + 1) * rows]
        for c in range(2):
            start = (part * 2 + c) * rows
            up_scratch[start : start + rows, :] = merged(
                block, [lane_up + 2 * layer + c for layer in range(layers)]
            )
        for c in range(3):
            start = c * width + part * size
            qkv_scratch[start : start + size, :] = merged(
                block[:size], [lane_qkv + 3 * layer + c for layer in range(layers)]
            )
    up_out[...] = up_scratch[...].T[: up_out.shape[0]]
    qkv_out[...] = qkv_scratch[...].T[: qkv_out.shape[0]]


def pack_grads_kernel(layers, size, *refs):
    out, rows_scratch, up_scratch, qkv_scratch = refs[-4:]
    lane_up, lane_qkv = lanes_of(layers)
    rows_scratch[...] = jnp.zeros(rows_scratch.shape, F32)
    up_scratch[...] = jnp.zeros(up_scratch.shape, F32)
    qkv_scratch[...] = jnp.zeros(qkv_scratch.shape, F32)
    for layer in range(layers):
        given = refs[8 * layer : 8 * layer + 8]
        for number in range(6):
            line = 6 * layer + number
            rows_scratch[line : line + 1, :] = given[number][...]
        up_scratch[layer : layer + 1, :] = given[6][...]
        qkv_scratch[layer : layer + 1, :] = given[7][...]
    columns = rows_scratch[...].T
    up, qkv = up_scratch[...].T, qkv_scratch[...].T
    rows = out.shape[0] // PARTS
    width = qkv.shape[0] // 3
    lane = lax.broadcasted_iota(jnp.int32, (rows, LANES), 1)
    for part in range(PARTS):
        total = columns[part * rows : (part + 1) * rows]
        for layer in range(layers):
            for c in range(2):
                start = (part * 2 + c) * rows
                value = up[start : start + rows, layer : layer + 1]
                total = jnp.where(lane == lane_up + 2 * layer + c, value, total)
            for c in range(3):
                start = c * width + part * size
                value = jnp.concatenate(
                    [
                        qkv[start : start + size, layer : layer + 1],
                        jnp.zeros((rows - size, 1), F32),
                    ],
                    axis=0,
                )
                total = jnp.where(lane == lane_qkv + 3 * layer + c, value, total)
        out[part * rows : (part + 1) * rows, :] = total.astype(BF)


def finish_kernel(layers, counts, *refs):
    outs, groups, start = refs[sum(counts) :], [], 0
    for count in counts:
        groups.append(refs[start : start + count])
        start += count
    gains, shifts, qkv, b_qkv, out, up, b_up, down = outs
    rows, width = qkv.shape[2:]
    hidden = up.shape[2]
    lane_up, lane_qkv = lanes_of(layers)
    for layer in range(layers):
        first, second = groups[2 * layer], groups[2 * layer + 1]

        def total(group, start, size):
            value = group[0][:, start : start + size].astype(F32)
            for term in group[1:]:
                value = value + term[:, start : start + size].astype(F32)
            return value

        for c in range(3):
            qkv[layer, c] = total(first, c * width, width)
        out[layer] = total(first, 3 * width, width)
        down[layer] = total(second, 0, hidden)
        up[layer] = total(second, hidden, hidden)
        if layer == 0:
            small = total(first, 4 * width, LANES)
            small = jnp.concatenate([small, jnp.zeros((LANES - rows, LANES), F32)], axis=0).T
            for k in range(layers):
                gains[k] = small[6 * k : 6 * k + 2, :rows]
                shifts[k] = small[6 * k + 2 : 6 * k + 6, :rows]
                for c in range(2):
                    line = lane_up + 2 * k + c
                    b_up[k : k + 1, c * rows : (c + 1) * rows] = small[line : line + 1, :rows]
                for c in range(3):
                    line = lane_qkv + 3 * k + c
                    b_qkv[c, k : k + 1] = small[line : line + 1, : b_qkv.shape[2]]


def attention_forward_kernel(layer, *refs):
    if layer == 0:
        tokens, *refs = refs
        state = tokens[...].astype(F32)
    else:
        middle, own, moved, *refs = refs
    rows, b_qkv, weight, seg_row, seg_column, x_ref, first_ref, proj_ref, attn_ref, lse_ref, part_ref, turned = refs
    base = 6 * layer
    if layer > 0:
        state = middle[...] + (own[...].astype(F32) + moved[...].astype(F32))
        state = state + rows[base - 1 : base, :]
    x_ref[...] = state
    norm, _ = normed(state)
    first = (norm * rows[base : base + 1, :] + rows[base + 2 : base + 3, :]).astype(BF)
    first_ref[...] = first
    width = weight.shape[1] // 512 * 128
    proj = dot_nn(first, weight[:, : 3 * width]) + b_qkv[layer : layer + 1, :]
    proj_ref[...] = proj.astype(BF).T
    length = state.shape[0]
    lse_ref[...] = jnp.zeros(lse_ref.shape, F32)
    for head in range(width // HD):
        own_rows = slice(head * HD, (head + 1) * HD)
        query = proj_ref[own_rows, :] * BF(HD**-0.5)
        keys = proj_ref[width + head * HD : width + (head + 1) * HD, :]
        values = proj_ref[2 * width + head * HD : 2 * width + (head + 1) * HD, :]
        for start, low, high in query_blocks(length):
            block = slice(start, start + QUERY_BLOCK)
            scores = dot_tn(keys[:, low:high], query[:, block])
            same = seg_column[low:high, :] == seg_row[:, block]
            scores = jnp.where(same, scores, MASKED)
            highest = jnp.max(scores, axis=0, keepdims=True)
            unnormed = jnp.exp(scores - highest)
            summed = jnp.sum(unnormed, axis=0, keepdims=True)
            lse_ref[head : head + 1, block] = highest + jnp.log(summed)
            probs = (unnormed * (1.0 / summed)).astype(BF)
            turned[own_rows, block] = dot_nn(values[:, low:high], probs).astype(BF)
    attn = turned[...].T
    attn_ref[...] = attn
    part_ref[...] = dot_nt(attn, weight[:, 3 * width : 4 * width]).astype(BF)


def up_kernel(layer, state, own, moved, rows, b_up, weight, middle_ref, second_ref, hidden_ref, slope_ref):
    base = 6 * layer
    middle = state[...] + (own[...].astype(F32) + moved[...].astype(F32))
    middle = middle + rows[base + 4 : base + 5, :]
    middle_ref[...] = middle
    norm, _ = normed(middle)
    second = (norm * rows[base + 1 : base + 2, :] + rows[base + 3 : base + 4, :]).astype(BF)
    second_ref[...] = second
    for start in range(0, hidden_ref.shape[1], HIDDEN_BLOCK):
        block = slice(start, start + HIDDEN_BLOCK)
        pre = dot_nn(second, weight[:, block]) + b_up[layer : layer + 1, block]
        below = 0.5 * (1.0 + lax.erf(pre * 0.7071067811865476))
        hidden_ref[:, block] = (pre * below).astype(BF)
        density = jnp.exp(-0.5 * pre * pre) * 0.3989422804014327
        slope_ref[:, block] = below + pre * density


def down_kernel(hidden, weight, part_ref):
    part_ref[...] = dot_nt(hidden[...], weight[...]).astype(BF)


def hidden_back_kernel(layer, last, *refs):
    if last:
        cotangent, *refs = refs
        grad = cotangent[...].astype(F32)
    else:
        above, own, moved, state, *refs = refs
    rows, w_up, w_down, slope, grad_ref, low_ref, pre_ref, part_ref, shift_ref, bias_ref, *more = refs
    if not last:
        gain_ref, norm_shift_ref = more
        arrived = own[...].astype(F32) + moved[...].astype(F32)
        norm, inverse = normed(state[...])
        upper = 6 * (layer + 1)
        back, gain_ref[...], norm_shift_ref[...] = norm_back(
            arrived, norm, inverse, rows[upper : upper + 1, :]
        )
        grad = above[...] + back
    grad_ref[...] = grad
    low = grad.astype(BF)
    low_ref[...] = low
    shift_ref[...] = jnp.sum(grad, axis=0, keepdims=True)
    for start in range(0, w_up.shape[1], HIDDEN_BLOCK):
        block = slice(start, start + HIDDEN_BLOCK)
        back = dot_nn(low, w_down[:, block])
        pre = (back * slope[:, block]).astype(BF)
        pre_ref[:, block] = pre
        bias_ref[:, block] = jnp.sum(pre.astype(F32), axis=0, keepdims=True)
    part_ref[...] = dot_nt(pre_ref[...], w_up[...]).astype(BF)


def attention_back_kernel(layer, *refs):
    (grad, own, moved, middle, rows, weight, proj, lse, seg_row, seg_column) = refs[:10]
    (below_ref, low_ref, grad_qk_ref, grad_v_ref, part_ref, gain_ref, norm_shift_ref, shift_ref, bias_ref) = refs[10:19]
    turned, turned_proj, probs_ref, scores_ref = refs[19:]
    base = 6 * layer
    arrived = own[...].astype(F32) + moved[...].astype(F32)
    norm, inverse = normed(middle[...])
    back, gain_ref[...], norm_shift_ref[...] = norm_back(
        arrived, norm, inverse, rows[base + 1 : base + 2, :]
    )
    below = grad[...] + back
    below_ref[...] = below
    shift_ref[...] = jnp.sum(below, axis=0, keepdims=True)
    low = below.astype(BF)
    low_ref[...] = low
    width = weight.shape[1] // 512 * 128
    turned[...] = dot_nn(low, weight[:, 3 * width : 4 * width]).astype(BF).T
    length = below.shape[0]
    probs_ref[...] = jnp.zeros(probs_ref.shape, BF)
    scores_ref[...] = jnp.zeros(scores_ref.shape, BF)
    for head in range(width // HD):
        slot = head % 2
        own_rows = slice(head * HD, (head + 1) * HD)
        key_rows = slice(width + head * HD, width + (head + 1) * HD)
        value_rows = slice(2 * width + head * HD, 2 * width + (head + 1) * HD)
        query = proj[own_rows, :] * BF(HD**-0.5)
        keys, values, mixed = proj[key_rows, :], proj[value_rows, :], turned[own_rows, :]
        for start, low_key, high in query_blocks(length):
            block = slice(start, start + QUERY_BLOCK)
            scores = dot_tn(keys[:, low_key:high], query[:, block])
            same = seg_column[low_key:high, :] == seg_row[:, block]
            scores = jnp.where(same, scores, MASKED)
            probs = jnp.exp(scores - lse[head : head + 1, block])
            probs_ref[slot, low_key:high, block] = probs.astype(BF)
            grad_probs = dot_tn(values[:, low_key:high], mixed[:, block])
            centre = jnp.sum(probs * grad_probs, axis=0, keepdims=True)
            scores_ref[slot, low_key:high, block] = (probs * (grad_probs - centre)).astype(BF)
        grad_scores = scores_ref[slot]
        scaled_keys = keys * BF(HD**-0.5)
        turned_proj[own_rows, :] = dot_nn(scaled_keys, grad_scores).astype(BF)
        turned_proj[key_rows, :] = dot_nt(query, grad_scores).astype(BF)
        turned_proj[value_rows, :] = dot_nt(mixed, probs_ref[slot]).astype(BF)
    grad_proj = turned_proj[...].T
    grad_qk_ref[...] = grad_proj[:, : 2 * width]
    grad_v_ref[...] = grad_proj[:, 2 * width :]
    bias_ref[...] = jnp.sum(grad_proj.astype(F32), axis=0, keepdims=True)
    part_ref[...] = dot_nt(grad_proj, weight[:, : 3 * width]).astype(BF)


def input_back_kernel(above, own, moved, tokens, rows, out_ref, gain_ref, norm_shift_ref):
    arrived = own[...].astype(F32) + moved[...].astype(F32)
    norm, inverse = normed(tokens[...].astype(F32))
    back, gain_ref[...], norm_shift_ref[...] = norm_back(arrived, norm, inverse, rows[:1, :])
    out_ref[...] = above[...] + back


def packed_plainly(norm_gains, shifts, qkv_weight, qkv_bias, out_turned, up_weight, up_bias, down_turned):
    layers = norm_gains.shape[0]
    pieces = []
    for layer in range(layers):
        first = [qkv_weight[layer, c] for c in range(3)] + [out_turned[layer]]
        given = [jnp.concatenate(first, axis=1), up_weight[layer], down_turned[layer]]
        pieces.append([lax.all_gather(w.astype(BF), "dp", axis=0, tiled=True) for w in given])

    def whole(vector, axis):
        return lax.all_gather(vector.astype(BF), "dp", axis=axis, tiled=True).astype(F32)

    both = jnp.concatenate([norm_gains, shifts], axis=1)
    rows = whole(both, 2).reshape(6 * layers, -1)
    rows = jnp.pad(rows, ((0, -rows.shape[0] % 16), (0, 0)))
    up = jnp.pad(whole(up_bias, 1), ((0, 8 - layers), (0, 0)))
    qkv = jnp.pad(whole(qkv_bias, 2).reshape(layers, -1), ((0, 8 - layers), (0, 0)))
    return pieces, (rows, up, qkv)


def on_device(
    tokens,
    segments,
    cotangent,
    norm_gains,
    shifts,
    qkv_weight,
    qkv_bias,
    out_weight,
    up_weight,
    up_bias,
    down_weight,
):
    count, length, width = tokens.shape
    layers, _, rows, head_width = qkv_weight.shape
    hidden = up_weight.shape[2]
    planned = lax.axis_size("dp") == PARTS and rows % 48 == 0 and layers == 2
    tokens = tokens.reshape(length, width)
    cotangent = cotangent.reshape(length, width)
    seg_row, seg_column = segments.reshape(1, length), segments.reshape(length, 1)
    out_turned, down_turned = jnp.swapaxes(out_weight, 1, 2), jnp.swapaxes(down_weight, 1, 2)

    if planned:
        size = qkv_bias.shape[2]
        bias_turned = jnp.swapaxes(qkv_bias, 0, 1)
        wide = 4 * head_width
        given = [norm_gains, shifts, up_bias, bias_turned, qkv_weight, out_turned]
        held = [a.shape for a in given[:4]] + [a.shape[1:] for a in given[4:]]
        (first_piece,) = call(
            pack_first_kernel,
            [((rows, wide + LANES), BF)],
            given,
            scratch=[pltpu.VMEM(shape, F32) for shape in held]
            + [pltpu.VMEM((LANES, LANES), F32), pltpu.SemaphoreType.DMA((len(held),))],
            limit=8,
            space=pl.ANY,
        )
        half = hidden // 2
        shapes = [((rows, size), BF) for size in (2 * hidden, wide, hidden, half, hidden - half)]
        ffn, *others = call(pack_kernel, shapes, [qkv_weight, out_turned, up_weight, down_turned])
        arrays = gather(
            [first_piece, ffn, others[:2], others[2:]],
            [[wide, LANES], [hidden, hidden], [wide, hidden], [hidden]],
        )
        arrays = [array for bundle in arrays for array in bundle]
        columns = arrays.pop(1)
        weights = [arrays[:3], arrays[3:]]
        vectors = call(
            functools.partial(unpack_kernel, layers, size),
            [((16, width), F32), ((8, hidden), F32), ((8, 3 * head_width), F32)],
            [columns],
            scratch=[pltpu.VMEM((hidden, LANES), F32), pltpu.VMEM((3 * head_width, LANES), F32)],
            limit=8,
        )
        links = [Link(window) for window in WINDOWS]
    else:
        weights, vectors = packed_plainly(
            norm_gains, shifts, qkv_weight, qkv_bias, out_turned, up_weight, up_bias, down_turned
        )
    rows_all, b_up, b_qkv = vectors

    token_f32, token_bf = ((length, width), F32), ((length, width), BF)
    proj_flops = 2 * length * width * 3 * head_width
    out_flops = 2 * length * width * head_width
    hidden_flops = 2 * length * width * hidden
    head_flops = 2 * length * length * head_width

    records, before = [], [tokens]
    for layer in range(layers):
        w_qkvo, w_up, w_down = weights[layer]
        state, first, proj, attn, lse, part = call(
            functools.partial(attention_forward_kernel, layer),
            [
                token_f32,
                token_bf,
                ((3 * head_width, length), BF),
                ((length, head_width), BF),
                ((8, length), F32),
                token_bf,
            ],
            before + [rows_all, b_qkv, w_qkvo, seg_row, seg_column],
            scratch=[pltpu.VMEM((head_width, length), BF)],
            flops=proj_flops + out_flops + 2 * head_flops,
        )
        middle, second, active, slope = call(
            functools.partial(up_kernel, layer),
            [token_f32, token_bf, ((length, hidden), BF), ((length, hidden), F32)],
            [state, part, swap(part), rows_all, b_up, w_up],
            flops=2 * hidden_flops,
        )
        (part,) = call(down_kernel, [token_bf], [active, w_down], flops=hidden_flops)
        before = [middle, part, swap(part)]
        records.append((state, first, proj, attn, lse, middle, second, active, slope))
    middle, part, moved = before
    result = middle + (part.astype(F32) + moved.astype(F32)) + rows_all[6 * layers - 1]
    result = result.astype(BF).reshape(count, length, width)

    vector_grads = [[None] * 8 for _ in range(layers)]
    orders = ("x", "y") if planned else (None, None)
    line = ((1, width), F32)
    above, terms = [cotangent], [None] * (2 * layers)
    halves_of, begun, folded = [None] * (2 * layers), [None] * (2 * layers), [None] * (2 * layers)

    def begin(number, front, back):
        halves_of[number] = [products(orders[0], *front), products(orders[1], *back)]
        if planned:
            begun[number] = scatter_begin(links, *halves_of[number])
        return [half[0] for half in halves_of[number]]

    def fold(number, token):
        if not planned:
            return []
        halves = [(after(stay, token), moved) for stay, moved in begun[number]]
        folded[number], sent = scatter_fold(links, *halves)
        return sent

    def end(number, token):
        kind, (stay, *others) = "line" if number else "steps", folded[number]
        terms[number] = scatter_end(links, kind, [after(stay, token)] + others)

    def arrived(number):
        return [moved for _, moved in begun[number]] if planned else []

    for layer in reversed(range(layers)):
        w_qkvo, w_up, w_down = weights[layer]
        state, first, proj, attn, lse, middle, second, active, slope = records[layer]
        last = layer == layers - 1
        if not last:
            above[0] = after(above[0], fold(2 * layer + 3, ready))
        outs = [token_f32, token_bf, ((length, hidden), BF), token_bf, line, ((1, hidden), F32)]
        grad, low, pre, part, grad_shift, grad_up, *more = call(
            functools.partial(hidden_back_kernel, layer, last),
            outs + ([] if last else [line] * 2),
            above + [rows_all, w_up, w_down, slope],
            flops=2 * hidden_flops,
        )
        mine = vector_grads[layer]
        mine[5], mine[6] = grad_shift, grad_up
        if not last:
            vector_grads[layer + 1][0], vector_grads[layer + 1][2] = more
        moved = swap(part)
        ready = begin(2 * layer + 1, [(low, active)], [(second, pre)])
        if not last:
            ready += arrived(2 * layer + 2)
        below, low, grad_qk, grad_v, part, *more = call(
            functools.partial(attention_back_kernel, layer),
            [
                token_f32,
                token_bf,
                ((length, 2 * head_width), BF),
                ((length, head_width), BF),
                token_bf,
                line,
                line,
                line,
                ((1, 3 * head_width), F32),
            ],
            [after(grad, ready), part, moved, middle, rows_all, w_qkvo, proj, lse]
            + [seg_row, seg_column],
            scratch=[
                pltpu.VMEM((head_width, length), BF),
                pltpu.VMEM((3 * head_width, length), BF),
                pltpu.VMEM((2, length, length), BF),
                pltpu.VMEM((2, length, length), BF),
            ],
            flops=proj_flops + out_flops + 5 * head_flops,
        )
        mine[1], mine[3], mine[4], mine[7] = more
        moved = swap(part)
        front, back = [(first, grad_qk)], [(first, grad_v), (low, attn)]
        if not last:
            fold(2 * layer + 2, part)
        if layer > 0:
            ready = begin(2 * layer, front, back)
            below = after(below, ready)
        above = [below, part, moved, state]
    below, part, moved, _ = above
    input_grad, grad_gain, grad_shift = call(
        input_back_kernel, [token_f32, line, line], [below, part, moved, tokens, rows_all]
    )
    vector_grads[0][0], vector_grads[0][2] = grad_gain, grad_shift
    input_grad = input_grad.reshape(count, length, width)

    if planned:
        (columns,) = call(
            functools.partial(pack_grads_kernel, layers, size),
            [((width, LANES), BF)],
            [vector for mine in vector_grads for vector in mine],
            scratch=[
                pltpu.VMEM((LANES, width), F32),
                pltpu.VMEM((LANES, hidden), F32),
                pltpu.VMEM((LANES, 3 * head_width), F32),
            ],
            limit=16,
        )
        halves_of[0] = products("x", *front), products("y", *back, columns)
        ready = [half[0] for half in halves_of[0]]
        begun[0] = scatter_begin(links, *halves_of[0])
        end(3, vector_grads[0][1])
        fold(1, ready)
        end(2, ready)
        fold(0, ready)
        end(1, ready)
        end(0, ready)
        outs = [
            (norm_gains.shape, F32),
            (shifts.shape, F32),
            (qkv_weight.shape, F32),
            (bias_turned.shape, F32),
            (out_turned.shape, F32),
            (up_weight.shape, F32),
            (up_bias.shape, F32),
            (down_turned.shape, F32),
        ]
        given = [term for number in range(2 * layers) for term in terms[number]]
        counts = [len(group) for group in terms]
        done = call(functools.partial(finish_kernel, layers, counts), outs, given, limit=24)
        gains, shift, qkv, b_qkv_grad, out, up, b_up_grad, down = done
        b_qkv_grad = jnp.swapaxes(b_qkv_grad, 0, 1)
    else:
        terms = halves_of
        terms[0] = [products(orders[0], *front), products(orders[1], *back)]

        def shared(value, axis):
            return lax.psum_scatter(value, "dp", scatter_dimension=axis, tiled=True)

        summed = [[shared(half[0].astype(F32), 0) for half in pair] for pair in terms]
        cut = [jnp.concatenate(summed[2 * layer], axis=1) for layer in range(layers)]
        qkv = jnp.stack(
            [
                jnp.stack([piece[:, c * head_width : (c + 1) * head_width] for c in range(3)])
                for piece in cut
            ]
        )
        out = jnp.stack([piece[:, 3 * head_width :] for piece in cut])
        down = jnp.stack([summed[2 * layer + 1][0] for layer in range(layers)])
        up = jnp.stack([summed[2 * layer + 1][1] for layer in range(layers)])
        both = jnp.stack([jnp.concatenate(mine[:6], axis=0) for mine in vector_grads])
        both = shared(both, 2)
        gains, shift = both[:, :2], both[:, 2:]
        b_up_grad = shared(jnp.concatenate([mine[6] for mine in vector_grads], axis=0), 1)
        b_qkv_grad = jnp.stack([mine[7].reshape(3, head_width) for mine in vector_grads])
        b_qkv_grad = shared(b_qkv_grad, 2)
    out, down = jnp.swapaxes(out, 1, 2), jnp.swapaxes(down, 1, 2)
    return (result, input_grad, gains, shift, qkv, b_qkv_grad, out, up, b_up_grad, down)


def solution(mesh):
    weights = (
        P(None, None, "dp"),
        P(None, None, "dp"),
        P(None, None, "dp", "tensor"),
        P(None, None, ("tensor", "dp")),
        P(None, "tensor", "dp"),
        P(None, "dp", "tensor"),
        P(None, ("tensor", "dp")),
        P(None, "tensor", "dp"),
    )
    rows = P("dp", None, None)
    return jax.shard_map(
        on_device,
        mesh=mesh,
        in_specs=(rows, P("dp", None), rows) + weights,
        out_specs=(rows, rows) + weights,
        check_vma=False,
    )
```

```python
import functools
import math

import jax
import jax.numpy as jnp
from jax import lax
from jax.experimental import pallas as pl
from jax.experimental.pallas import tpu as pltpu
from jax.sharding import PartitionSpec as P

HD = 64
EPSILON = 1e-05
MASKED = -1e30
BF = jnp.bfloat16
F32 = jnp.float32
SEGMENT_MAX = 96
QUERY_BLOCK = 128
HIDDEN_BLOCK = 256
LANES = 128
WINDOWS = 2, 2, 3

SZ, SY, SX = 4, 2, 2
PARTS = SZ * SY * SX


def contract(left, right, left_dim, right_dim):
    dims = (((left_dim,), (right_dim,)), ((), ()))
    return lax.dot_general(left, right, dims, preferred_element_type=F32)


def dot_nn(left, right):
    return contract(left, right, 1, 0)


def dot_nt(left, right):
    return contract(left, right, 1, 1)


def dot_tn(left, right):
    return contract(left, right, 0, 0)


def normed(state):
    mean = jnp.mean(state, axis=-1, keepdims=True)
    centred = state - mean
    inverse = lax.rsqrt(jnp.mean(centred * centred, axis=-1, keepdims=True) + EPSILON)
    return centred * inverse, inverse


def norm_back(grad, norm, inverse, gain):
    grad_gain = jnp.sum(grad * norm, axis=0, keepdims=True)
    grad_shift = jnp.sum(grad, axis=0, keepdims=True)
    scaled = grad * gain
    back = inverse * (
        scaled
        - jnp.mean(scaled, axis=-1, keepdims=True)
        - norm * jnp.mean(scaled * norm, axis=-1, keepdims=True)
    )
    return back, grad_gain, grad_shift


def query_blocks(length):
    blocks = []
    for start in range(0, length, QUERY_BLOCK):
        low = max(0, start - SEGMENT_MAX + 1) // QUERY_BLOCK * QUERY_BLOCK
        high = min(length, -(-(start + QUERY_BLOCK + SEGMENT_MAX - 1) // QUERY_BLOCK) * QUERY_BLOCK)
        blocks.append((start, low, high))
    return blocks


def call(kernel, outs, args, scratch=(), flops=0, limit=20, space=pltpu.VMEM):
    shapes = [jax.ShapeDtypeStruct(shape, kind) for shape, kind in outs]
    moved = sum(math.prod(a.shape) * a.dtype.itemsize for a in list(args) + shapes)
    vmem = pl.BlockSpec(memory_space=pltpu.VMEM)
    return pl.pallas_call(
        kernel,
        out_shape=shapes,
        in_specs=[pl.BlockSpec(memory_space=space)] * len(args),
        out_specs=[vmem] * len(outs),
        scratch_shapes=list(scratch),
        cost_estimate=pl.CostEstimate(flops=flops, bytes_accessed=moved, transcendentals=0),
        compiler_params=pltpu.CompilerParams(vmem_limit_bytes=limit << 20),
    )(*args)


def flip(value, mask):
    count = lax.axis_size("dp")
    return lax.ppermute(value, "dp", [(i, i ^ mask) for i in range(count)])


class Link:
    def __init__(self, window):
        self.window, self.sent = window, []

    def send(self, value, mask):
        if len(self.sent) >= self.window:
            value, _ = lax.optimization_barrier((value, self.sent[-self.window]))
        self.sent.append(flip(value, mask))
        return self.sent[-1]


def after(value, token):
    return lax.optimization_barrier((value, token))[0]


def swap(part):
    count = lax.axis_size("tensor")
    return lax.ppermute(part, "tensor", [(i, (i + 1) % count) for i in range(count)])


def place():
    me = lax.axis_index("dp")
    return me // (SY * SX), (me // SX) % SY, me % SX


def relative(order, y, x):
    blocks = []
    for number in range(PARTS):
        first, second, line = number // 8, number // 4 % 2, number % 4
        ky, kx = (second, first) if order == "x" else (first, second)
        blocks.append((line * SY + (y ^ ky)) * SX + (x ^ kx))
    return blocks


def join_kernel(split, *refs):
    blocks, front, back = refs[:-2], refs[-2], refs[-1]
    rows = front.shape[0] // SZ
    z = place()[0]
    for distance, ref in enumerate(blocks):
        line = pl.ds(pl.multiple_of((z ^ distance) * rows, 16), rows)
        front[line, :] = ref[:, :split]
        back[line, :] = ref[:, split:]


def cut_kernel(line, *outs):
    start = 0
    for out in outs:
        out[...] = line[:, start : start + out.shape[1]]
        start += out.shape[1]


def place_kernel(*refs):
    parts, outs = refs[:8], refs[8:]
    _, y, x = place()
    rows = outs[0].shape[0] // PARTS
    reach = 0
    for half, order in enumerate("yx"):
        begin, reach = reach, reach + parts[4 * half].shape[1]
        start = 0
        for out in outs:
            end = start + out.shape[1]
            low, high = max(start, begin), min(end, reach)
            if low < high:
                for number, block in enumerate(relative(order, y, x)):
                    ref, line = parts[half * 4 + number // 4], number % 4
                    out[pl.ds(pl.multiple_of(block * rows, 16), rows), low - start : high - start] = ref[
                        line * rows : (line + 1) * rows, low - begin : high - begin
                    ]
            start = end


def lines():
    across = SY * SX
    return [[z * across + column for z in range(SZ)] for column in range(across)]


def pair_kernel(front, front_y, back, back_x, out):
    rows, split = front.shape
    for number, (left, right) in enumerate(((front, back), (front_y, back_x))):
        line = slice(number * rows, (number + 1) * rows)
        out[line, :split] = left[...]
        out[line, split:] = right[...]


def place_pairs_kernel(front, front_x, back, back_y, *outs):
    _, y, x = place()
    rows = outs[0].shape[0] // PARTS
    reach = 0
    for half, refs in enumerate(((front, front_x), (back, back_y))):
        begin, reach = reach, reach + refs[0].shape[1]
        start = 0
        for out in outs:
            end = start + out.shape[1]
            low, high = max(start, begin), min(end, reach)
            if low < high:
                for number in range(PARTS):
                    last, line, first = number // 8, number // 2 % 4, number % 2
                    ky, kx = (first, last) if half == 0 else (last, first)
                    block = (line * SY + (y ^ ky)) * SX + (x ^ kx)
                    at = (line * 2 + first) * rows
                    out[pl.ds(pl.multiple_of(block * rows, 16), rows), low - start : high - start] = refs[last][
                        at : at + rows, low - begin : high - begin
                    ]
            start = end


def over_z(piece):
    return lax.all_gather(piece, "dp", axis=0, tiled=True, axis_index_groups=lines())


def gather(pieces, widths):
    along_x, along_y, along_z = (Link(window) for window in WINDOWS)
    whole, line = [], None
    early = [(front, flip(front, SX), back, flip(back, 1)) for front, back in pieces[2:]]
    for number, piece in enumerate(pieces[:2]):
        rows, columns = piece.shape
        split = columns // 256 * 128
        shapes = [((SZ * rows, split), BF), ((SZ * rows, columns - split), BF)]
        if number == 0:
            arrived = [piece] + [along_z.send(piece, kz * SY * SX) for kz in range(1, SZ)]
            arrived[0] = after(piece, early)
            front, back = call(functools.partial(join_kernel, split), shapes, arrived, limit=8)
            tokens = [front]
        else:
            line = after(over_z(piece), tokens)
            tokens.append(line)
            front, back = call(cut_kernel, shapes, [line], limit=8)
        front_y, back_x = along_y.send(front, SX), along_x.send(back, 1)
        front_x, back_y = along_x.send(front, 1), along_y.send(back, SX)
        front_xy, back_xy = along_x.send(front_y, 1), along_y.send(back_x, SX)
        parts = [front, front_x, front_y, front_xy, back, back_y, back_x, back_xy]
        outs = [((PARTS * rows, width), BF) for width in widths[number]]
        whole.append(call(place_kernel, outs, parts, limit=12))
    for number, given in enumerate(early):
        rows, columns = given[0].shape[0], given[0].shape[1] + given[2].shape[1]
        (pair,) = call(pair_kernel, [((2 * rows, columns), BF)], given, limit=8)
        line = over_z(after(pair, tokens[number]))
        shapes = [((2 * SZ * rows, half.shape[1]), BF) for half in given[::2]]
        front, back = call(cut_kernel, shapes, [line], limit=8)
        front_x, back_y = along_x.send(front, 1), along_y.send(back, SX)
        outs = [((PARTS * rows, width), BF) for width in widths[2 + number]]
        whole.append(call(place_pairs_kernel, outs, [front, front_x, back, back_y], limit=12))
    return whole


def product_kernel(order, shares, *refs):
    count = 1 if order is None else 2
    scratch = refs[-1]
    outs = refs[-1 - count : -1]
    width = scratch.shape[0]
    blocks = None if order is None else relative(order, *place()[1:])
    rows = width // PARTS

    def put(start, size):
        if order is None:
            outs[0][:, start : start + size] = scratch[:, :size]
            return
        for number, block in enumerate(blocks):
            out, line = outs[number // 8 == 0], number % 8
            out[line * rows : (line + 1) * rows, start : start + size] = scratch[
                pl.ds(pl.multiple_of(block * rows, 16), rows), :size
            ]

    start, place_in = 0, 0
    for kind in shares:
        if kind == "ready":
            ready = refs[place_in]
            place_in += 1
            size = ready.shape[1]
            scratch[:, :size] = ready[...]
            put(start, size)
            start += size
            continue
        left, right = refs[place_in], refs[place_in + 1]
        place_in += 2
        turned = left[...].T
        for first in range(0, right.shape[1], 384):
            size = min(384, right.shape[1] - first)
            scratch[:, :size] = dot_nn(turned, right[:, first : first + size]).astype(BF)
            put(start, size)
            start += size


def products(order, *shares):
    args, kinds, columns, flops = [], [], 0, 0
    for share in shares:
        if isinstance(share, tuple):
            kinds.append("product")
            args += share
            columns += share[1].shape[1]
            width = share[0].shape[1]
            flops += 2 * math.prod(share[0].shape) * share[1].shape[1]
        else:
            kinds.append("ready")
            args.append(share)
            columns += share.shape[1]
            width = share.shape[0]
    outs = [((width, columns), BF)] if order is None else [((width // 2, columns), BF)] * 2
    return call(
        functools.partial(product_kernel, order, tuple(kinds)),
        outs,
        args,
        scratch=[pltpu.VMEM((width, 384), BF)],
        flops=flops,
        limit=24,
    )


def fold_kernel(keep, moved, away, stay):
    half = keep.shape[0] // 2
    total = keep[...].astype(F32) + moved[...].astype(F32)
    stay[...] = total[:half].astype(BF)
    away[...] = total[half:].astype(BF)


def line_kernel(groups, *refs):
    ends, outs = refs[: 4 * groups], refs[4 * groups :]
    rows = ends[0].shape[0] // SZ
    z = place()[0]
    for distance, out in enumerate(outs):
        line = slice(None)
        if len(outs) > 1:
            line = pl.ds(pl.multiple_of((z ^ distance) * rows, 16), rows)
        start = 0
        for keep, moved in zip(ends[::2], ends[1::2]):
            size = keep.shape[1]
            total = keep[line, :].astype(F32) + moved[line, :].astype(F32)
            out[:, start : start + size] = total.astype(out.dtype)
            start += size


def scatter_begin(links, half_a, half_b):
    along_x, along_y, _ = links
    moved_a, moved_b = along_x.send(half_a[0], 1), along_y.send(half_b[0], SX)
    return (half_a[1], moved_a), (half_b[1], moved_b)


def scatter_fold(links, *halves):
    along_x, along_y, _ = links
    folded = []
    for stay, moved in halves:
        shape = (stay.shape[0] // 2, stay.shape[1])
        folded.append(call(fold_kernel, [(shape, BF)] * 2, [stay, moved], limit=8))
    (away_a, stay_a), (away_b, stay_b) = folded
    moved_a, moved_b = along_y.send(away_a, SX), along_x.send(away_b, 1)
    return [stay_a, moved_a, stay_b, moved_b], [away_a, away_b]


def scatter_line(ends):
    height, columns = ends[0].shape[0], sum(end.shape[1] for end in ends[::2])
    kernel = functools.partial(line_kernel, len(ends) // 4)
    (line,) = call(kernel, [((height, columns), BF)], ends, limit=8)
    return lax.psum_scatter(
        line, "dp", scatter_dimension=0, tiled=True, axis_index_groups=lines()
    )


def scatter_steps(along_z, ends):
    rows, columns = ends[0].shape[0] // SZ, sum(end.shape[1] for end in ends[::2])
    outs = [((rows, columns), F32)] + [((rows, columns), BF)] * (SZ - 1)
    own, *line = call(functools.partial(line_kernel, len(ends) // 4), outs, ends, limit=8)
    return [own] + [along_z.send(block, kz * SY * SX) for kz, block in zip(range(1, SZ), line)]


def lanes_of(layers):
    up = 6 * layers
    return up, up + 2 * layers


def pack_first_kernel(*refs):
    given, piece, held, scratch, sems = refs[:6], refs[6], refs[7:13], refs[13], refs[14]
    sources = list(given[:4]) + [given[4].at[0], given[5].at[0]]
    copies = [
        pltpu.make_async_copy(source, target, sems.at[number])
        for number, (source, target) in enumerate(zip(sources, held))
    ]
    for copy in copies:
        copy.start()
    scratch[...] = jnp.zeros(scratch.shape, F32)
    for copy in copies:
        copy.wait()
    gains, shifts, b_up, b_qkv, qkv, out = held
    _, rows, width = qkv.shape
    layers = gains.shape[0]
    lane_up, lane_qkv = lanes_of(layers)
    for layer in range(layers):
        base = 6 * layer
        scratch[base : base + 2, :rows] = gains[layer]
        scratch[base + 2 : base + 6, :rows] = shifts[layer]
        for c in range(2):
            line = lane_up + 2 * layer + c
            scratch[line : line + 1, :rows] = b_up[layer : layer + 1, c * rows : (c + 1) * rows]
        for c in range(3):
            line = lane_qkv + 3 * layer + c
            scratch[line : line + 1, : b_qkv.shape[2]] = b_qkv[c, layer : layer + 1]
    for c in range(3):
        piece[:, c * width : (c + 1) * width] = qkv[c].astype(BF)
    piece[:, 3 * width : 4 * width] = out[...].astype(BF)
    piece[:, 4 * width :] = scratch[...].T[:rows].astype(BF)


def pack_kernel(qkv, out, up, down, ffn, second, up_half, down_front, down_back):
    width, hidden = qkv.shape[3], up.shape[2]
    ffn[:, :hidden] = up[0].astype(BF)
    ffn[:, hidden:] = down[0].astype(BF)
    for c in range(3):
        second[:, c * width : (c + 1) * width] = qkv[1, c].astype(BF)
    second[:, 3 * width :] = out[1].astype(BF)
    up_half[...] = up[1].astype(BF)
    split = down_front.shape[1]
    down_front[...] = down[1, :, :split].astype(BF)
    down_back[...] = down[1, :, split:].astype(BF)


def unpack_kernel(layers, size, columns, rows_out, up_out, qkv_out, up_scratch, qkv_scratch):
    lane_up, lane_qkv = lanes_of(layers)
    wide = columns[...].astype(F32)
    rows_out[...] = wide.T[: rows_out.shape[0]]
    rows = columns.shape[0] // PARTS
    lane = lax.broadcasted_iota(jnp.int32, (rows, LANES), 1)

    def merged(block, lanes):
        total = jnp.zeros((block.shape[0], LANES), F32)
        for layer, at in enumerate(lanes):
            total = jnp.where(lane[: block.shape[0]] == layer, block[:, at : at + 1], total)
        return total

    width = qkv_out.shape[1] // 3
    for part in range(PARTS):
        block = wide[part * rows : (part + 1) * rows]
        for c in range(2):
            start = (part * 2 + c) * rows
            up_scratch[start : start + rows, :] = merged(
                block, [lane_up + 2 * layer + c for layer in range(layers)]
            )
        for c in range(3):
            start = c * width + part * size
            qkv_scratch[start : start + size, :] = merged(
                block[:size], [lane_qkv + 3 * layer + c for layer in range(layers)]
            )
    up_out[...] = up_scratch[...].T[: up_out.shape[0]]
    qkv_out[...] = qkv_scratch[...].T[: qkv_out.shape[0]]


def pack_grads_kernel(layers, size, *refs):
    out, rows_scratch, up_scratch, qkv_scratch = refs[-4:]
    lane_up, lane_qkv = lanes_of(layers)
    rows_scratch[...] = jnp.zeros(rows_scratch.shape, F32)
    up_scratch[...] = jnp.zeros(up_scratch.shape, F32)
    qkv_scratch[...] = jnp.zeros(qkv_scratch.shape, F32)
    for layer in range(layers):
        given = refs[8 * layer : 8 * layer + 8]
        for number in range(6):
            line = 6 * layer + number
            rows_scratch[line : line + 1, :] = given[number][...]
        up_scratch[layer : layer + 1, :] = given[6][...]
        qkv_scratch[layer : layer + 1, :] = given[7][...]
    columns = rows_scratch[...].T
    up, qkv = up_scratch[...].T, qkv_scratch[...].T
    rows = out.shape[0] // PARTS
    width = qkv.shape[0] // 3
    lane = lax.broadcasted_iota(jnp.int32, (rows, LANES), 1)
    for part in range(PARTS):
        total = columns[part * rows : (part + 1) * rows]
        for layer in range(layers):
            for c in range(2):
                start = (part * 2 + c) * rows
                value = up[start : start + rows, layer : layer + 1]
                total = jnp.where(lane == lane_up + 2 * layer + c, value, total)
            for c in range(3):
                start = c * width + part * size
                value = jnp.concatenate(
                    [
                        qkv[start : start + size, layer : layer + 1],
                        jnp.zeros((rows - size, 1), F32),
                    ],
                    axis=0,
                )
                total = jnp.where(lane == lane_qkv + 3 * layer + c, value, total)
        out[part * rows : (part + 1) * rows, :] = total.astype(BF)


def finish_kernel(layers, counts, *refs):
    outs, groups, start = refs[sum(counts) :], [], 0
    for count in counts:
        groups.append(refs[start : start + count])
        start += count
    gains, shifts, qkv, b_qkv, out, up, b_up, down = outs
    rows, width = qkv.shape[2:]
    hidden = up.shape[2]
    lane_up, lane_qkv = lanes_of(layers)
    for layer in range(layers):
        first, second = groups[2 * layer], groups[2 * layer + 1]

        def total(group, start, size):
            value = group[0][:, start : start + size].astype(F32)
            for term in group[1:]:
                value = value + term[:, start : start + size].astype(F32)
            return value

        for c in range(3):
            qkv[layer, c] = total(first, c * width, width)
        out[layer] = total(first, 3 * width, width)
        down[layer] = total(second, 0, hidden)
        up[layer] = total(second, hidden, hidden)
        if layer == 0:
            small = total(first, 4 * width, LANES)
            small = jnp.concatenate([small, jnp.zeros((LANES - rows, LANES), F32)], axis=0).T
            for k in range(layers):
                gains[k] = small[6 * k : 6 * k + 2, :rows]
                shifts[k] = small[6 * k + 2 : 6 * k + 6, :rows]
                for c in range(2):
                    line = lane_up + 2 * k + c
                    b_up[k : k + 1, c * rows : (c + 1) * rows] = small[line : line + 1, :rows]
                for c in range(3):
                    line = lane_qkv + 3 * k + c
                    b_qkv[c, k : k + 1] = small[line : line + 1, : b_qkv.shape[2]]


def attention_forward_kernel(layer, *refs):
    if layer == 0:
        tokens, *refs = refs
        state = tokens[...].astype(F32)
    else:
        middle, own, moved, *refs = refs
    rows, b_qkv, weight, seg_row, seg_column, x_ref, first_ref, proj_ref, attn_ref, lse_ref, part_ref, turned = refs
    base = 6 * layer
    if layer > 0:
        state = middle[...] + (own[...].astype(F32) + moved[...].astype(F32))
        state = state + rows[base - 1 : base, :]
    x_ref[...] = state
    norm, _ = normed(state)
    first = (norm * rows[base : base + 1, :] + rows[base + 2 : base + 3, :]).astype(BF)
    first_ref[...] = first
    width = weight.shape[1] // 512 * 128
    proj = dot_nn(first, weight[:, : 3 * width]) + b_qkv[layer : layer + 1, :]
    proj_ref[...] = proj.astype(BF).T
    length = state.shape[0]
    lse_ref[...] = jnp.zeros(lse_ref.shape, F32)
    for head in range(width // HD):
        own_rows = slice(head * HD, (head + 1) * HD)
        query = proj_ref[own_rows, :] * BF(HD**-0.5)
        keys = proj_ref[width + head * HD : width + (head + 1) * HD, :]
        values = proj_ref[2 * width + head * HD : 2 * width + (head + 1) * HD, :]
        for start, low, high in query_blocks(length):
            block = slice(start, start + QUERY_BLOCK)
            scores = dot_tn(keys[:, low:high], query[:, block])
            same = seg_column[low:high, :] == seg_row[:, block]
            scores = jnp.where(same, scores, MASKED)
            highest = jnp.max(scores, axis=0, keepdims=True)
            unnormed = jnp.exp(scores - highest)
            summed = jnp.sum(unnormed, axis=0, keepdims=True)
            lse_ref[head : head + 1, block] = highest + jnp.log(summed)
            probs = (unnormed * (1.0 / summed)).astype(BF)
            turned[own_rows, block] = dot_nn(values[:, low:high], probs).astype(BF)
    attn = turned[...].T
    attn_ref[...] = attn
    part_ref[...] = dot_nt(attn, weight[:, 3 * width : 4 * width]).astype(BF)


def up_kernel(layer, state, own, moved, rows, b_up, weight, middle_ref, second_ref, hidden_ref, slope_ref):
    base = 6 * layer
    middle = state[...] + (own[...].astype(F32) + moved[...].astype(F32))
    middle = middle + rows[base + 4 : base + 5, :]
    middle_ref[...] = middle
    norm, _ = normed(middle)
    second = (norm * rows[base + 1 : base + 2, :] + rows[base + 3 : base + 4, :]).astype(BF)
    second_ref[...] = second
    for start in range(0, hidden_ref.shape[1], HIDDEN_BLOCK):
        block = slice(start, start + HIDDEN_BLOCK)
        pre = dot_nn(second, weight[:, block]) + b_up[layer : layer + 1, block]
        below = 0.5 * (1.0 + lax.erf(pre * 0.7071067811865476))
        hidden_ref[:, block] = (pre * below).astype(BF)
        density = jnp.exp(-0.5 * pre * pre) * 0.3989422804014327
        slope_ref[:, block] = below + pre * density


def down_kernel(hidden, weight, part_ref):
    part_ref[...] = dot_nt(hidden[...], weight[...]).astype(BF)


def hidden_back_kernel(layer, last, *refs):
    if last:
        cotangent, *refs = refs
        grad = cotangent[...].astype(F32)
    else:
        above, own, moved, state, *refs = refs
    rows, w_up, w_down, slope, grad_ref, low_ref, pre_ref, part_ref, shift_ref, bias_ref, *more = refs
    if not last:
        gain_ref, norm_shift_ref = more
        arrived = own[...].astype(F32) + moved[...].astype(F32)
        norm, inverse = normed(state[...])
        upper = 6 * (layer + 1)
        back, gain_ref[...], norm_shift_ref[...] = norm_back(
            arrived, norm, inverse, rows[upper : upper + 1, :]
        )
        grad = above[...] + back
    grad_ref[...] = grad
    low = grad.astype(BF)
    low_ref[...] = low
    shift_ref[...] = jnp.sum(grad, axis=0, keepdims=True)
    for start in range(0, w_up.shape[1], HIDDEN_BLOCK):
        block = slice(start, start + HIDDEN_BLOCK)
        back = dot_nn(low, w_down[:, block])
        pre = (back * slope[:, block]).astype(BF)
        pre_ref[:, block] = pre
        bias_ref[:, block] = jnp.sum(pre.astype(F32), axis=0, keepdims=True)
    part_ref[...] = dot_nt(pre_ref[...], w_up[...]).astype(BF)


def attention_back_kernel(layer, *refs):
    (grad, own, moved, middle, rows, weight, proj, lse, seg_row, seg_column) = refs[:10]
    (below_ref, low_ref, grad_qk_ref, grad_v_ref, part_ref, gain_ref, norm_shift_ref, shift_ref, bias_ref) = refs[10:19]
    turned, turned_proj, probs_ref, scores_ref = refs[19:]
    base = 6 * layer
    arrived = own[...].astype(F32) + moved[...].astype(F32)
    norm, inverse = normed(middle[...])
    back, gain_ref[...], norm_shift_ref[...] = norm_back(
        arrived, norm, inverse, rows[base + 1 : base + 2, :]
    )
    below = grad[...] + back
    below_ref[...] = below
    shift_ref[...] = jnp.sum(below, axis=0, keepdims=True)
    low = below.astype(BF)
    low_ref[...] = low
    width = weight.shape[1] // 512 * 128
    turned[...] = dot_nn(low, weight[:, 3 * width : 4 * width]).astype(BF).T
    length = below.shape[0]
    probs_ref[...] = jnp.zeros(probs_ref.shape, BF)
    scores_ref[...] = jnp.zeros(scores_ref.shape, BF)
    for head in range(width // HD):
        slot = head % 2
        own_rows = slice(head * HD, (head + 1) * HD)
        key_rows = slice(width + head * HD, width + (head + 1) * HD)
        value_rows = slice(2 * width + head * HD, 2 * width + (head + 1) * HD)
        query = proj[own_rows, :] * BF(HD**-0.5)
        keys, values, mixed = proj[key_rows, :], proj[value_rows, :], turned[own_rows, :]
        for start, low_key, high in query_blocks(length):
            block = slice(start, start + QUERY_BLOCK)
            scores = dot_tn(keys[:, low_key:high], query[:, block])
            same = seg_column[low_key:high, :] == seg_row[:, block]
            scores = jnp.where(same, scores, MASKED)
            probs = jnp.exp(scores - lse[head : head + 1, block])
            probs_ref[slot, low_key:high, block] = probs.astype(BF)
            grad_probs = dot_tn(values[:, low_key:high], mixed[:, block])
            centre = jnp.sum(probs * grad_probs, axis=0, keepdims=True)
            scores_ref[slot, low_key:high, block] = (probs * (grad_probs - centre)).astype(BF)
        grad_scores = scores_ref[slot]
        scaled_keys = keys * BF(HD**-0.5)
        turned_proj[own_rows, :] = dot_nn(scaled_keys, grad_scores).astype(BF)
        turned_proj[key_rows, :] = dot_nt(query, grad_scores).astype(BF)
        turned_proj[value_rows, :] = dot_nt(mixed, probs_ref[slot]).astype(BF)
    grad_proj = turned_proj[...].T
    grad_qk_ref[...] = grad_proj[:, : 2 * width]
    grad_v_ref[...] = grad_proj[:, 2 * width :]
    bias_ref[...] = jnp.sum(grad_proj.astype(F32), axis=0, keepdims=True)
    part_ref[...] = dot_nt(grad_proj, weight[:, : 3 * width]).astype(BF)


def input_back_kernel(above, own, moved, tokens, rows, out_ref, gain_ref, norm_shift_ref):
    arrived = own[...].astype(F32) + moved[...].astype(F32)
    norm, inverse = normed(tokens[...].astype(F32))
    back, gain_ref[...], norm_shift_ref[...] = norm_back(arrived, norm, inverse, rows[:1, :])
    out_ref[...] = above[...] + back


def packed_plainly(norm_gains, shifts, qkv_weight, qkv_bias, out_turned, up_weight, up_bias, down_turned):
    layers = norm_gains.shape[0]
    pieces = []
    for layer in range(layers):
        first = [qkv_weight[layer, c] for c in range(3)] + [out_turned[layer]]
        given = [jnp.concatenate(first, axis=1), up_weight[layer], down_turned[layer]]
        pieces.append([lax.all_gather(w.astype(BF), "dp", axis=0, tiled=True) for w in given])

    def whole(vector, axis):
        return lax.all_gather(vector.astype(BF), "dp", axis=axis, tiled=True).astype(F32)

    both = jnp.concatenate([norm_gains, shifts], axis=1)
    rows = whole(both, 2).reshape(6 * layers, -1)
    rows = jnp.pad(rows, ((0, -rows.shape[0] % 16), (0, 0)))
    up = jnp.pad(whole(up_bias, 1), ((0, 8 - layers), (0, 0)))
    qkv = jnp.pad(whole(qkv_bias, 2).reshape(layers, -1), ((0, 8 - layers), (0, 0)))
    return pieces, (rows, up, qkv)


def on_device(
    tokens,
    segments,
    cotangent,
    norm_gains,
    shifts,
    qkv_weight,
    qkv_bias,
    out_weight,
    up_weight,
    up_bias,
    down_weight,
):
    count, length, width = tokens.shape
    layers, _, rows, head_width = qkv_weight.shape
    hidden = up_weight.shape[2]
    planned = lax.axis_size("dp") == PARTS and rows % 48 == 0 and layers == 2
    tokens = tokens.reshape(length, width)
    cotangent = cotangent.reshape(length, width)
    seg_row, seg_column = segments.reshape(1, length), segments.reshape(length, 1)
    out_turned, down_turned = jnp.swapaxes(out_weight, 1, 2), jnp.swapaxes(down_weight, 1, 2)

    if planned:
        size = qkv_bias.shape[2]
        bias_turned = jnp.swapaxes(qkv_bias, 0, 1)
        wide = 4 * head_width
        given = [norm_gains, shifts, up_bias, bias_turned, qkv_weight, out_turned]
        held = [a.shape for a in given[:4]] + [a.shape[1:] for a in given[4:]]
        (first_piece,) = call(
            pack_first_kernel,
            [((rows, wide + LANES), BF)],
            given,
            scratch=[pltpu.VMEM(shape, F32) for shape in held]
            + [pltpu.VMEM((LANES, LANES), F32), pltpu.SemaphoreType.DMA((len(held),))],
            limit=8,
            space=pl.ANY,
        )
        half = hidden // 2
        shapes = [((rows, size), BF) for size in (2 * hidden, wide, hidden, half, hidden - half)]
        ffn, *others = call(pack_kernel, shapes, [qkv_weight, out_turned, up_weight, down_turned])
        arrays = gather(
            [first_piece, ffn, others[:2], others[2:]],
            [[wide, LANES], [hidden, hidden], [wide, hidden], [hidden]],
        )
        arrays = [array for bundle in arrays for array in bundle]
        columns = arrays.pop(1)
        weights = [arrays[:3], arrays[3:]]
        vectors = call(
            functools.partial(unpack_kernel, layers, size),
            [((16, width), F32), ((8, hidden), F32), ((8, 3 * head_width), F32)],
            [columns],
            scratch=[pltpu.VMEM((hidden, LANES), F32), pltpu.VMEM((3 * head_width, LANES), F32)],
            limit=8,
        )
        links = [Link(window) for window in WINDOWS]
    else:
        weights, vectors = packed_plainly(
            norm_gains, shifts, qkv_weight, qkv_bias, out_turned, up_weight, up_bias, down_turned
        )
    rows_all, b_up, b_qkv = vectors

    token_f32, token_bf = ((length, width), F32), ((length, width), BF)
    proj_flops = 2 * length * width * 3 * head_width
    out_flops = 2 * length * width * head_width
    hidden_flops = 2 * length * width * hidden
    head_flops = 2 * length * length * head_width

    records, before = [], [tokens]
    for layer in range(layers):
        w_qkvo, w_up, w_down = weights[layer]
        state, first, proj, attn, lse, part = call(
            functools.partial(attention_forward_kernel, layer),
            [
                token_f32,
                token_bf,
                ((3 * head_width, length), BF),
                ((length, head_width), BF),
                ((8, length), F32),
                token_bf,
            ],
            before + [rows_all, b_qkv, w_qkvo, seg_row, seg_column],
            scratch=[pltpu.VMEM((head_width, length), BF)],
            flops=proj_flops + out_flops + 2 * head_flops,
        )
        middle, second, active, slope = call(
            functools.partial(up_kernel, layer),
            [token_f32, token_bf, ((length, hidden), BF), ((length, hidden), F32)],
            [state, part, swap(part), rows_all, b_up, w_up],
            flops=2 * hidden_flops,
        )
        (part,) = call(down_kernel, [token_bf], [active, w_down], flops=hidden_flops)
        before = [middle, part, swap(part)]
        records.append((state, first, proj, attn, lse, middle, second, active, slope))
    middle, part, moved = before
    result = middle + (part.astype(F32) + moved.astype(F32)) + rows_all[6 * layers - 1]
    result = result.astype(BF).reshape(count, length, width)

    vector_grads = [[None] * 8 for _ in range(layers)]
    orders = ("x", "y") if planned else (None, None)
    line = ((1, width), F32)
    above, terms = [cotangent], [None] * (2 * layers)
    halves_of, begun, folded = [None] * (2 * layers), [None] * (2 * layers), [None] * (2 * layers)

    def begin(number, front, back):
        halves_of[number] = [products(orders[0], *front), products(orders[1], *back)]
        if planned:
            begun[number] = scatter_begin(links, *halves_of[number])
        return [half[0] for half in halves_of[number]]

    def fold(number, token):
        if not planned:
            return []
        halves = [(after(stay, token), moved) for stay, moved in begun[number]]
        folded[number], sent = scatter_fold(links, *halves)
        return sent

    def arrived(number):
        return [moved for _, moved in begun[number]] if planned else []

    for layer in reversed(range(layers)):
        w_qkvo, w_up, w_down = weights[layer]
        state, first, proj, attn, lse, middle, second, active, slope = records[layer]
        last = layer == layers - 1
        if not last:
            above[0] = after(above[0], fold(2 * layer + 3, ready))
        outs = [token_f32, token_bf, ((length, hidden), BF), token_bf, line, ((1, hidden), F32)]
        grad, low, pre, part, grad_shift, grad_up, *more = call(
            functools.partial(hidden_back_kernel, layer, last),
            outs + ([] if last else [line] * 2),
            above + [rows_all, w_up, w_down, slope],
            flops=2 * hidden_flops,
        )
        mine = vector_grads[layer]
        mine[5], mine[6] = grad_shift, grad_up
        if not last:
            vector_grads[layer + 1][0], vector_grads[layer + 1][2] = more
        moved = swap(part)
        ready = begin(2 * layer + 1, [(low, active)], [(second, pre)])
        if not last:
            ready += arrived(2 * layer + 2)
        below, low, grad_qk, grad_v, part, *more = call(
            functools.partial(attention_back_kernel, layer),
            [
                token_f32,
                token_bf,
                ((length, 2 * head_width), BF),
                ((length, head_width), BF),
                token_bf,
                line,
                line,
                line,
                ((1, 3 * head_width), F32),
            ],
            [after(grad, ready), part, moved, middle, rows_all, w_qkvo, proj, lse]
            + [seg_row, seg_column],
            scratch=[
                pltpu.VMEM((head_width, length), BF),
                pltpu.VMEM((3 * head_width, length), BF),
                pltpu.VMEM((2, length, length), BF),
                pltpu.VMEM((2, length, length), BF),
            ],
            flops=proj_flops + out_flops + 5 * head_flops,
        )
        mine[1], mine[3], mine[4], mine[7] = more
        moved = swap(part)
        front, back = [(first, grad_qk)], [(first, grad_v), (low, attn)]
        if not last:
            fold(2 * layer + 2, part)
        if layer > 0:
            ready = begin(2 * layer, front, back)
            below = after(below, ready)
        above = [below, part, moved, state]
    below, part, moved, _ = above
    input_grad, grad_gain, grad_shift = call(
        input_back_kernel, [token_f32, line, line], [below, part, moved, tokens, rows_all]
    )
    vector_grads[0][0], vector_grads[0][2] = grad_gain, grad_shift
    input_grad = input_grad.reshape(count, length, width)

    if planned:
        (columns,) = call(
            functools.partial(pack_grads_kernel, layers, size),
            [((width, LANES), BF)],
            [vector for mine in vector_grads for vector in mine],
            scratch=[
                pltpu.VMEM((LANES, width), F32),
                pltpu.VMEM((LANES, hidden), F32),
                pltpu.VMEM((LANES, 3 * head_width), F32),
            ],
            limit=16,
        )
        halves_of[0] = products("x", *front), products("y", *back, columns)
        ready = [half[0] for half in halves_of[0]]
        begun[0] = scatter_begin(links, *halves_of[0])
        ends = [after(folded[3][0], part), *folded[3][1:], *folded[2]]
        last_layer = scatter_line(ends)
        split = 2 * hidden
        terms[3], terms[2] = [last_layer[:, :split]], [last_layer[:, split:]]
        fold(1, ready)
        fold(0, ready)
        terms[1] = [scatter_line([after(folded[1][0], ready), *folded[1][1:]])]
        terms[0] = scatter_steps(links[2], [after(folded[0][0], ready), *folded[0][1:]])
        outs = [
            (norm_gains.shape, F32),
            (shifts.shape, F32),
            (qkv_weight.shape, F32),
            (bias_turned.shape, F32),
            (out_turned.shape, F32),
            (up_weight.shape, F32),
            (up_bias.shape, F32),
            (down_turned.shape, F32),
        ]
        given = [term for number in range(2 * layers) for term in terms[number]]
        counts = [len(group) for group in terms]
        done = call(functools.partial(finish_kernel, layers, counts), outs, given, limit=24)
        gains, shift, qkv, b_qkv_grad, out, up, b_up_grad, down = done
        b_qkv_grad = jnp.swapaxes(b_qkv_grad, 0, 1)
    else:
        terms = halves_of
        terms[0] = [products(orders[0], *front), products(orders[1], *back)]

        def shared(value, axis):
            return lax.psum_scatter(value, "dp", scatter_dimension=axis, tiled=True)

        summed = [[shared(half[0].astype(F32), 0) for half in pair] for pair in terms]
        cut = [jnp.concatenate(summed[2 * layer], axis=1) for layer in range(layers)]
        qkv = jnp.stack(
            [
                jnp.stack([piece[:, c * head_width : (c + 1) * head_width] for c in range(3)])
                for piece in cut
            ]
        )
        out = jnp.stack([piece[:, 3 * head_width :] for piece in cut])
        down = jnp.stack([summed[2 * layer + 1][0] for layer in range(layers)])
        up = jnp.stack([summed[2 * layer + 1][1] for layer in range(layers)])
        both = jnp.stack([jnp.concatenate(mine[:6], axis=0) for mine in vector_grads])
        both = shared(both, 2)
        gains, shift = both[:, :2], both[:, 2:]
        b_up_grad = shared(jnp.concatenate([mine[6] for mine in vector_grads], axis=0), 1)
        b_qkv_grad = jnp.stack([mine[7].reshape(3, head_width) for mine in vector_grads])
        b_qkv_grad = shared(b_qkv_grad, 2)
    out, down = jnp.swapaxes(out, 1, 2), jnp.swapaxes(down, 1, 2)
    return (result, input_grad, gains, shift, qkv, b_qkv_grad, out, up, b_up_grad, down)


def solution(mesh):
    weights = (
        P(None, None, "dp"),
        P(None, None, "dp"),
        P(None, None, "dp", "tensor"),
        P(None, None, ("tensor", "dp")),
        P(None, "tensor", "dp"),
        P(None, "dp", "tensor"),
        P(None, ("tensor", "dp")),
        P(None, "tensor", "dp"),
    )
    rows = P("dp", None, None)
    return jax.shard_map(
        on_device,
        mesh=mesh,
        in_specs=(rows, P("dp", None), rows) + weights,
        out_specs=(rows, rows) + weights,
        check_vma=False,
    )
```

```python
import functools
import math

import jax
import jax.numpy as jnp
from jax import lax
from jax.experimental import pallas as pl
from jax.experimental.pallas import tpu as pltpu
from jax.sharding import PartitionSpec as P

HD = 64
EPSILON = 1e-05
MASKED = -1e30
BF = jnp.bfloat16
F32 = jnp.float32
SEGMENT_MAX = 96
QUERY_BLOCK = 128
HIDDEN_BLOCK = 256
LANES = 128
WINDOWS = 2, 2, 3

SZ, SY, SX = 4, 2, 2
PARTS = SZ * SY * SX


def contract(left, right, left_dim, right_dim):
    dims = (((left_dim,), (right_dim,)), ((), ()))
    return lax.dot_general(left, right, dims, preferred_element_type=F32)


def dot_nn(left, right):
    return contract(left, right, 1, 0)


def dot_nt(left, right):
    return contract(left, right, 1, 1)


def dot_tn(left, right):
    return contract(left, right, 0, 0)


def normed(state):
    mean = jnp.mean(state, axis=-1, keepdims=True)
    centred = state - mean
    inverse = lax.rsqrt(jnp.mean(centred * centred, axis=-1, keepdims=True) + EPSILON)
    return centred * inverse, inverse


def norm_back(grad, norm, inverse, gain):
    grad_gain = jnp.sum(grad * norm, axis=0, keepdims=True)
    grad_shift = jnp.sum(grad, axis=0, keepdims=True)
    scaled = grad * gain
    back = inverse * (
        scaled
        - jnp.mean(scaled, axis=-1, keepdims=True)
        - norm * jnp.mean(scaled * norm, axis=-1, keepdims=True)
    )
    return back, grad_gain, grad_shift


def query_blocks(length):
    blocks = []
    for start in range(0, length, QUERY_BLOCK):
        low = max(0, start - SEGMENT_MAX + 1) // QUERY_BLOCK * QUERY_BLOCK
        high = min(length, -(-(start + QUERY_BLOCK + SEGMENT_MAX - 1) // QUERY_BLOCK) * QUERY_BLOCK)
        blocks.append((start, low, high))
    return blocks


def call(kernel, outs, args, scratch=(), flops=0, limit=16, space=pltpu.VMEM):
    shapes = [jax.ShapeDtypeStruct(shape, kind) for shape, kind in outs]
    moved = sum(math.prod(a.shape) * a.dtype.itemsize for a in list(args) + shapes)
    vmem = pl.BlockSpec(memory_space=pltpu.VMEM)
    return pl.pallas_call(
        kernel,
        out_shape=shapes,
        in_specs=[pl.BlockSpec(memory_space=space)] * len(args),
        out_specs=[vmem] * len(outs),
        scratch_shapes=list(scratch),
        cost_estimate=pl.CostEstimate(flops=flops, bytes_accessed=moved, transcendentals=0),
        compiler_params=pltpu.CompilerParams(vmem_limit_bytes=limit << 20),
    )(*args)


def flip(value, mask):
    count = lax.axis_size("dp")
    return lax.ppermute(value, "dp", [(i, i ^ mask) for i in range(count)])


class Link:
    def __init__(self, window):
        self.window, self.sent = window, []

    def send(self, value, mask):
        if len(self.sent) >= self.window:
            value, _ = lax.optimization_barrier((value, self.sent[-self.window]))
        self.sent.append(flip(value, mask))
        return self.sent[-1]


def after(value, token):
    return lax.optimization_barrier((value, token))[0]


def swap(part):
    count = lax.axis_size("tensor")
    return lax.ppermute(part, "tensor", [(i, (i + 1) % count) for i in range(count)])


def place():
    me = lax.axis_index("dp")
    return me // (SY * SX), (me // SX) % SY, me % SX


def relative(order, y, x):
    blocks = []
    for number in range(PARTS):
        first, second, line = number // 8, number // 4 % 2, number % 4
        if order in "XY":
            line, second = number // 2 % 4, number % 2
        ky, kx = (second, first) if order in "xX" else (first, second)
        blocks.append((line * SY + (y ^ ky)) * SX + (x ^ kx))
    return blocks


def join_kernel(split, *refs):
    blocks, front, back = refs[:-2], refs[-2], refs[-1]
    rows = front.shape[0] // SZ
    z = place()[0]
    for distance, ref in enumerate(blocks):
        line = pl.ds(pl.multiple_of((z ^ distance) * rows, 16), rows)
        front[line, :] = ref[:, :split]
        back[line, :] = ref[:, split:]


def cut_kernel(line, *outs):
    start = 0
    for out in outs:
        out[...] = line[:, start : start + out.shape[1]]
        start += out.shape[1]


def place_kernel(*refs):
    parts, outs = refs[:8], refs[8:]
    _, y, x = place()
    rows = outs[0].shape[0] // PARTS
    reach = 0
    for half, order in enumerate("yx"):
        begin, reach = reach, reach + parts[4 * half].shape[1]
        start = 0
        for out in outs:
            end = start + out.shape[1]
            low, high = max(start, begin), min(end, reach)
            if low < high:
                for number, block in enumerate(relative(order, y, x)):
                    ref, line = parts[half * 4 + number // 4], number % 4
                    out[pl.ds(pl.multiple_of(block * rows, 16), rows), low - start : high - start] = ref[
                        line * rows : (line + 1) * rows, low - begin : high - begin
                    ]
            start = end


def lines():
    across = SY * SX
    return [[z * across + column for z in range(SZ)] for column in range(across)]


def pair_kernel(front, front_y, back, back_x, out):
    rows, split = front.shape
    for number, (left, right) in enumerate(((front, back), (front_y, back_x))):
        line = slice(number * rows, (number + 1) * rows)
        out[line, :split] = left[...]
        out[line, split:] = right[...]


def place_pairs_kernel(front, front_x, back, back_y, *outs):
    _, y, x = place()
    rows = outs[0].shape[0] // PARTS
    reach = 0
    for half, refs in enumerate(((front, front_x), (back, back_y))):
        begin, reach = reach, reach + refs[0].shape[1]
        start = 0
        for out in outs:
            end = start + out.shape[1]
            low, high = max(start, begin), min(end, reach)
            if low < high:
                for number in range(PARTS):
                    last, line, first = number // 8, number // 2 % 4, number % 2
                    ky, kx = (first, last) if half == 0 else (last, first)
                    block = (line * SY + (y ^ ky)) * SX + (x ^ kx)
                    at = (line * 2 + first) * rows
                    out[pl.ds(pl.multiple_of(block * rows, 16), rows), low - start : high - start] = refs[last][
                        at : at + rows, low - begin : high - begin
                    ]
            start = end


def over_z(piece):
    return lax.all_gather(piece, "dp", axis=0, tiled=True, axis_index_groups=lines())


def gather(pieces, widths):
    along_x, along_y, along_z = (Link(3) for _ in range(3))
    whole, line = [], None
    early = [(front, flip(front, SX), back, flip(back, 1)) for front, back in pieces[2:]]
    for number, piece in enumerate(pieces[:2]):
        rows, columns = piece.shape
        split = columns // 256 * 128
        shapes = [((SZ * rows, split), BF), ((SZ * rows, columns - split), BF)]
        if number == 0:
            arrived = [piece] + [along_z.send(piece, kz * SY * SX) for kz in range(1, SZ)]
            arrived[0] = after(piece, early)
            front, back = call(functools.partial(join_kernel, split), shapes, arrived, limit=8)
            tokens = [front]
        else:
            line = after(over_z(piece), tokens)
            tokens.append(line)
            front, back = call(cut_kernel, shapes, [line], limit=8)
        front_y, back_x = along_y.send(front, SX), along_x.send(back, 1)
        front_x, back_y = along_x.send(front, 1), along_y.send(back, SX)
        front_xy, back_xy = along_x.send(front_y, 1), along_y.send(back_x, SX)
        parts = [front, front_x, front_y, front_xy, back, back_y, back_x, back_xy]
        outs = [((PARTS * rows, width), BF) for width in widths[number]]
        whole.append(call(place_kernel, outs, parts, limit=12))
    for number, given in enumerate(early):
        rows, columns = given[0].shape[0], given[0].shape[1] + given[2].shape[1]
        (pair,) = call(pair_kernel, [((2 * rows, columns), BF)], given, limit=8)
        line = over_z(after(pair, tokens[number]))
        shapes = [((2 * SZ * rows, half.shape[1]), BF) for half in given[::2]]
        front, back = call(cut_kernel, shapes, [line], limit=8)
        front_x, back_y = along_x.send(front, 1), along_y.send(back, SX)
        outs = [((PARTS * rows, width), BF) for width in widths[2 + number]]
        whole.append(call(place_pairs_kernel, outs, [front, front_x, back, back_y], limit=12))
    return whole


def product_kernel(order, shares, *refs):
    count = 1 if order is None else 2
    scratch = refs[-1]
    outs = refs[-1 - count : -1]
    width = scratch.shape[0]
    blocks = None if order is None else relative(order, *place()[1:])
    rows = width // PARTS

    def put(start, size):
        if order is None:
            outs[0][:, start : start + size] = scratch[:, :size]
            return
        for number, block in enumerate(blocks):
            out, line = outs[number // 8 == 0], number % 8
            out[line * rows : (line + 1) * rows, start : start + size] = scratch[
                pl.ds(pl.multiple_of(block * rows, 16), rows), :size
            ]

    start, place_in = 0, 0
    for kind in shares:
        if kind == "ready":
            ready = refs[place_in]
            place_in += 1
            size = ready.shape[1]
            scratch[:, :size] = ready[...]
            put(start, size)
            start += size
            continue
        left, right = refs[place_in], refs[place_in + 1]
        place_in += 2
        turned = left[...].T
        for first in range(0, right.shape[1], 384):
            size = min(384, right.shape[1] - first)
            scratch[:, :size] = dot_nn(turned, right[:, first : first + size]).astype(BF)
            put(start, size)
            start += size


def products(order, *shares):
    args, kinds, columns, flops = [], [], 0, 0
    for share in shares:
        if isinstance(share, tuple):
            kinds.append("product")
            args += share
            columns += share[1].shape[1]
            width = share[0].shape[1]
            flops += 2 * math.prod(share[0].shape) * share[1].shape[1]
        else:
            kinds.append("ready")
            args.append(share)
            columns += share.shape[1]
            width = share.shape[0]
    outs = [((width, columns), BF)] if order is None else [((width // 2, columns), BF)] * 2
    return call(
        functools.partial(product_kernel, order, tuple(kinds)),
        outs,
        args,
        scratch=[pltpu.VMEM((width, 384), BF)],
        flops=flops,
        limit=24,
    )


def fold_kernel(keep, moved, away, stay):
    half = keep.shape[0] // 2
    total = keep[...].astype(F32) + moved[...].astype(F32)
    stay[...] = total[:half].astype(BF)
    away[...] = total[half:].astype(BF)


def line_kernel(*refs):
    ends, outs = refs[:4], refs[4:]
    rows = ends[0].shape[0] // SZ
    z = place()[0]
    for distance, out in enumerate(outs):
        line = slice(None)
        if len(outs) > 1:
            line = pl.ds(pl.multiple_of((z ^ distance) * rows, 16), rows)
        start = 0
        for keep, moved in zip(ends[::2], ends[1::2]):
            size = keep.shape[1]
            total = keep[line, :].astype(F32) + moved[line, :].astype(F32)
            out[:, start : start + size] = total.astype(out.dtype)
            start += size


def wide_line_kernel(*refs):
    ends, halves, out = refs[:4], refs[4:8], refs[8]
    rows = out.shape[0] // SZ
    start = 0
    for keep, moved in zip(ends[::2], ends[1::2]):
        size = keep.shape[1]
        total = keep[...].astype(F32) + moved[...].astype(F32)
        out[:, start : start + size] = total.astype(BF)
        start += size
    for distance in range(2):
        for stay, moved in zip(halves[::2], halves[1::2]):
            size = stay.shape[1]
            for line in range(SZ):
                at = slice((2 * line + distance) * rows, (2 * line + distance + 1) * rows)
                total = stay[at, :].astype(F32) + moved[at, :].astype(F32)
                out[line * rows : (line + 1) * rows, start : start + size] = total.astype(BF)
            start += size


def scatter_begin(links, half_a, half_b):
    along_x, along_y, _ = links
    moved_a, moved_b = along_x.send(half_a[0], 1), along_y.send(half_b[0], SX)
    return (half_a[1], moved_a), (half_b[1], moved_b)


def scatter_fold(links, *halves):
    along_x, along_y, _ = links
    folded = []
    for stay, moved in halves:
        shape = (stay.shape[0] // 2, stay.shape[1])
        folded.append(call(fold_kernel, [(shape, BF)] * 2, [stay, moved], limit=8))
    (away_a, stay_a), (away_b, stay_b) = folded
    moved_a, moved_b = along_y.send(away_a, SX), along_x.send(away_b, 1)
    return [stay_a, moved_a, stay_b, moved_b], [away_a, away_b]


def scatter_line(ends, halves=()):
    height, columns = ends[0].shape[0], sum(end.shape[1] for end in ends[::2])
    columns += 2 * sum(stay.shape[1] for stay, _ in halves)
    given = [*ends, *(value for half in halves for value in half)]
    kernel = wide_line_kernel if halves else line_kernel
    (line,) = call(kernel, [((height, columns), BF)], given, limit=12)
    return lax.psum_scatter(
        line, "dp", scatter_dimension=0, tiled=True, axis_index_groups=lines()
    )


def scatter_steps(along_z, ends):
    rows, columns = ends[0].shape[0] // SZ, sum(end.shape[1] for end in ends[::2])
    outs = [((rows, columns), F32)] + [((rows, columns), BF)] * (SZ - 1)
    own, *line = call(line_kernel, outs, ends, limit=8)
    return [own] + [along_z.send(block, kz * SY * SX) for kz, block in zip(range(1, SZ), line)]


def lanes_of(layers):
    up = 6 * layers
    return up, up + 2 * layers


def pack_first_kernel(*refs):
    given, piece, held, scratch, sems = refs[:6], refs[6], refs[7:13], refs[13], refs[14]
    sources = list(given[:4]) + [given[4].at[0], given[5].at[0]]
    copies = [
        pltpu.make_async_copy(source, target, sems.at[number])
        for number, (source, target) in enumerate(zip(sources, held))
    ]
    for copy in copies:
        copy.start()
    scratch[...] = jnp.zeros(scratch.shape, F32)
    for copy in copies:
        copy.wait()
    gains, shifts, b_up, b_qkv, qkv, out = held
    _, rows, width = qkv.shape
    layers = gains.shape[0]
    lane_up, lane_qkv = lanes_of(layers)
    for layer in range(layers):
        base = 6 * layer
        scratch[base : base + 2, :rows] = gains[layer]
        scratch[base + 2 : base + 6, :rows] = shifts[layer]
        for c in range(2):
            line = lane_up + 2 * layer + c
            scratch[line : line + 1, :rows] = b_up[layer : layer + 1, c * rows : (c + 1) * rows]
        for c in range(3):
            line = lane_qkv + 3 * layer + c
            scratch[line : line + 1, : b_qkv.shape[2]] = b_qkv[c, layer : layer + 1]
    for c in range(3):
        piece[:, c * width : (c + 1) * width] = qkv[c].astype(BF)
    piece[:, 3 * width : 4 * width] = out[...].astype(BF)
    piece[:, 4 * width :] = scratch[...].T[:rows].astype(BF)


def pack_kernel(qkv, out, up, down, ffn, second, up_half, down_front, down_back):
    width, hidden = qkv.shape[3], up.shape[2]
    ffn[:, :hidden] = up[0].astype(BF)
    ffn[:, hidden:] = down[0].astype(BF)
    for c in range(3):
        second[:, c * width : (c + 1) * width] = qkv[1, c].astype(BF)
    second[:, 3 * width :] = out[1].astype(BF)
    up_half[...] = up[1].astype(BF)
    split = down_front.shape[1]
    down_front[...] = down[1, :, :split].astype(BF)
    down_back[...] = down[1, :, split:].astype(BF)


def unpack_kernel(layers, size, columns, rows_out, up_out, qkv_out, up_scratch, qkv_scratch):
    lane_up, lane_qkv = lanes_of(layers)
    wide = columns[...].astype(F32)
    rows_out[...] = wide.T[: rows_out.shape[0]]
    rows = columns.shape[0] // PARTS
    lane = lax.broadcasted_iota(jnp.int32, (rows, LANES), 1)

    def merged(block, lanes):
        total = jnp.zeros((block.shape[0], LANES), F32)
        for layer, at in enumerate(lanes):
            total = jnp.where(lane[: block.shape[0]] == layer, block[:, at : at + 1], total)
        return total

    width = qkv_out.shape[1] // 3
    for part in range(PARTS):
        block = wide[part * rows : (part + 1) * rows]
        for c in range(2):
            start = (part * 2 + c) * rows
            up_scratch[start : start + rows, :] = merged(
                block, [lane_up + 2 * layer + c for layer in range(layers)]
            )
        for c in range(3):
            start = c * width + part * size
            qkv_scratch[start : start + size, :] = merged(
                block[:size], [lane_qkv + 3 * layer + c for layer in range(layers)]
            )
    up_out[...] = up_scratch[...].T[: up_out.shape[0]]
    qkv_out[...] = qkv_scratch[...].T[: qkv_out.shape[0]]


def pack_grads_kernel(layers, size, *refs):
    out, rows_scratch, up_scratch, qkv_scratch = refs[-4:]
    lane_up, lane_qkv = lanes_of(layers)
    rows_scratch[...] = jnp.zeros(rows_scratch.shape, F32)
    up_scratch[...] = jnp.zeros(up_scratch.shape, F32)
    qkv_scratch[...] = jnp.zeros(qkv_scratch.shape, F32)
    for layer in range(layers):
        given = refs[8 * layer : 8 * layer + 8]
        for number in range(6):
            line = 6 * layer + number
            rows_scratch[line : line + 1, :] = given[number][...]
        up_scratch[layer : layer + 1, :] = given[6][...]
        qkv_scratch[layer : layer + 1, :] = given[7][...]
    columns = rows_scratch[...].T
    up, qkv = up_scratch[...].T, qkv_scratch[...].T
    rows = out.shape[0] // PARTS
    width = qkv.shape[0] // 3
    lane = lax.broadcasted_iota(jnp.int32, (rows, LANES), 1)
    for part in range(PARTS):
        total = columns[part * rows : (part + 1) * rows]
        for layer in range(layers):
            for c in range(2):
                start = (part * 2 + c) * rows
                value = up[start : start + rows, layer : layer + 1]
                total = jnp.where(lane == lane_up + 2 * layer + c, value, total)
            for c in range(3):
                start = c * width + part * size
                value = jnp.concatenate(
                    [
                        qkv[start : start + size, layer : layer + 1],
                        jnp.zeros((rows - size, 1), F32),
                    ],
                    axis=0,
                )
                total = jnp.where(lane == lane_qkv + 3 * layer + c, value, total)
        out[part * rows : (part + 1) * rows, :] = total.astype(BF)


def finish_kernel(layers, counts, *refs):
    outs, groups, start = refs[sum(counts) :], [], 0
    for count in counts:
        groups.append(refs[start : start + count])
        start += count
    gains, shifts, qkv, b_qkv, out, up, b_up, down = outs
    rows, width = qkv.shape[2:]
    hidden = up.shape[2]
    lane_up, lane_qkv = lanes_of(layers)
    for layer in range(layers):
        first, second = groups[2 * layer], groups[2 * layer + 1]

        def total(group, start, size):
            if len(group) == 3:
                own, *moved = group
                split = moved[0].shape[1]
                other, at = (moved[0], start) if start < split else (moved[1], start - split)
                value = own[:, start : start + size].astype(F32)
                return value + other[:, at : at + size].astype(F32)
            value = group[0][:, start : start + size].astype(F32)
            for term in group[1:]:
                value = value + term[:, start : start + size].astype(F32)
            return value

        for c in range(3):
            qkv[layer, c] = total(first, c * width, width)
        out[layer] = total(first, 3 * width, width)
        down[layer] = total(second, 0, hidden)
        up[layer] = total(second, hidden, hidden)
        if layer == 0:
            small = total(first, 4 * width, LANES)
            small = jnp.concatenate([small, jnp.zeros((LANES - rows, LANES), F32)], axis=0).T
            for k in range(layers):
                gains[k] = small[6 * k : 6 * k + 2, :rows]
                shifts[k] = small[6 * k + 2 : 6 * k + 6, :rows]
                for c in range(2):
                    line = lane_up + 2 * k + c
                    b_up[k : k + 1, c * rows : (c + 1) * rows] = small[line : line + 1, :rows]
                for c in range(3):
                    line = lane_qkv + 3 * k + c
                    b_qkv[c, k : k + 1] = small[line : line + 1, : b_qkv.shape[2]]


def attention_forward_kernel(layer, *refs):
    if layer == 0:
        tokens, *refs = refs
        state = tokens[...].astype(F32)
    else:
        middle, own, moved, *refs = refs
    rows, b_qkv, weight, seg_row, seg_column, x_ref, first_ref, proj_ref, attn_ref, lse_ref, part_ref, turned = refs
    base = 6 * layer
    if layer > 0:
        state = middle[...] + (own[...].astype(F32) + moved[...].astype(F32))
        state = state + rows[base - 1 : base, :]
    x_ref[...] = state
    norm, _ = normed(state)
    first = (norm * rows[base : base + 1, :] + rows[base + 2 : base + 3, :]).astype(BF)
    first_ref[...] = first
    width = weight.shape[1] // 512 * 128
    proj = dot_nn(first, weight[:, : 3 * width]) + b_qkv[layer : layer + 1, :]
    proj_ref[...] = proj.astype(BF).T
    length = state.shape[0]
    lse_ref[...] = jnp.zeros(lse_ref.shape, F32)
    for head in range(width // HD):
        own_rows = slice(head * HD, (head + 1) * HD)
        query = proj_ref[own_rows, :] * BF(HD**-0.5)
        keys = proj_ref[width + head * HD : width + (head + 1) * HD, :]
        values = proj_ref[2 * width + head * HD : 2 * width + (head + 1) * HD, :]
        for start, low, high in query_blocks(length):
            block = slice(start, start + QUERY_BLOCK)
            scores = dot_tn(keys[:, low:high], query[:, block])
            same = seg_column[low:high, :] == seg_row[:, block]
            scores = jnp.where(same, scores, MASKED)
            highest = jnp.max(scores, axis=0, keepdims=True)
            unnormed = jnp.exp(scores - highest)
            summed = jnp.sum(unnormed, axis=0, keepdims=True)
            lse_ref[head : head + 1, block] = highest + jnp.log(summed)
            probs = (unnormed * (1.0 / summed)).astype(BF)
            turned[own_rows, block] = dot_nn(values[:, low:high], probs).astype(BF)
    attn = turned[...].T
    attn_ref[...] = attn
    part_ref[...] = dot_nt(attn, weight[:, 3 * width : 4 * width]).astype(BF)


def up_kernel(layer, state, own, moved, rows, b_up, weight, middle_ref, second_ref, hidden_ref, slope_ref):
    base = 6 * layer
    middle = state[...] + (own[...].astype(F32) + moved[...].astype(F32))
    middle = middle + rows[base + 4 : base + 5, :]
    middle_ref[...] = middle
    norm, _ = normed(middle)
    second = (norm * rows[base + 1 : base + 2, :] + rows[base + 3 : base + 4, :]).astype(BF)
    second_ref[...] = second
    for start in range(0, hidden_ref.shape[1], HIDDEN_BLOCK):
        block = slice(start, start + HIDDEN_BLOCK)
        pre = dot_nn(second, weight[:, block]) + b_up[layer : layer + 1, block]
        below = 0.5 * (1.0 + lax.erf(pre * 0.7071067811865476))
        hidden_ref[:, block] = (pre * below).astype(BF)
        density = jnp.exp(-0.5 * pre * pre) * 0.3989422804014327
        slope_ref[:, block] = below + pre * density


def down_kernel(hidden, weight, part_ref):
    part_ref[...] = dot_nt(hidden[...], weight[...]).astype(BF)


def hidden_back_kernel(layer, last, *refs):
    if last:
        cotangent, *refs = refs
        grad = cotangent[...].astype(F32)
    else:
        above, own, moved, state, *refs = refs
    rows, w_up, w_down, slope, grad_ref, low_ref, pre_ref, part_ref, shift_ref, bias_ref, *more = refs
    if not last:
        gain_ref, norm_shift_ref = more
        arrived = own[...].astype(F32) + moved[...].astype(F32)
        norm, inverse = normed(state[...])
        upper = 6 * (layer + 1)
        back, gain_ref[...], norm_shift_ref[...] = norm_back(
            arrived, norm, inverse, rows[upper : upper + 1, :]
        )
        grad = above[...] + back
    grad_ref[...] = grad
    low = grad.astype(BF)
    low_ref[...] = low
    shift_ref[...] = jnp.sum(grad, axis=0, keepdims=True)
    for start in range(0, w_up.shape[1], HIDDEN_BLOCK):
        block = slice(start, start + HIDDEN_BLOCK)
        back = dot_nn(low, w_down[:, block])
        pre = (back * slope[:, block]).astype(BF)
        pre_ref[:, block] = pre
        bias_ref[:, block] = jnp.sum(pre.astype(F32), axis=0, keepdims=True)
    part_ref[...] = dot_nt(pre_ref[...], w_up[...]).astype(BF)


def attention_back_kernel(layer, *refs):
    (grad, own, moved, middle, rows, weight, proj, lse, seg_row, seg_column) = refs[:10]
    (below_ref, low_ref, grad_qk_ref, grad_v_ref, part_ref, gain_ref, norm_shift_ref, shift_ref, bias_ref) = refs[10:19]
    turned, turned_proj, probs_ref, scores_ref = refs[19:]
    base = 6 * layer
    arrived = own[...].astype(F32) + moved[...].astype(F32)
    norm, inverse = normed(middle[...])
    back, gain_ref[...], norm_shift_ref[...] = norm_back(
        arrived, norm, inverse, rows[base + 1 : base + 2, :]
    )
    below = grad[...] + back
    below_ref[...] = below
    shift_ref[...] = jnp.sum(below, axis=0, keepdims=True)
    low = below.astype(BF)
    low_ref[...] = low
    width = weight.shape[1] // 512 * 128
    turned[...] = dot_nn(low, weight[:, 3 * width : 4 * width]).astype(BF).T
    length = below.shape[0]
    probs_ref[...] = jnp.zeros(probs_ref.shape, BF)
    scores_ref[...] = jnp.zeros(scores_ref.shape, BF)
    for head in range(width // HD):
        slot = head % 2
        own_rows = slice(head * HD, (head + 1) * HD)
        key_rows = slice(width + head * HD, width + (head + 1) * HD)
        value_rows = slice(2 * width + head * HD, 2 * width + (head + 1) * HD)
        query = proj[own_rows, :] * BF(HD**-0.5)
        keys, values, mixed = proj[key_rows, :], proj[value_rows, :], turned[own_rows, :]
        for start, low_key, high in query_blocks(length):
            block = slice(start, start + QUERY_BLOCK)
            scores = dot_tn(keys[:, low_key:high], query[:, block])
            same = seg_column[low_key:high, :] == seg_row[:, block]
            scores = jnp.where(same, scores, MASKED)
            probs = jnp.exp(scores - lse[head : head + 1, block])
            probs_ref[slot, low_key:high, block] = probs.astype(BF)
            grad_probs = dot_tn(values[:, low_key:high], mixed[:, block])
            centre = jnp.sum(probs * grad_probs, axis=0, keepdims=True)
            scores_ref[slot, low_key:high, block] = (probs * (grad_probs - centre)).astype(BF)
        grad_scores = scores_ref[slot]
        scaled_keys = keys * BF(HD**-0.5)
        turned_proj[own_rows, :] = dot_nn(scaled_keys, grad_scores).astype(BF)
        turned_proj[key_rows, :] = dot_nt(query, grad_scores).astype(BF)
        turned_proj[value_rows, :] = dot_nt(mixed, probs_ref[slot]).astype(BF)
    grad_proj = turned_proj[...].T
    grad_qk_ref[...] = grad_proj[:, : 2 * width]
    grad_v_ref[...] = grad_proj[:, 2 * width :]
    bias_ref[...] = jnp.sum(grad_proj.astype(F32), axis=0, keepdims=True)
    part_ref[...] = dot_nt(grad_proj, weight[:, : 3 * width]).astype(BF)


def input_back_kernel(above, own, moved, tokens, rows, out_ref, gain_ref, norm_shift_ref):
    arrived = own[...].astype(F32) + moved[...].astype(F32)
    norm, inverse = normed(tokens[...].astype(F32))
    back, gain_ref[...], norm_shift_ref[...] = norm_back(arrived, norm, inverse, rows[:1, :])
    out_ref[...] = above[...] + back


def packed_plainly(norm_gains, shifts, qkv_weight, qkv_bias, out_turned, up_weight, up_bias, down_turned):
    layers = norm_gains.shape[0]
    pieces = []
    for layer in range(layers):
        first = [qkv_weight[layer, c] for c in range(3)] + [out_turned[layer]]
        given = [jnp.concatenate(first, axis=1), up_weight[layer], down_turned[layer]]
        pieces.append([lax.all_gather(w.astype(BF), "dp", axis=0, tiled=True) for w in given])

    def whole(vector, axis):
        return lax.all_gather(vector.astype(BF), "dp", axis=axis, tiled=True).astype(F32)

    both = jnp.concatenate([norm_gains, shifts], axis=1)
    rows = whole(both, 2).reshape(6 * layers, -1)
    rows = jnp.pad(rows, ((0, -rows.shape[0] % 16), (0, 0)))
    up = jnp.pad(whole(up_bias, 1), ((0, 8 - layers), (0, 0)))
    qkv = jnp.pad(whole(qkv_bias, 2).reshape(layers, -1), ((0, 8 - layers), (0, 0)))
    return pieces, (rows, up, qkv)


def on_device(
    tokens,
    segments,
    cotangent,
    norm_gains,
    shifts,
    qkv_weight,
    qkv_bias,
    out_weight,
    up_weight,
    up_bias,
    down_weight,
):
    count, length, width = tokens.shape
    layers, _, rows, head_width = qkv_weight.shape
    hidden = up_weight.shape[2]
    planned = lax.axis_size("dp") == PARTS and rows % 48 == 0 and layers == 2
    tokens = tokens.reshape(length, width)
    cotangent = cotangent.reshape(length, width)
    seg_row, seg_column = segments.reshape(1, length), segments.reshape(length, 1)
    out_turned, down_turned = jnp.swapaxes(out_weight, 1, 2), jnp.swapaxes(down_weight, 1, 2)

    if planned:
        size = qkv_bias.shape[2]
        bias_turned = jnp.swapaxes(qkv_bias, 0, 1)
        wide = 4 * head_width
        given = [norm_gains, shifts, up_bias, bias_turned, qkv_weight, out_turned]
        held = [a.shape for a in given[:4]] + [a.shape[1:] for a in given[4:]]
        (first_piece,) = call(
            pack_first_kernel,
            [((rows, wide + LANES), BF)],
            given,
            scratch=[pltpu.VMEM(shape, F32) for shape in held]
            + [pltpu.VMEM((LANES, LANES), F32), pltpu.SemaphoreType.DMA((len(held),))],
            limit=8,
            space=pl.ANY,
        )
        half = hidden // 2
        shapes = [((rows, size), BF) for size in (2 * hidden, wide, hidden, half, hidden - half)]
        ffn, *others = call(pack_kernel, shapes, [qkv_weight, out_turned, up_weight, down_turned])
        arrays = gather(
            [first_piece, ffn, others[:2], others[2:]],
            [[wide, LANES], [hidden, hidden], [wide, hidden], [hidden]],
        )
        arrays = [array for bundle in arrays for array in bundle]
        columns = arrays.pop(1)
        weights = [arrays[:3], arrays[3:]]
        vectors = call(
            functools.partial(unpack_kernel, layers, size),
            [((16, width), F32), ((8, hidden), F32), ((8, 3 * head_width), F32)],
            [columns],
            scratch=[pltpu.VMEM((hidden, LANES), F32), pltpu.VMEM((3 * head_width, LANES), F32)],
            limit=8,
        )
        links = [Link(window) for window in WINDOWS]
    else:
        weights, vectors = packed_plainly(
            norm_gains, shifts, qkv_weight, qkv_bias, out_turned, up_weight, up_bias, down_turned
        )
    rows_all, b_up, b_qkv = vectors

    token_f32, token_bf = ((length, width), F32), ((length, width), BF)
    proj_flops = 2 * length * width * 3 * head_width
    out_flops = 2 * length * width * head_width
    hidden_flops = 2 * length * width * hidden
    head_flops = 2 * length * length * head_width

    records, before = [], [tokens]
    for layer in range(layers):
        w_qkvo, w_up, w_down = weights[layer]
        state, first, proj, attn, lse, part = call(
            functools.partial(attention_forward_kernel, layer),
            [
                token_f32,
                token_bf,
                ((3 * head_width, length), BF),
                ((length, head_width), BF),
                ((8, length), F32),
                token_bf,
            ],
            before + [rows_all, b_qkv, w_qkvo, seg_row, seg_column],
            scratch=[pltpu.VMEM((head_width, length), BF)],
            flops=proj_flops + out_flops + 2 * head_flops,
        )
        middle, second, active, slope = call(
            functools.partial(up_kernel, layer),
            [token_f32, token_bf, ((length, hidden), BF), ((length, hidden), F32)],
            [state, part, swap(part), rows_all, b_up, w_up],
            flops=2 * hidden_flops,
        )
        (part,) = call(down_kernel, [token_bf], [active, w_down], flops=hidden_flops)
        before = [middle, part, swap(part)]
        records.append((state, first, proj, attn, lse, middle, second, active, slope))
    middle, part, moved = before
    result = middle + (part.astype(F32) + moved.astype(F32)) + rows_all[6 * layers - 1]
    result = result.astype(BF).reshape(count, length, width)

    vector_grads = [[None] * 8 for _ in range(layers)]
    orders = ("x", "y") if planned else (None, None)
    line = ((1, width), F32)
    above, terms = [cotangent], [None] * (2 * layers)
    halves_of, begun, folded = [None] * (2 * layers), [None] * (2 * layers), [None] * (2 * layers)

    def begin(number, front, back):
        late = planned and number == 2
        halves_of[number] = [
            products(order.upper() if late else order, *given)
            for order, given in zip(orders, (front, back))
        ]
        if planned:
            begun[number] = scatter_begin(links, *halves_of[number])
        return [half[0] for half in halves_of[number]]

    def fold(number, token):
        if not planned:
            return []
        halves = [(after(stay, token), moved) for stay, moved in begun[number]]
        folded[number], sent = scatter_fold(links, *halves)
        return sent

    def arrived(number):
        return [moved for _, moved in begun[number]] if planned else []

    for layer in reversed(range(layers)):
        w_qkvo, w_up, w_down = weights[layer]
        state, first, proj, attn, lse, middle, second, active, slope = records[layer]
        last = layer == layers - 1
        if not last:
            above[0] = after(above[0], fold(2 * layer + 3, ready))
        outs = [token_f32, token_bf, ((length, hidden), BF), token_bf, line, ((1, hidden), F32)]
        grad, low, pre, part, grad_shift, grad_up, *more = call(
            functools.partial(hidden_back_kernel, layer, last),
            outs + ([] if last else [line] * 2),
            above + [rows_all, w_up, w_down, slope],
            flops=2 * hidden_flops,
        )
        mine = vector_grads[layer]
        mine[5], mine[6] = grad_shift, grad_up
        if not last:
            vector_grads[layer + 1][0], vector_grads[layer + 1][2] = more
        moved = swap(part)
        if last:
            low = cotangent
        ready = begin(2 * layer + 1, [(low, active)], [(second, pre)])
        if not last:
            ready += arrived(2 * layer + 2)
        below, low, grad_qk, grad_v, part, *more = call(
            functools.partial(attention_back_kernel, layer),
            [
                token_f32,
                token_bf,
                ((length, 2 * head_width), BF),
                ((length, head_width), BF),
                token_bf,
                line,
                line,
                line,
                ((1, 3 * head_width), F32),
            ],
            [after(grad, ready), part, moved, middle, rows_all, w_qkvo, proj, lse]
            + [seg_row, seg_column],
            scratch=[
                pltpu.VMEM((head_width, length), BF),
                pltpu.VMEM((3 * head_width, length), BF),
                pltpu.VMEM((2, length, length), BF),
                pltpu.VMEM((2, length, length), BF),
            ],
            flops=proj_flops + out_flops + 5 * head_flops,
        )
        mine[1], mine[3], mine[4], mine[7] = more
        moved = swap(part)
        front, back = [(first, grad_qk)], [(first, grad_v), (low, attn)]
        if layer > 0:
            ready = begin(2 * layer, front, back)
            below = after(below, ready)
        above = [below, part, moved, state]
    below, part, moved, _ = above
    input_grad, grad_gain, grad_shift = call(
        input_back_kernel, [token_f32, line, line], [below, part, moved, tokens, rows_all]
    )
    vector_grads[0][0], vector_grads[0][2] = grad_gain, grad_shift
    input_grad = input_grad.reshape(count, length, width)

    if planned:
        (columns,) = call(
            functools.partial(pack_grads_kernel, layers, size),
            [((width, LANES), BF)],
            [vector for mine in vector_grads for vector in mine],
            scratch=[
                pltpu.VMEM((LANES, width), F32),
                pltpu.VMEM((LANES, hidden), F32),
                pltpu.VMEM((LANES, 3 * head_width), F32),
            ],
            limit=16,
        )
        halves_of[0] = products("x", *front), products("y", *back, columns)
        ready = [half[0] for half in halves_of[0]]
        begun[0] = scatter_begin(links, *halves_of[0])
        last_layer = scatter_line([after(folded[3][0], part), *folded[3][1:]], begun[2])
        ends = [2 * hidden]
        for half in 2 * begun[2]:
            ends.append(ends[-1] + half[0].shape[1])
        terms[3], terms[2] = [last_layer[:, : ends[0]]], [last_layer[:, ends[0] : ends[2]]]
        terms[2] += [
            flip(last_layer[:, ends[2] : ends[3]], SX),
            flip(last_layer[:, ends[3] : ends[4]], 1),
        ]
        fold(1, ready)
        fold(0, ready)
        terms[1] = [scatter_line([after(folded[1][0], ready), *folded[1][1:]])]
        terms[0] = scatter_steps(links[2], [after(folded[0][0], ready), *folded[0][1:]])
        outs = [
            (norm_gains.shape, F32),
            (shifts.shape, F32),
            (qkv_weight.shape, F32),
            (bias_turned.shape, F32),
            (out_turned.shape, F32),
            (up_weight.shape, F32),
            (up_bias.shape, F32),
            (down_turned.shape, F32),
        ]
        given = [term for number in range(2 * layers) for term in terms[number]]
        counts = [len(group) for group in terms]
        done = call(functools.partial(finish_kernel, layers, counts), outs, given, limit=24)
        gains, shift, qkv, b_qkv_grad, out, up, b_up_grad, down = done
        b_qkv_grad = jnp.swapaxes(b_qkv_grad, 0, 1)
    else:
        terms = halves_of
        terms[0] = [products(orders[0], *front), products(orders[1], *back)]

        def shared(value, axis):
            return lax.psum_scatter(value, "dp", scatter_dimension=axis, tiled=True)

        summed = [[shared(half[0].astype(F32), 0) for half in pair] for pair in terms]
        cut = [jnp.concatenate(summed[2 * layer], axis=1) for layer in range(layers)]
        qkv = jnp.stack(
            [
                jnp.stack([piece[:, c * head_width : (c + 1) * head_width] for c in range(3)])
                for piece in cut
            ]
        )
        out = jnp.stack([piece[:, 3 * head_width :] for piece in cut])
        down = jnp.stack([summed[2 * layer + 1][0] for layer in range(layers)])
        up = jnp.stack([summed[2 * layer + 1][1] for layer in range(layers)])
        both = jnp.stack([jnp.concatenate(mine[:6], axis=0) for mine in vector_grads])
        both = shared(both, 2)
        gains, shift = both[:, :2], both[:, 2:]
        b_up_grad = shared(jnp.concatenate([mine[6] for mine in vector_grads], axis=0), 1)
        b_qkv_grad = jnp.stack([mine[7].reshape(3, head_width) for mine in vector_grads])
        b_qkv_grad = shared(b_qkv_grad, 2)
    out, down = jnp.swapaxes(out, 1, 2), jnp.swapaxes(down, 1, 2)
    return (result, input_grad, gains, shift, qkv, b_qkv_grad, out, up, b_up_grad, down)


def solution(mesh):
    weights = (
        P(None, None, "dp"),
        P(None, None, "dp"),
        P(None, None, "dp", "tensor"),
        P(None, None, ("tensor", "dp")),
        P(None, "tensor", "dp"),
        P(None, "dp", "tensor"),
        P(None, ("tensor", "dp")),
        P(None, "tensor", "dp"),
    )
    rows = P("dp", None, None)
    return jax.shard_map(
        on_device,
        mesh=mesh,
        in_specs=(rows, P("dp", None), rows) + weights,
        out_specs=(rows, rows) + weights,
        check_vma=False,
    )
```

```python
import functools
import math

import jax
import jax.numpy as jnp
from jax import lax
from jax.experimental import pallas as pl
from jax.experimental.pallas import tpu as pltpu
from jax.sharding import PartitionSpec as P

HD = 64
EPSILON = 1e-05
MASKED = -1e30
BF = jnp.bfloat16
F32 = jnp.float32
SEGMENT_MAX = 96
QUERY_BLOCK = 128
HIDDEN_BLOCK = 256
LANES = 128
WINDOWS = 2, 2, 3

SZ, SY, SX = 4, 2, 2
PARTS = SZ * SY * SX


def contract(left, right, left_dim, right_dim):
    dims = (((left_dim,), (right_dim,)), ((), ()))
    return lax.dot_general(left, right, dims, preferred_element_type=F32)


def dot_nn(left, right):
    return contract(left, right, 1, 0)


def dot_nt(left, right):
    return contract(left, right, 1, 1)


def dot_tn(left, right):
    return contract(left, right, 0, 0)


def normed(state):
    mean = jnp.mean(state, axis=-1, keepdims=True)
    centred = state - mean
    inverse = lax.rsqrt(jnp.mean(centred * centred, axis=-1, keepdims=True) + EPSILON)
    return centred * inverse, inverse


def norm_back(grad, norm, inverse, gain):
    grad_gain = jnp.sum(grad * norm, axis=0, keepdims=True)
    grad_shift = jnp.sum(grad, axis=0, keepdims=True)
    scaled = grad * gain
    back = inverse * (
        scaled
        - jnp.mean(scaled, axis=-1, keepdims=True)
        - norm * jnp.mean(scaled * norm, axis=-1, keepdims=True)
    )
    return back, grad_gain, grad_shift


def query_blocks(length):
    blocks = []
    for start in range(0, length, QUERY_BLOCK):
        low = max(0, start - SEGMENT_MAX + 1) // QUERY_BLOCK * QUERY_BLOCK
        high = min(length, -(-(start + QUERY_BLOCK + SEGMENT_MAX - 1) // QUERY_BLOCK) * QUERY_BLOCK)
        blocks.append((start, low, high))
    return blocks


def call(kernel, outs, args, scratch=(), flops=0, limit=16, space=pltpu.VMEM):
    shapes = [jax.ShapeDtypeStruct(shape, kind) for shape, kind in outs]
    moved = sum(math.prod(a.shape) * a.dtype.itemsize for a in list(args) + shapes)
    vmem = pl.BlockSpec(memory_space=pltpu.VMEM)
    return pl.pallas_call(
        kernel,
        out_shape=shapes,
        in_specs=[pl.BlockSpec(memory_space=space)] * len(args),
        out_specs=[vmem] * len(outs),
        scratch_shapes=list(scratch),
        cost_estimate=pl.CostEstimate(flops=flops, bytes_accessed=moved, transcendentals=0),
        compiler_params=pltpu.CompilerParams(vmem_limit_bytes=limit << 20),
    )(*args)


def flip(value, mask):
    count = lax.axis_size("dp")
    return lax.ppermute(value, "dp", [(i, i ^ mask) for i in range(count)])


class Link:
    def __init__(self, window):
        self.window, self.sent = window, []

    def send(self, value, mask):
        if len(self.sent) >= self.window:
            value, _ = lax.optimization_barrier((value, self.sent[-self.window]))
        self.sent.append(flip(value, mask))
        return self.sent[-1]


def after(value, token):
    return lax.optimization_barrier((value, token))[0]


def swap(part):
    count = lax.axis_size("tensor")
    return lax.ppermute(part, "tensor", [(i, (i + 1) % count) for i in range(count)])


def place():
    me = lax.axis_index("dp")
    return me // (SY * SX), (me // SX) % SY, me % SX


def relative(order, y, x):
    blocks = []
    for number in range(PARTS):
        first, second, line = number // 8, number // 4 % 2, number % 4
        if order in "XY":
            line, second = number // 2 % 4, number % 2
        ky, kx = (second, first) if order in "xX" else (first, second)
        blocks.append((line * SY + (y ^ ky)) * SX + (x ^ kx))
    return blocks


def join_kernel(split, *refs):
    blocks, front, back = refs[:-2], refs[-2], refs[-1]
    rows = front.shape[0] // SZ
    z = place()[0]
    for distance, ref in enumerate(blocks):
        line = pl.ds(pl.multiple_of((z ^ distance) * rows, 16), rows)
        front[line, :] = ref[:, :split]
        back[line, :] = ref[:, split:]


def cut_kernel(line, *outs):
    start = 0
    for out in outs:
        out[...] = line[:, start : start + out.shape[1]]
        start += out.shape[1]


def place_kernel(*refs):
    parts, outs = refs[:8], refs[8:]
    _, y, x = place()
    rows = outs[0].shape[0] // PARTS
    reach = 0
    for half, order in enumerate("yx"):
        begin, reach = reach, reach + parts[4 * half].shape[1]
        start = 0
        for out in outs:
            end = start + out.shape[1]
            low, high = max(start, begin), min(end, reach)
            if low < high:
                for number, block in enumerate(relative(order, y, x)):
                    ref, line = parts[half * 4 + number // 4], number % 4
                    out[pl.ds(pl.multiple_of(block * rows, 16), rows), low - start : high - start] = ref[
                        line * rows : (line + 1) * rows, low - begin : high - begin
                    ]
            start = end


def lines():
    across = SY * SX
    return [[z * across + column for z in range(SZ)] for column in range(across)]


def pair_kernel(front, front_y, back, back_x, out):
    rows, split = front.shape
    for number, (left, right) in enumerate(((front, back), (front_y, back_x))):
        line = slice(number * rows, (number + 1) * rows)
        out[line, :split] = left[...]
        out[line, split:] = right[...]


def place_pairs_kernel(front, front_x, back, back_y, *outs):
    _, y, x = place()
    rows = outs[0].shape[0] // PARTS
    reach = 0
    for half, refs in enumerate(((front, front_x), (back, back_y))):
        begin, reach = reach, reach + refs[0].shape[1]
        start = 0
        for out in outs:
            end = start + out.shape[1]
            low, high = max(start, begin), min(end, reach)
            if low < high:
                for number in range(PARTS):
                    last, line, first = number // 8, number // 2 % 4, number % 2
                    ky, kx = (first, last) if half == 0 else (last, first)
                    block = (line * SY + (y ^ ky)) * SX + (x ^ kx)
                    at = (line * 2 + first) * rows
                    out[pl.ds(pl.multiple_of(block * rows, 16), rows), low - start : high - start] = refs[last][
                        at : at + rows, low - begin : high - begin
                    ]
            start = end


def over_z(piece):
    return lax.all_gather(piece, "dp", axis=0, tiled=True, axis_index_groups=lines())


def gather(pieces, widths):
    along_x, along_y, along_z = (Link(3) for _ in range(3))
    whole, line = [], None
    early = [(front, flip(front, SX), back, flip(back, 1)) for front, back in pieces[2:]]
    for number, piece in enumerate(pieces[:2]):
        rows, columns = piece.shape
        split = columns // 256 * 128
        shapes = [((SZ * rows, split), BF), ((SZ * rows, columns - split), BF)]
        if number == 0:
            arrived = [piece] + [along_z.send(piece, kz * SY * SX) for kz in range(1, SZ)]
            arrived[0] = after(piece, early)
            front, back = call(functools.partial(join_kernel, split), shapes, arrived, limit=8)
            tokens = [front]
        else:
            line = after(over_z(piece), tokens)
            tokens.append(line)
            front, back = call(cut_kernel, shapes, [line], limit=8)
        front_y, back_x = along_y.send(front, SX), along_x.send(back, 1)
        front_x, back_y = along_x.send(front, 1), along_y.send(back, SX)
        front_xy, back_xy = along_x.send(front_y, 1), along_y.send(back_x, SX)
        parts = [front, front_x, front_y, front_xy, back, back_y, back_x, back_xy]
        outs = [((PARTS * rows, width), BF) for width in widths[number]]
        whole.append(call(place_kernel, outs, parts, limit=12))
    for number, given in enumerate(early):
        rows, columns = given[0].shape[0], given[0].shape[1] + given[2].shape[1]
        (pair,) = call(pair_kernel, [((2 * rows, columns), BF)], given, limit=8)
        line = over_z(after(pair, tokens[number]))
        shapes = [((2 * SZ * rows, half.shape[1]), BF) for half in given[::2]]
        front, back = call(cut_kernel, shapes, [line], limit=8)
        front_x, back_y = along_x.send(front, 1), along_y.send(back, SX)
        outs = [((PARTS * rows, width), BF) for width in widths[2 + number]]
        whole.append(call(place_pairs_kernel, outs, [front, front_x, back, back_y], limit=12))
    return whole


def product_kernel(order, shares, *refs):
    count = 1 if order is None else 2
    scratch = refs[-1]
    outs = refs[-1 - count : -1]
    width = scratch.shape[0]
    blocks = None if order is None else relative(order, *place()[1:])
    rows = width // PARTS

    def put(start, size):
        if order is None:
            outs[0][:, start : start + size] = scratch[:, :size]
            return
        for number, block in enumerate(blocks):
            out, line = outs[number // 8 == 0], number % 8
            out[line * rows : (line + 1) * rows, start : start + size] = scratch[
                pl.ds(pl.multiple_of(block * rows, 16), rows), :size
            ]

    start, place_in = 0, 0
    for kind in shares:
        if kind == "ready":
            ready = refs[place_in]
            place_in += 1
            size = ready.shape[1]
            scratch[:, :size] = ready[...]
            put(start, size)
            start += size
            continue
        left, right = refs[place_in], refs[place_in + 1]
        place_in += 2
        turned = left[...].T
        for first in range(0, right.shape[1], 384):
            size = min(384, right.shape[1] - first)
            scratch[:, :size] = dot_nn(turned, right[:, first : first + size]).astype(BF)
            put(start, size)
            start += size


def products(order, *shares):
    args, kinds, columns, flops = [], [], 0, 0
    for share in shares:
        if isinstance(share, tuple):
            kinds.append("product")
            args += share
            columns += share[1].shape[1]
            width = share[0].shape[1]
            flops += 2 * math.prod(share[0].shape) * share[1].shape[1]
        else:
            kinds.append("ready")
            args.append(share)
            columns += share.shape[1]
            width = share.shape[0]
    outs = [((width, columns), BF)] if order is None else [((width // 2, columns), BF)] * 2
    return call(
        functools.partial(product_kernel, order, tuple(kinds)),
        outs,
        args,
        scratch=[pltpu.VMEM((width, 384), BF)],
        flops=flops,
        limit=24,
    )


def fold_kernel(keep, moved, away, stay):
    half = keep.shape[0] // 2
    total = keep[...].astype(F32) + moved[...].astype(F32)
    stay[...] = total[:half].astype(BF)
    away[...] = total[half:].astype(BF)


def line_kernel(*refs):
    ends, outs = refs[:4], refs[4:]
    rows = ends[0].shape[0] // SZ
    z = place()[0]
    for distance, out in enumerate(outs):
        line = slice(None)
        if len(outs) > 1:
            line = pl.ds(pl.multiple_of((z ^ distance) * rows, 16), rows)
        start = 0
        for keep, moved in zip(ends[::2], ends[1::2]):
            size = keep.shape[1]
            total = keep[line, :].astype(F32) + moved[line, :].astype(F32)
            out[:, start : start + size] = total.astype(out.dtype)
            start += size


def wide_line_kernel(*refs):
    ends, halves, out = refs[:4], refs[4:8], refs[8]
    rows = out.shape[0] // SZ
    start = 0
    for keep, moved in zip(ends[::2], ends[1::2]):
        size = keep.shape[1]
        total = keep[...].astype(F32) + moved[...].astype(F32)
        out[:, start : start + size] = total.astype(BF)
        start += size
    for distance in range(2):
        for stay, moved in zip(halves[::2], halves[1::2]):
            size = stay.shape[1]
            for line in range(SZ):
                at = slice((2 * line + distance) * rows, (2 * line + distance + 1) * rows)
                total = stay[at, :].astype(F32) + moved[at, :].astype(F32)
                out[line * rows : (line + 1) * rows, start : start + size] = total.astype(BF)
            start += size


def scatter_begin(links, half_a, half_b):
    along_x, along_y, _ = links
    moved_a, moved_b = along_x.send(half_a[0], 1), along_y.send(half_b[0], SX)
    return (half_a[1], moved_a), (half_b[1], moved_b)


def scatter_fold(links, *halves):
    along_x, along_y, _ = links
    folded = []
    for stay, moved in halves:
        shape = (stay.shape[0] // 2, stay.shape[1])
        folded.append(call(fold_kernel, [(shape, BF)] * 2, [stay, moved], limit=8))
    (away_a, stay_a), (away_b, stay_b) = folded
    moved_a, moved_b = along_y.send(away_a, SX), along_x.send(away_b, 1)
    return [stay_a, moved_a, stay_b, moved_b], [away_a, away_b]


def scatter_line(ends, halves=()):
    height, columns = ends[0].shape[0], sum(end.shape[1] for end in ends[::2])
    columns += 2 * sum(stay.shape[1] for stay, _ in halves)
    given = [*ends, *(value for half in halves for value in half)]
    kernel = wide_line_kernel if halves else line_kernel
    (line,) = call(kernel, [((height, columns), BF)], given, limit=12)
    return lax.psum_scatter(
        line, "dp", scatter_dimension=0, tiled=True, axis_index_groups=lines()
    )


def scatter_steps(along_z, ends):
    rows, columns = ends[0].shape[0] // SZ, sum(end.shape[1] for end in ends[::2])
    outs = [((rows, columns), F32)] + [((rows, columns), BF)] * (SZ - 1)
    own, *line = call(line_kernel, outs, ends, limit=8)
    return [own] + [along_z.send(block, kz * SY * SX) for kz, block in zip(range(1, SZ), line)]


def lanes_of(layers):
    up = 6 * layers
    return up, up + 2 * layers


def pack_first_kernel(*refs):
    given, piece, held, scratch, sems = refs[:6], refs[6], refs[7:13], refs[13], refs[14]
    sources = list(given[:4]) + [given[4].at[0], given[5].at[0]]
    copies = [
        pltpu.make_async_copy(source, target, sems.at[number])
        for number, (source, target) in enumerate(zip(sources, held))
    ]
    for copy in copies:
        copy.start()
    scratch[...] = jnp.zeros(scratch.shape, F32)
    for copy in copies:
        copy.wait()
    gains, shifts, b_up, b_qkv, qkv, out = held
    _, rows, width = qkv.shape
    layers = gains.shape[0]
    lane_up, lane_qkv = lanes_of(layers)
    for layer in range(layers):
        base = 6 * layer
        scratch[base : base + 2, :rows] = gains[layer]
        scratch[base + 2 : base + 6, :rows] = shifts[layer]
        for c in range(2):
            line = lane_up + 2 * layer + c
            scratch[line : line + 1, :rows] = b_up[layer : layer + 1, c * rows : (c + 1) * rows]
        for c in range(3):
            line = lane_qkv + 3 * layer + c
            scratch[line : line + 1, : b_qkv.shape[2]] = b_qkv[c, layer : layer + 1]
    for c in range(3):
        piece[:, c * width : (c + 1) * width] = qkv[c].astype(BF)
    piece[:, 3 * width : 4 * width] = out[...].astype(BF)
    piece[:, 4 * width :] = scratch[...].T[:rows].astype(BF)


def pack_kernel(*refs):
    given, (ffn, second, up_half, down_front, down_back), held, sems = refs[:4], refs[4:9], refs[9:13], refs[13]
    sources = [given[0].at[1], given[1].at[1], given[2], given[3]]
    copies = [
        pltpu.make_async_copy(source, target, sems.at[number])
        for number, (source, target) in enumerate(zip(sources, held))
    ]
    for copy in copies[::-1]:
        copy.start()
    qkv, out, up, down = held
    width, hidden = qkv.shape[2], up.shape[2]
    copies[2].wait()
    ffn[:, :hidden] = up[0].astype(BF)
    up_half[...] = up[1].astype(BF)
    copies[3].wait()
    ffn[:, hidden:] = down[0].astype(BF)
    split = down_front.shape[1]
    down_front[...] = down[1, :, :split].astype(BF)
    down_back[...] = down[1, :, split:].astype(BF)
    copies[0].wait()
    copies[1].wait()
    for c in range(3):
        second[:, c * width : (c + 1) * width] = qkv[c].astype(BF)
    second[:, 3 * width :] = out[...].astype(BF)


def unpack_kernel(layers, size, columns, rows_out, up_out, qkv_out, up_scratch, qkv_scratch):
    lane_up, lane_qkv = lanes_of(layers)
    wide = columns[...].astype(F32)
    rows_out[...] = wide.T[: rows_out.shape[0]]
    rows = columns.shape[0] // PARTS
    lane = lax.broadcasted_iota(jnp.int32, (rows, LANES), 1)

    def merged(block, lanes):
        total = jnp.zeros((block.shape[0], LANES), F32)
        for layer, at in enumerate(lanes):
            total = jnp.where(lane[: block.shape[0]] == layer, block[:, at : at + 1], total)
        return total

    width = qkv_out.shape[1] // 3
    for part in range(PARTS):
        block = wide[part * rows : (part + 1) * rows]
        for c in range(2):
            start = (part * 2 + c) * rows
            up_scratch[start : start + rows, :] = merged(
                block, [lane_up + 2 * layer + c for layer in range(layers)]
            )
        for c in range(3):
            start = c * width + part * size
            qkv_scratch[start : start + size, :] = merged(
                block[:size], [lane_qkv + 3 * layer + c for layer in range(layers)]
            )
    up_out[...] = up_scratch[...].T[: up_out.shape[0]]
    qkv_out[...] = qkv_scratch[...].T[: qkv_out.shape[0]]


def pack_grads_kernel(layers, size, *refs):
    out, rows_scratch, up_scratch, qkv_scratch = refs[-4:]
    lane_up, lane_qkv = lanes_of(layers)
    rows_scratch[...] = jnp.zeros(rows_scratch.shape, F32)
    up_scratch[...] = jnp.zeros(up_scratch.shape, F32)
    qkv_scratch[...] = jnp.zeros(qkv_scratch.shape, F32)
    for layer in range(layers):
        given = refs[8 * layer : 8 * layer + 8]
        for number in range(6):
            line = 6 * layer + number
            rows_scratch[line : line + 1, :] = given[number][...]
        up_scratch[layer : layer + 1, :] = given[6][...]
        qkv_scratch[layer : layer + 1, :] = given[7][...]
    columns = rows_scratch[...].T
    up, qkv = up_scratch[...].T, qkv_scratch[...].T
    rows = out.shape[0] // PARTS
    width = qkv.shape[0] // 3
    lane = lax.broadcasted_iota(jnp.int32, (rows, LANES), 1)
    for part in range(PARTS):
        total = columns[part * rows : (part + 1) * rows]
        for layer in range(layers):
            for c in range(2):
                start = (part * 2 + c) * rows
                value = up[start : start + rows, layer : layer + 1]
                total = jnp.where(lane == lane_up + 2 * layer + c, value, total)
            for c in range(3):
                start = c * width + part * size
                value = jnp.concatenate(
                    [
                        qkv[start : start + size, layer : layer + 1],
                        jnp.zeros((rows - size, 1), F32),
                    ],
                    axis=0,
                )
                total = jnp.where(lane == lane_qkv + 3 * layer + c, value, total)
        out[part * rows : (part + 1) * rows, :] = total.astype(BF)


def finish_kernel(layers, counts, *refs):
    outs, groups, start = refs[sum(counts) :], [], 0
    for count in counts:
        groups.append(refs[start : start + count])
        start += count
    gains, shifts, qkv, b_qkv, out, up, b_up, down = outs
    rows, width = qkv.shape[2:]
    hidden = up.shape[2]
    lane_up, lane_qkv = lanes_of(layers)
    for layer in range(layers):
        first, second = groups[2 * layer], groups[2 * layer + 1]

        def total(group, start, size):
            if len(group) == 3:
                own, *moved = group
                split = moved[0].shape[1]
                other, at = (moved[0], start) if start < split else (moved[1], start - split)
                value = own[:, start : start + size].astype(F32)
                return value + other[:, at : at + size].astype(F32)
            value = group[0][:, start : start + size].astype(F32)
            for term in group[1:]:
                value = value + term[:, start : start + size].astype(F32)
            return value

        for c in range(3):
            qkv[layer, c] = total(first, c * width, width)
        out[layer] = total(first, 3 * width, width)
        down[layer] = total(second, 0, hidden)
        up[layer] = total(second, hidden, hidden)
        if layer == 0:
            small = total(first, 4 * width, LANES)
            small = jnp.concatenate([small, jnp.zeros((LANES - rows, LANES), F32)], axis=0).T
            for k in range(layers):
                gains[k] = small[6 * k : 6 * k + 2, :rows]
                shifts[k] = small[6 * k + 2 : 6 * k + 6, :rows]
                for c in range(2):
                    line = lane_up + 2 * k + c
                    b_up[k : k + 1, c * rows : (c + 1) * rows] = small[line : line + 1, :rows]
                for c in range(3):
                    line = lane_qkv + 3 * k + c
                    b_qkv[c, k : k + 1] = small[line : line + 1, : b_qkv.shape[2]]


def attention_forward_kernel(layer, *refs):
    if layer == 0:
        tokens, *refs = refs
        state = tokens[...].astype(F32)
    else:
        middle, own, moved, *refs = refs
    rows, b_qkv, weight, seg_row, seg_column, x_ref, first_ref, proj_ref, attn_ref, lse_ref, part_ref, turned = refs
    base = 6 * layer
    if layer > 0:
        state = middle[...] + (own[...].astype(F32) + moved[...].astype(F32))
        state = state + rows[base - 1 : base, :]
    x_ref[...] = state
    norm, _ = normed(state)
    first = (norm * rows[base : base + 1, :] + rows[base + 2 : base + 3, :]).astype(BF)
    first_ref[...] = first
    width = weight.shape[1] // 512 * 128
    proj = dot_nn(first, weight[:, : 3 * width]) + b_qkv[layer : layer + 1, :]
    proj_ref[...] = proj.astype(BF).T
    length = state.shape[0]
    lse_ref[...] = jnp.zeros(lse_ref.shape, F32)
    for head in range(width // HD):
        own_rows = slice(head * HD, (head + 1) * HD)
        query = proj_ref[own_rows, :] * BF(HD**-0.5)
        keys = proj_ref[width + head * HD : width + (head + 1) * HD, :]
        values = proj_ref[2 * width + head * HD : 2 * width + (head + 1) * HD, :]
        for start, low, high in query_blocks(length):
            block = slice(start, start + QUERY_BLOCK)
            scores = dot_tn(keys[:, low:high], query[:, block])
            same = seg_column[low:high, :] == seg_row[:, block]
            scores = jnp.where(same, scores, MASKED)
            highest = jnp.max(scores, axis=0, keepdims=True)
            unnormed = jnp.exp(scores - highest)
            summed = jnp.sum(unnormed, axis=0, keepdims=True)
            lse_ref[head : head + 1, block] = highest + jnp.log(summed)
            probs = (unnormed * (1.0 / summed)).astype(BF)
            turned[own_rows, block] = dot_nn(values[:, low:high], probs).astype(BF)
    attn = turned[...].T
    attn_ref[...] = attn
    part_ref[...] = dot_nt(attn, weight[:, 3 * width : 4 * width]).astype(BF)


def up_kernel(layer, state, own, moved, rows, b_up, weight, middle_ref, second_ref, hidden_ref, slope_ref):
    base = 6 * layer
    middle = state[...] + (own[...].astype(F32) + moved[...].astype(F32))
    middle = middle + rows[base + 4 : base + 5, :]
    middle_ref[...] = middle
    norm, _ = normed(middle)
    second = (norm * rows[base + 1 : base + 2, :] + rows[base + 3 : base + 4, :]).astype(BF)
    second_ref[...] = second
    for start in range(0, hidden_ref.shape[1], HIDDEN_BLOCK):
        block = slice(start, start + HIDDEN_BLOCK)
        pre = dot_nn(second, weight[:, block]) + b_up[layer : layer + 1, block]
        below = 0.5 * (1.0 + lax.erf(pre * 0.7071067811865476))
        hidden_ref[:, block] = (pre * below).astype(BF)
        density = jnp.exp(-0.5 * pre * pre) * 0.3989422804014327
        slope_ref[:, block] = below + pre * density


def down_kernel(hidden, weight, part_ref):
    part_ref[...] = dot_nt(hidden[...], weight[...]).astype(BF)


def hidden_back_kernel(layer, last, *refs):
    if last:
        cotangent, *refs = refs
        grad = cotangent[...].astype(F32)
    else:
        above, own, moved, state, *refs = refs
    rows, w_up, w_down, slope, grad_ref, low_ref, pre_ref, part_ref, shift_ref, bias_ref, *more = refs
    if not last:
        gain_ref, norm_shift_ref = more
        arrived = own[...].astype(F32) + moved[...].astype(F32)
        norm, inverse = normed(state[...])
        upper = 6 * (layer + 1)
        back, gain_ref[...], norm_shift_ref[...] = norm_back(
            arrived, norm, inverse, rows[upper : upper + 1, :]
        )
        grad = above[...] + back
    grad_ref[...] = grad
    low = grad.astype(BF)
    low_ref[...] = low
    shift_ref[...] = jnp.sum(grad, axis=0, keepdims=True)
    for start in range(0, w_up.shape[1], HIDDEN_BLOCK):
        block = slice(start, start + HIDDEN_BLOCK)
        back = dot_nn(low, w_down[:, block])
        pre = (back * slope[:, block]).astype(BF)
        pre_ref[:, block] = pre
        bias_ref[:, block] = jnp.sum(pre.astype(F32), axis=0, keepdims=True)
    part_ref[...] = dot_nt(pre_ref[...], w_up[...]).astype(BF)


def attention_back_kernel(layer, *refs):
    (grad, own, moved, middle, rows, weight, proj, lse, seg_row, seg_column) = refs[:10]
    (below_ref, low_ref, grad_qk_ref, grad_v_ref, part_ref, gain_ref, norm_shift_ref, shift_ref, bias_ref) = refs[10:19]
    turned, turned_proj, probs_ref, scores_ref = refs[19:]
    base = 6 * layer
    arrived = own[...].astype(F32) + moved[...].astype(F32)
    norm, inverse = normed(middle[...])
    back, gain_ref[...], norm_shift_ref[...] = norm_back(
        arrived, norm, inverse, rows[base + 1 : base + 2, :]
    )
    below = grad[...] + back
    below_ref[...] = below
    shift_ref[...] = jnp.sum(below, axis=0, keepdims=True)
    low = below.astype(BF)
    low_ref[...] = low
    width = weight.shape[1] // 512 * 128
    turned[...] = dot_nn(low, weight[:, 3 * width : 4 * width]).astype(BF).T
    length = below.shape[0]
    probs_ref[...] = jnp.zeros(probs_ref.shape, BF)
    scores_ref[...] = jnp.zeros(scores_ref.shape, BF)
    for head in range(width // HD):
        slot = head % 2
        own_rows = slice(head * HD, (head + 1) * HD)
        key_rows = slice(width + head * HD, width + (head + 1) * HD)
        value_rows = slice(2 * width + head * HD, 2 * width + (head + 1) * HD)
        query = proj[own_rows, :] * BF(HD**-0.5)
        keys, values, mixed = proj[key_rows, :], proj[value_rows, :], turned[own_rows, :]
        for start, low_key, high in query_blocks(length):
            block = slice(start, start + QUERY_BLOCK)
            scores = dot_tn(keys[:, low_key:high], query[:, block])
            same = seg_column[low_key:high, :] == seg_row[:, block]
            scores = jnp.where(same, scores, MASKED)
            probs = jnp.exp(scores - lse[head : head + 1, block])
            probs_ref[slot, low_key:high, block] = probs.astype(BF)
            grad_probs = dot_tn(values[:, low_key:high], mixed[:, block])
            centre = jnp.sum(probs * grad_probs, axis=0, keepdims=True)
            scores_ref[slot, low_key:high, block] = (probs * (grad_probs - centre)).astype(BF)
        grad_scores = scores_ref[slot]
        scaled_keys = keys * BF(HD**-0.5)
        turned_proj[own_rows, :] = dot_nn(scaled_keys, grad_scores).astype(BF)
        turned_proj[key_rows, :] = dot_nt(query, grad_scores).astype(BF)
        turned_proj[value_rows, :] = dot_nt(mixed, probs_ref[slot]).astype(BF)
    grad_proj = turned_proj[...].T
    grad_qk_ref[...] = grad_proj[:, : 2 * width]
    grad_v_ref[...] = grad_proj[:, 2 * width :]
    bias_ref[...] = jnp.sum(grad_proj.astype(F32), axis=0, keepdims=True)
    part_ref[...] = dot_nt(grad_proj, weight[:, : 3 * width]).astype(BF)


def input_back_kernel(above, own, moved, tokens, rows, out_ref, gain_ref, norm_shift_ref):
    arrived = own[...].astype(F32) + moved[...].astype(F32)
    norm, inverse = normed(tokens[...].astype(F32))
    back, gain_ref[...], norm_shift_ref[...] = norm_back(arrived, norm, inverse, rows[:1, :])
    out_ref[...] = above[...] + back


def packed_plainly(norm_gains, shifts, qkv_weight, qkv_bias, out_turned, up_weight, up_bias, down_turned):
    layers = norm_gains.shape[0]
    pieces = []
    for layer in range(layers):
        first = [qkv_weight[layer, c] for c in range(3)] + [out_turned[layer]]
        given = [jnp.concatenate(first, axis=1), up_weight[layer], down_turned[layer]]
        pieces.append([lax.all_gather(w.astype(BF), "dp", axis=0, tiled=True) for w in given])

    def whole(vector, axis):
        return lax.all_gather(vector.astype(BF), "dp", axis=axis, tiled=True).astype(F32)

    both = jnp.concatenate([norm_gains, shifts], axis=1)
    rows = whole(both, 2).reshape(6 * layers, -1)
    rows = jnp.pad(rows, ((0, -rows.shape[0] % 16), (0, 0)))
    up = jnp.pad(whole(up_bias, 1), ((0, 8 - layers), (0, 0)))
    qkv = jnp.pad(whole(qkv_bias, 2).reshape(layers, -1), ((0, 8 - layers), (0, 0)))
    return pieces, (rows, up, qkv)


def on_device(
    tokens,
    segments,
    cotangent,
    norm_gains,
    shifts,
    qkv_weight,
    qkv_bias,
    out_weight,
    up_weight,
    up_bias,
    down_weight,
):
    count, length, width = tokens.shape
    layers, _, rows, head_width = qkv_weight.shape
    hidden = up_weight.shape[2]
    planned = lax.axis_size("dp") == PARTS and rows % 48 == 0 and layers == 2
    tokens = tokens.reshape(length, width)
    cotangent = cotangent.reshape(length, width)
    seg_row, seg_column = segments.reshape(1, length), segments.reshape(length, 1)
    out_turned, down_turned = jnp.swapaxes(out_weight, 1, 2), jnp.swapaxes(down_weight, 1, 2)

    if planned:
        size = qkv_bias.shape[2]
        bias_turned = jnp.swapaxes(qkv_bias, 0, 1)
        wide = 4 * head_width
        given = [norm_gains, shifts, up_bias, bias_turned, qkv_weight, out_turned]
        held = [a.shape for a in given[:4]] + [a.shape[1:] for a in given[4:]]
        (first_piece,) = call(
            pack_first_kernel,
            [((rows, wide + LANES), BF)],
            given,
            scratch=[pltpu.VMEM(shape, F32) for shape in held]
            + [pltpu.VMEM((LANES, LANES), F32), pltpu.SemaphoreType.DMA((len(held),))],
            limit=8,
            space=pl.ANY,
        )
        half = hidden // 2
        shapes = [((rows, size), BF) for size in (2 * hidden, wide, hidden, half, hidden - half)]
        given = [qkv_weight, out_turned, up_weight, down_turned]
        held = [a.shape[1:] for a in given[:2]] + [a.shape for a in given[2:]]
        ffn, *others = call(
            pack_kernel,
            shapes,
            given,
            scratch=[pltpu.VMEM(shape, F32) for shape in held]
            + [pltpu.SemaphoreType.DMA((len(held),))],
            limit=56,
            space=pl.ANY,
        )
        arrays = gather(
            [first_piece, ffn, others[:2], others[2:]],
            [[wide, LANES], [hidden, hidden], [wide, hidden], [hidden]],
        )
        arrays = [array for bundle in arrays for array in bundle]
        columns = arrays.pop(1)
        weights = [arrays[:3], arrays[3:]]
        vectors = call(
            functools.partial(unpack_kernel, layers, size),
            [((16, width), F32), ((8, hidden), F32), ((8, 3 * head_width), F32)],
            [columns],
            scratch=[pltpu.VMEM((hidden, LANES), F32), pltpu.VMEM((3 * head_width, LANES), F32)],
            limit=8,
        )
        links = [Link(window) for window in WINDOWS]
    else:
        weights, vectors = packed_plainly(
            norm_gains, shifts, qkv_weight, qkv_bias, out_turned, up_weight, up_bias, down_turned
        )
    rows_all, b_up, b_qkv = vectors

    token_f32, token_bf = ((length, width), F32), ((length, width), BF)
    proj_flops = 2 * length * width * 3 * head_width
    out_flops = 2 * length * width * head_width
    hidden_flops = 2 * length * width * hidden
    head_flops = 2 * length * length * head_width

    records, before = [], [tokens]
    for layer in range(layers):
        w_qkvo, w_up, w_down = weights[layer]
        state, first, proj, attn, lse, part = call(
            functools.partial(attention_forward_kernel, layer),
            [
                token_f32,
                token_bf,
                ((3 * head_width, length), BF),
                ((length, head_width), BF),
                ((8, length), F32),
                token_bf,
            ],
            before + [rows_all, b_qkv, w_qkvo, seg_row, seg_column],
            scratch=[pltpu.VMEM((head_width, length), BF)],
            flops=proj_flops + out_flops + 2 * head_flops,
        )
        middle, second, active, slope = call(
            functools.partial(up_kernel, layer),
            [token_f32, token_bf, ((length, hidden), BF), ((length, hidden), F32)],
            [state, part, swap(part), rows_all, b_up, w_up],
            flops=2 * hidden_flops,
        )
        (part,) = call(down_kernel, [token_bf], [active, w_down], flops=hidden_flops)
        before = [middle, part, swap(part)]
        records.append((state, first, proj, attn, lse, middle, second, active, slope))
    middle, part, moved = before
    result = middle + (part.astype(F32) + moved.astype(F32)) + rows_all[6 * layers - 1]
    result = result.astype(BF).reshape(count, length, width)

    vector_grads = [[None] * 8 for _ in range(layers)]
    orders = ("x", "y") if planned else (None, None)
    line = ((1, width), F32)
    above, terms = [cotangent], [None] * (2 * layers)
    halves_of, begun, folded = [None] * (2 * layers), [None] * (2 * layers), [None] * (2 * layers)

    def begin(number, front, back):
        late = planned and number == 2
        halves_of[number] = [
            products(order.upper() if late else order, *given)
            for order, given in zip(orders, (front, back))
        ]
        if planned:
            begun[number] = scatter_begin(links, *halves_of[number])
        return [half[0] for half in halves_of[number]]

    def fold(number, token):
        if not planned:
            return []
        halves = [(after(stay, token), moved) for stay, moved in begun[number]]
        folded[number], sent = scatter_fold(links, *halves)
        return sent

    def arrived(number):
        return [moved for _, moved in begun[number]] if planned else []

    for layer in reversed(range(layers)):
        w_qkvo, w_up, w_down = weights[layer]
        state, first, proj, attn, lse, middle, second, active, slope = records[layer]
        last = layer == layers - 1
        if not last:
            above[0] = after(above[0], fold(2 * layer + 3, ready))
        outs = [token_f32, token_bf, ((length, hidden), BF), token_bf, line, ((1, hidden), F32)]
        grad, low, pre, part, grad_shift, grad_up, *more = call(
            functools.partial(hidden_back_kernel, layer, last),
            outs + ([] if last else [line] * 2),
            above + [rows_all, w_up, w_down, slope],
            flops=2 * hidden_flops,
        )
        mine = vector_grads[layer]
        mine[5], mine[6] = grad_shift, grad_up
        if not last:
            vector_grads[layer + 1][0], vector_grads[layer + 1][2] = more
        moved = swap(part)
        if last:
            low = cotangent
        ready = begin(2 * layer + 1, [(low, active)], [(second, pre)])
        if not last:
            ready += arrived(2 * layer + 2)
        below, low, grad_qk, grad_v, part, *more = call(
            functools.partial(attention_back_kernel, layer),
            [
                token_f32,
                token_bf,
                ((length, 2 * head_width), BF),
                ((length, head_width), BF),
                token_bf,
                line,
                line,
                line,
                ((1, 3 * head_width), F32),
            ],
            [after(grad, ready), part, moved, middle, rows_all, w_qkvo, proj, lse]
            + [seg_row, seg_column],
            scratch=[
                pltpu.VMEM((head_width, length), BF),
                pltpu.VMEM((3 * head_width, length), BF),
                pltpu.VMEM((2, length, length), BF),
                pltpu.VMEM((2, length, length), BF),
            ],
            flops=proj_flops + out_flops + 5 * head_flops,
        )
        mine[1], mine[3], mine[4], mine[7] = more
        moved = swap(part)
        front, back = [(first, grad_qk)], [(first, grad_v), (low, attn)]
        if layer > 0:
            ready = begin(2 * layer, front, back)
            below = after(below, ready)
        above = [below, part, moved, state]
    below, part, moved, _ = above
    input_grad, grad_gain, grad_shift = call(
        input_back_kernel, [token_f32, line, line], [below, part, moved, tokens, rows_all]
    )
    vector_grads[0][0], vector_grads[0][2] = grad_gain, grad_shift
    input_grad = input_grad.reshape(count, length, width)

    if planned:
        (columns,) = call(
            functools.partial(pack_grads_kernel, layers, size),
            [((width, LANES), BF)],
            [vector for mine in vector_grads for vector in mine],
            scratch=[
                pltpu.VMEM((LANES, width), F32),
                pltpu.VMEM((LANES, hidden), F32),
                pltpu.VMEM((LANES, 3 * head_width), F32),
            ],
            limit=16,
        )
        halves_of[0] = products("x", *front), products("y", *back, columns)
        ready = [half[0] for half in halves_of[0]]
        begun[0] = scatter_begin(links, *halves_of[0])
        last_layer = scatter_line([after(folded[3][0], part), *folded[3][1:]], begun[2])
        ends = [2 * hidden]
        for half in 2 * begun[2]:
            ends.append(ends[-1] + half[0].shape[1])
        terms[3], terms[2] = [last_layer[:, : ends[0]]], [last_layer[:, ends[0] : ends[2]]]
        terms[2] += [
            flip(last_layer[:, ends[2] : ends[3]], SX),
            flip(last_layer[:, ends[3] : ends[4]], 1),
        ]
        fold(1, ready)
        fold(0, ready)
        terms[1] = [scatter_line([after(folded[1][0], ready), *folded[1][1:]])]
        terms[0] = scatter_steps(links[2], [after(folded[0][0], ready), *folded[0][1:]])
        outs = [
            (norm_gains.shape, F32),
            (shifts.shape, F32),
            (qkv_weight.shape, F32),
            (bias_turned.shape, F32),
            (out_turned.shape, F32),
            (up_weight.shape, F32),
            (up_bias.shape, F32),
            (down_turned.shape, F32),
        ]
        given = [term for number in range(2 * layers) for term in terms[number]]
        counts = [len(group) for group in terms]
        done = call(functools.partial(finish_kernel, layers, counts), outs, given, limit=24)
        gains, shift, qkv, b_qkv_grad, out, up, b_up_grad, down = done
        b_qkv_grad = jnp.swapaxes(b_qkv_grad, 0, 1)
    else:
        terms = halves_of
        terms[0] = [products(orders[0], *front), products(orders[1], *back)]

        def shared(value, axis):
            return lax.psum_scatter(value, "dp", scatter_dimension=axis, tiled=True)

        summed = [[shared(half[0].astype(F32), 0) for half in pair] for pair in terms]
        cut = [jnp.concatenate(summed[2 * layer], axis=1) for layer in range(layers)]
        qkv = jnp.stack(
            [
                jnp.stack([piece[:, c * head_width : (c + 1) * head_width] for c in range(3)])
                for piece in cut
            ]
        )
        out = jnp.stack([piece[:, 3 * head_width :] for piece in cut])
        down = jnp.stack([summed[2 * layer + 1][0] for layer in range(layers)])
        up = jnp.stack([summed[2 * layer + 1][1] for layer in range(layers)])
        both = jnp.stack([jnp.concatenate(mine[:6], axis=0) for mine in vector_grads])
        both = shared(both, 2)
        gains, shift = both[:, :2], both[:, 2:]
        b_up_grad = shared(jnp.concatenate([mine[6] for mine in vector_grads], axis=0), 1)
        b_qkv_grad = jnp.stack([mine[7].reshape(3, head_width) for mine in vector_grads])
        b_qkv_grad = shared(b_qkv_grad, 2)
    out, down = jnp.swapaxes(out, 1, 2), jnp.swapaxes(down, 1, 2)
    return (result, input_grad, gains, shift, qkv, b_qkv_grad, out, up, b_up_grad, down)


def solution(mesh):
    weights = (
        P(None, None, "dp"),
        P(None, None, "dp"),
        P(None, None, "dp", "tensor"),
        P(None, None, ("tensor", "dp")),
        P(None, "tensor", "dp"),
        P(None, "dp", "tensor"),
        P(None, ("tensor", "dp")),
        P(None, "tensor", "dp"),
    )
    rows = P("dp", None, None)
    return jax.shard_map(
        on_device,
        mesh=mesh,
        in_specs=(rows, P("dp", None), rows) + weights,
        out_specs=(rows, rows) + weights,
        check_vma=False,
    )
```
